32 devices in a mesh: dp: 4 (over y, x), blk: 8 (over z, core).
Axes of the slice: x: 2, y: 2, z: 4, core: 2. Of those that a mesh axis runs over, the one named last changes fastest.
Arguments:
- tokens: bfloat16 [15360, 768], P(('dp', 'blk')), may hold values from -6 to 6
- item_lengths: int32 [4, 4], P('dp'), may hold values from 0 to 1200, as said below
- dataset_ids: int32 [4, 4], P('dp'), may hold values from 0 to 9
- dataset_table: float32 [10, 768], replicated, may hold values from -3 to 3
- norm1_gain: float32 [768], replicated, may hold values from 0.5 to 1.5
- norm1_bias: float32 [768], replicated, may hold values from -1.5 to 1.5
- query_weight: bfloat16 [768, 768], replicated, may hold values from -0.21875 to 0.21875
- key_weight: bfloat16 [768, 768], replicated, may hold values from -0.21875 to 0.21875
- value_weight: bfloat16 [768, 768], replicated, may hold values from -0.21875 to 0.21875
- out_weight: bfloat16 [768, 768], replicated, may hold values from -0.875 to 0.875
- norm2_gain: float32 [768], replicated, may hold values from 0.5 to 1.5
- norm2_bias: float32 [768], replicated, may hold values from -1.5 to 1.5
- fc1_weight: bfloat16 [768, 3072], replicated, may hold values from -0.21875 to 0.21875
- fc2_weight: bfloat16 [3072, 768], replicated, may hold values from -0.109375 to 0.109375
- project_weight: bfloat16 [768, 256], replicated, may hold values from -0.21875 to 0.21875
- unit1_first: bfloat16 [2304, 256], replicated, may hold values from -0.125 to 0.125
- unit1_second: bfloat16 [2304, 256], replicated, may hold values from -0.125 to 0.125
- unit2_first: bfloat16 [2304, 256], replicated, may hold values from -0.125 to 0.125
- unit2_second: bfloat16 [2304, 256], replicated, may hold values from -0.125 to 0.125
- output_weight: bfloat16 [256, 256], replicated, may hold values from -0.375 to 0.375
- block_cotangent: bfloat16 [15360, 768], P(('dp', 'blk')), may hold values from -6 to 6
- merged_cotangent: bfloat16 [15360, 1024], P(('dp', 'blk')), may hold values from -6 to 6
Outputs:
- block_out: bfloat16 [15360, 768], P(('dp', 'blk'))
- merged: bfloat16 [15360, 1024], P(('dp', 'blk'))
- tokens_grad: float32 [15360, 768], P(('dp', 'blk'))
- table_grad: float32 [10, 768], P(None, 'blk')
- norm1_gain_grad: float32 [768], P('blk')
- norm1_bias_grad: float32 [768], P('blk')
- query_grad: float32 [768, 768], P('blk')
- key_grad: float32 [768, 768], P('blk')
- value_grad: float32 [768, 768], P('blk')
- out_proj_grad: float32 [768, 768], P('blk')
- norm2_gain_grad: float32 [768], P('blk')
- norm2_bias_grad: float32 [768], P('blk')
- fc1_grad: float32 [768, 3072], P('blk')
- fc2_grad: float32 [3072, 768], P('blk')
- project_grad: float32 [768, 256], P('blk')
- unit1_first_grad: float32 [2304, 256], P('blk')
- unit1_second_grad: float32 [2304, 256], P('blk')
- unit2_first_grad: float32 [2304, 256], P('blk')
- unit2_second_grad: float32 [2304, 256], P('blk')
- output_grad: float32 [256, 256], P('blk')
The draws below stay inside these ranges and needn't reach their ends.
Inputs may be any that keep to these rules, and one draw needn't show every extreme that they name: `item_lengths`: row g lists group g's items in order. Entries are 0, 576 (an image of 24 x 24 patches) or 1200 (30 x 40 patches); the nonzero entries come first and the first entry is never 0; the heights (24 or 30 rows) of a row's items add up to at most 96.
All inputs are finite; a program needn't handle non-finite values.
Results may differ from the reference program's by a relative error of at most 0.023.
Values may be sent and summed in bfloat16 or wider, within the bound.
No kernel may reach another device: no remote copies, remote signals or barrier semaphores. Data moves between devices by JAX's collectives and lax.ppermute only.
A program may use at most 192 MiB of HBM per device.

```python
import math
import jax
import jax.numpy as jnp
from jax import lax

D = 768
HEADS = 12
HEAD = 64
FF = 3072
CH = 256
DATASETS = 10
ROWW = 40
SLOTS = 12
TOK_DEV = 480
GROUP_ROWS = 96
GROUP_TOKENS = 3840
TOKENS = 15360
ITEMS = 4
N_DP = 4
N_BLK = 8


def draw_item_lengths(key, part):
    key = jax.random.fold_in(key, 11)
    kinds = jax.random.randint(key, (N_DP, ITEMS), 0, 2).astype(jnp.int32)
    item_heights = jnp.where(kinds == 1, 30, 24)
    row_ends = jnp.cumsum(item_heights, axis=1)
    fitting = row_ends <= SLOTS * N_BLK
    return jnp.where(fitting, jnp.where(kinds == 1, 1200, 576), 0).astype(jnp.int32)


def with_ends(drawn, rng, low, high):
    longest = drawn.shape.index(max(drawn.shape))
    spots = []
    for shift in (0, 1):
        where = [jax.random.randint(jax.random.fold_in(rng, axis), (), 0, length) for axis, length in enumerate(drawn.shape)]
        where[longest] = (where[longest] + shift) % drawn.shape[longest]
        spots.append(tuple(where))
    return drawn.at[spots[0]].set(low).at[spots[1]].set(high)


def block_levels(own_key, dims, shards, smallest, high):
    gain = 1.0
    for position, blocks in shards:
        steps = jax.random.uniform(jax.random.fold_in(jax.random.fold_in(own_key, 6), position), (blocks,), jnp.float32, smallest / len(shards), high / len(shards))
        gain = gain * jnp.repeat(jnp.exp(steps), dims[position] // blocks).reshape((-1,) + (1,) * (len(dims) - 1 - position))
    return gain


def gaussian(stream_key, dims, scale, reach, cuts=(), kind=jnp.bfloat16):
    entries = scale * jax.random.normal(stream_key, dims, jnp.float32)
    if cuts:
        entries = entries * block_levels(stream_key, dims, cuts, -0.22, 0.18)
    return jnp.clip(entries, -reach, reach).astype(kind)


def setup_inputs(seed: int = 0) -> dict:
    arg_keys = jax.random.split(jax.random.key(seed), 23)
    return {
        "tokens": gaussian(arg_keys[0], (TOKENS, D), 1.0, 6.0, ((0, 32),)),
        "item_lengths": draw_item_lengths(jax.random.fold_in(arg_keys[22], 71), 0),
        "dataset_ids": with_ends(jax.random.randint(arg_keys[2], (N_DP, ITEMS), 0, DATASETS), jax.random.fold_in(arg_keys[2], 1), 0, DATASETS - 1).astype(jnp.int32),
        "dataset_table": gaussian(arg_keys[3], (DATASETS, D), 0.5, 3.0, (), jnp.float32),
        "norm1_gain": jnp.clip(1.0 + 0.1 * jax.random.normal(arg_keys[4], (D,), jnp.float32), 0.5, 1.5),
        "norm1_bias": gaussian(arg_keys[5], (D,), 0.3, 1.5, (), jnp.float32),
        "query_weight": gaussian(arg_keys[6], (D, D), D ** -0.5, 0.21875),
        "key_weight": gaussian(arg_keys[7], (D, D), D ** -0.5, 0.21875),
        "value_weight": gaussian(arg_keys[8], (D, D), D ** -0.5, 0.21875),
        "out_weight": gaussian(arg_keys[9], (D, D), (D // 16) ** -0.5, 0.875),
        "norm2_gain": jnp.clip(1.0 + 0.1 * jax.random.normal(arg_keys[10], (D,), jnp.float32), 0.5, 1.5),
        "norm2_bias": gaussian(arg_keys[11], (D,), 0.3, 1.5, (), jnp.float32),
        "fc1_weight": gaussian(arg_keys[12], (D, FF), D ** -0.5, 0.21875),
        "fc2_weight": gaussian(arg_keys[13], (FF, D), FF ** -0.5, 0.109375),
        "project_weight": gaussian(arg_keys[14], (D, CH), D ** -0.5, 0.21875),
        "unit1_first": gaussian(arg_keys[15], (9 * CH, CH), (9 * CH) ** -0.5, 0.125),
        "unit1_second": gaussian(arg_keys[16], (9 * CH, CH), (9 * CH) ** -0.5, 0.125),
        "unit2_first": gaussian(arg_keys[17], (9 * CH, CH), (9 * CH) ** -0.5, 0.125),
        "unit2_second": gaussian(arg_keys[18], (9 * CH, CH), (9 * CH) ** -0.5, 0.125),
        "output_weight": gaussian(arg_keys[19], (CH, CH), CH ** -0.5, 0.375),
        "block_cotangent": gaussian(arg_keys[20], (TOKENS, D), 1.0, 6.0, ((0, 32),)),
        "merged_cotangent": gaussian(arg_keys[21], (TOKENS, 4 * CH), 1.0, 6.0, ((0, 32),)),
    }


NEG = -1e+30
EPS = 1e-06
HIGH = lax.Precision.HIGHEST

@jax.custom_vjp
def low(v):
    return lax.optimization_barrier(v.astype(jnp.bfloat16)).astype(jnp.float32)

@jax.custom_vjp
def low_back(v):
    return v

def low_keep(v):
    return (low(v), None)

def low_pass(kept, grad):
    return (grad,)

def back_keep(v):
    return (v, None)

def back_low(kept, grad):
    return (low(grad),)
low.defvjp(low_keep, low_pass)
low_back.defvjp(back_keep, back_low)

def rounded(values):
    return low(low_back(values))

def gelu_tanh(values):
    return 0.5 * values * (1.0 + jnp.tanh(0.7978845608028654 * (values + 0.044715 * values * values * values)))

def layer_norm(hidden, norm_gain, norm_bias):
    centred = hidden - lax.optimization_barrier(jnp.mean(hidden, axis=-1, keepdims=True))
    spread = lax.optimization_barrier(jnp.mean(centred * centred, axis=-1, keepdims=True))
    return centred * lax.rsqrt(spread + EPS) * norm_gain + norm_bias

def softmax_rows(scores):
    row_max = lax.optimization_barrier(jnp.max(scores, axis=-1, keepdims=True))
    raised = jnp.exp(scores - row_max)
    return raised / lax.optimization_barrier(jnp.sum(raised, axis=-1, keepdims=True))

def geometry(lengths, row_ids, col_count):
    item_count = lengths.shape[0]
    item_heights = jnp.where(lengths == 1200, 30, jnp.where(lengths == 576, 24, 0)).astype(jnp.int32)
    item_widths = jnp.where(lengths == 1200, 40, 24).astype(jnp.int32)
    row_ends = jnp.cumsum(item_heights).astype(jnp.int32)
    row_begins = row_ends - item_heights
    number = lax.optimization_barrier(jnp.sum((row_ends[None, :] <= row_ids[:, None]).astype(jnp.int32), axis=1))
    item_pick = jnp.arange(item_count, dtype=jnp.int32)[None, :] == number[:, None]
    row_start = lax.optimization_barrier(jnp.sum(jnp.where(item_pick, row_begins[None, :], 0), axis=1)).astype(jnp.int32)
    item_height = lax.optimization_barrier(jnp.sum(jnp.where(item_pick, item_heights[None, :], 0), axis=1)).astype(jnp.int32)
    item_width = lax.optimization_barrier(jnp.sum(jnp.where(item_pick, item_widths[None, :], 0), axis=1)).astype(jnp.int32)
    column = jnp.arange(col_count, dtype=jnp.int32)
    is_real = (number < item_count)[:, None] & (column[None, :] < item_width[:, None])
    item_ids = jnp.where(is_real, number[:, None], item_count).astype(jnp.int32)
    return (item_ids, item_pick, row_ids - row_start, item_height, item_width, is_real)

def tap_masks(local_row, item_height, item_width, is_real):
    column = jnp.arange(is_real.shape[1], dtype=jnp.int32)
    all_masks = []
    for row_step in (-1, 0, 1):
        rows_fine = (local_row + row_step >= 0) & (local_row + row_step < item_height)
        for col_step in (-1, 0, 1):
            cols_fine = (column + col_step >= 0)[None, :] & (column[None, :] + col_step < item_width[:, None])
            all_masks.append(is_real & rows_fine[:, None] & cols_fine)
    return all_masks

def shift_grid(values, row_step, col_step):
    padded = jnp.pad(values, ((1, 1), (1, 1), (0, 0)))
    return padded[1 + row_step:1 + row_step + values.shape[0], 1 + col_step:1 + col_step + values.shape[1]]

def to_cells(flattened):
    return flattened.reshape(GROUP_ROWS, ROWW, flattened.shape[-1])

def stencil_grid(values, kernel, all_masks):
    tap_parts = []
    for row_step in (-1, 0, 1):
        for col_step in (-1, 0, 1):
            tap_mask = all_masks[len(tap_parts)]
            tap_parts.append(jnp.where(tap_mask[:, :, None], shift_grid(values, row_step, col_step), 0.0))
    joined = jnp.concatenate(tap_parts, axis=2)
    return jnp.dot(joined.reshape(-1, joined.shape[2]), kernel, precision=HIGH)

def upsample_grid(values, all_masks):
    upper_value = jnp.where(all_masks[1][:, :, None], shift_grid(values, -1, 0), values)
    lower_value = jnp.where(all_masks[7][:, :, None], shift_grid(values, 1, 0), values)
    halves = (0.75 * values + 0.25 * upper_value, 0.75 * values + 0.25 * lower_value)
    pieces = []
    for half_rows in halves:
        left_value = jnp.where(all_masks[3][:, :, None], shift_grid(half_rows, 0, -1), half_rows)
        right_value = jnp.where(all_masks[5][:, :, None], shift_grid(half_rows, 0, 1), half_rows)
        pieces.append(0.75 * half_rows + 0.25 * left_value)
        pieces.append(0.75 * half_rows + 0.25 * right_value)
    joined = jnp.concatenate(pieces, axis=2)
    return joined.reshape(-1, joined.shape[2])

def attention_group(query_heads, key_heads, value_heads, item_ids):
    blocks = query_heads.shape[0] // TOK_DEV
    score_scale = 1.0 / math.sqrt(HEAD)

    def one_block(pieces):
        block_queries, block_items = pieces
        scores = jnp.einsum('qhd,khd->hqk', block_queries, key_heads, precision=HIGH) * score_scale
        scores = low_back(scores)
        same_item = (block_items[:, None] == item_ids[None, :])[None]
        weights = low(softmax_rows(jnp.where(same_item, scores, NEG)))
        return jnp.einsum('hqk,khd->qhd', weights, value_heads, precision=HIGH)
    attended = lax.map(jax.checkpoint(one_block), (query_heads.reshape(blocks, TOK_DEV, HEADS, HEAD), item_ids.reshape(blocks, TOK_DEV)))
    return attended.reshape(query_heads.shape[0], HEADS * HEAD)

def residual_unit(values, first_kernel, second_kernel, all_masks):
    act_one = low(gelu_tanh(values))
    conv_one = low_back(stencil_grid(to_cells(act_one), first_kernel, all_masks))
    act_two = low(gelu_tanh(conv_one))
    conv_two = low_back(stencil_grid(to_cells(act_two), second_kernel, all_masks))
    return values + conv_two

def group_forward(weights, tokens_grid, lengths, dataset_row):
    dataset_table, norm1_gain, norm1_bias, query_weight, key_weight, value_weight, out_weight, norm2_gain, norm2_bias, fc1_weight, fc2_weight, project_weight, unit1_first, unit1_second, unit2_first, unit2_second, output_weight = weights
    row_ids = jnp.arange(GROUP_ROWS, dtype=jnp.int32)
    item_ids, item_pick, local_row, item_height, item_width, is_real = geometry(lengths, row_ids, ROWW)
    all_masks = tap_masks(local_row, item_height, item_width, is_real)
    dataset_here = lax.optimization_barrier(jnp.sum(jnp.where(item_pick, dataset_row[None, :], 0), axis=1))
    onehot = (is_real[:, :, None] & (dataset_here[:, None, None] == jnp.arange(DATASETS, dtype=jnp.int32)[None, None, :])).astype(jnp.float32).reshape(-1, DATASETS)
    stream_start = tokens_grid + jnp.dot(onehot, dataset_table, precision=HIGH)
    normed_one = low(layer_norm(stream_start, norm1_gain, norm1_bias))
    query_flat = rounded(jnp.dot(normed_one, query_weight, precision=HIGH))
    key_flat = rounded(jnp.dot(normed_one, key_weight, precision=HIGH))
    value_flat = rounded(jnp.dot(normed_one, value_weight, precision=HIGH))
    head_shape = (-1, HEADS, HEAD)
    attended = rounded(attention_group(query_flat.reshape(head_shape), key_flat.reshape(head_shape), value_flat.reshape(head_shape), item_ids.reshape(-1)))
    after_attn = stream_start + low_back(jnp.dot(attended, out_weight, precision=HIGH))
    normed_two = low(layer_norm(after_attn, norm2_gain, norm2_bias))
    pre_act = low_back(jnp.dot(normed_two, fc1_weight, precision=HIGH))
    hidden = low(gelu_tanh(pre_act))
    block_out = low(after_attn + low_back(jnp.dot(hidden, fc2_weight, precision=HIGH)))
    reassembled = low_back(jnp.dot(block_out, project_weight, precision=HIGH))
    merged_one = residual_unit(reassembled, unit1_first, unit1_second, all_masks)
    merged_two = residual_unit(merged_one, unit2_first, unit2_second, all_masks)
    mapped = rounded(jnp.dot(low(merged_two), output_weight, precision=HIGH))
    return (block_out, upsample_grid(to_cells(mapped), all_masks))

def reference(tokens, item_lengths, dataset_ids, dataset_table, norm1_gain, norm1_bias, query_weight, key_weight, value_weight, out_weight, norm2_gain, norm2_bias, fc1_weight, fc2_weight, project_weight, unit1_first, unit1_second, unit2_first, unit2_second, output_weight, block_cotangent, merged_cotangent):
    weights = tuple((weight_array.astype(jnp.float32) for weight_array in (dataset_table, norm1_gain, norm1_bias, query_weight, key_weight, value_weight, out_weight, norm2_gain, norm2_bias, fc1_weight, fc2_weight, project_weight, unit1_first, unit1_second, unit2_first, unit2_second, output_weight)))
    groups = tokens.shape[0] // GROUP_TOKENS

    def device_to_grid(flattened):
        feature_count = flattened.shape[-1]
        return flattened.reshape(N_BLK, SLOTS, ROWW, feature_count).transpose(1, 0, 2, 3).reshape(GROUP_TOKENS, feature_count)

    def grid_to_device(flattened):
        feature_count = flattened.shape[-1]
        return flattened.reshape(SLOTS, N_BLK, ROWW, feature_count).transpose(1, 0, 2, 3).reshape(GROUP_TOKENS, feature_count)

    def whole_forward(weights, tokens_f32):

        def one_group(pieces):
            group_tokens, lengths, dataset_row = pieces
            block_grid, merged_grid = group_forward(weights, device_to_grid(group_tokens), lengths, dataset_row)
            return (grid_to_device(block_grid), grid_to_device(merged_grid))
        blocks_all, merged_all = lax.map(one_group, (tokens_f32.reshape(groups, GROUP_TOKENS, D), item_lengths, dataset_ids))
        return (blocks_all.reshape(-1, D), merged_all.reshape(-1, 4 * CH))
    (block_all, merged_all), pullback = jax.vjp(whole_forward, weights, tokens.astype(jnp.float32))
    weight_grads, tokens_grad = pullback((block_cotangent.astype(jnp.float32), merged_cotangent.astype(jnp.float32)))
    return (block_all.astype(jnp.bfloat16), merged_all.astype(jnp.bfloat16), tokens_grad, weight_grads[0], weight_grads[1], weight_grads[2], weight_grads[3], weight_grads[4], weight_grads[5], weight_grads[6], weight_grads[7], weight_grads[8], weight_grads[9], weight_grads[10], weight_grads[11], weight_grads[12], weight_grads[13], weight_grads[14], weight_grads[15], weight_grads[16])
```

```python
import functools
import math

import jax
import jax.numpy as jnp
from jax import lax
from jax.experimental import pallas as pl
from jax.experimental.pallas import tpu as pltpu
from jax.sharding import PartitionSpec as P
import numpy as np

HEADS = 12
HEAD = 64
ROWW = 40
SLOTS = 12
HALF = SLOTS // 2
REACH = 6

NEG = -1e30
EPS = 1e-06
HIGH = lax.Precision.HIGHEST
KEYS = 672
SPARE_KEYS = 768
QROWS = 64
ROWS = 512
VMEM = 60 * 1024 * 1024
NT = (((1,), (1,)), ((), ()))
F32 = jnp.float32
BF16 = jnp.bfloat16


def up16(value):
    return (value + 15) // 16 * 16


def own_blocks(heads, feats):
    row = lax.broadcasted_iota(jnp.int32, (heads * QROWS, feats), 0) // QROWS
    col = lax.broadcasted_iota(jnp.int32, (heads * QROWS, feats), 1) // HEAD
    return row == col


def spread(block, heads):
    wide = jnp.concatenate([block] * heads, axis=0)
    return jnp.where(own_blocks(heads, block.shape[1]), wide, jnp.zeros((), block.dtype))


def gathered(wide, heads):
    kept = jnp.where(own_blocks(heads, wide.shape[1]), wide, 0.0)
    total = kept[:QROWS]
    for head in range(1, heads):
        total = total + kept[head * QROWS : (head + 1) * QROWS]
    return total


def lanes(column, width):
    return jnp.concatenate([column] * (width // 128), axis=1)


def query_blocks(first, many, body):
    def pair(number, none):
        body(first + 2 * number, 2)
        return none

    lax.fori_loop(0, many // 2, pair, 0)

    @pl.when(many % 2 == 1)
    def _():
        body(first + many - 1, 1)


def for_items(items, klen, body):
    def one(item, none):
        body(item, KEYS, (klen[item] + KEYS - 1) // KEYS)
        return none

    lax.fori_loop(0, items - 1, one, 0)
    last = items - 1
    body(last, SPARE_KEYS, (klen[last] + SPARE_KEYS - 1) // SPARE_KEYS)


def as_column(row):
    return row.T[:, :1]


def attend_kernel(
    heads, units, items,
    koff, kcnt, kdst, kstart, klen, qfirst, qcount,
    q_ref, bias_ref, wk_ref, wv_ref, *refs,
):
    steps = units // 4
    n_refs = refs[:steps]
    o_ref, lse_ref, ns_ref, ks_ref, vs_ref = refs[steps : steps + 5]
    acc_ref, top_ref, total_ref = refs[steps + 5 :]
    stride = n_refs[0].shape[0]
    cols = heads * QROWS
    width = ns_ref.shape[1]
    o_ref[...] = jnp.zeros_like(o_ref)
    lse_ref[...] = jnp.zeros_like(lse_ref)
    used = kstart[items]

    @pl.when(pl.program_id(0) == 0)
    def _():
        def one_item(item, size, blocks):
            def one_unit(turn, unit, none):
                entry = (4 * turn + unit) * items + item
                count, source, target = kcnt[entry], koff[entry] - turn * stride, kdst[entry]

                def step(part, none):
                    src = pl.ds(pl.multiple_of(source + 64 * part, 16), 64)
                    dst = pl.ds(pl.multiple_of(target + 64 * part, 16), 64)
                    ns_ref[dst, :] = n_refs[turn][src, :]
                    return none

                return lax.fori_loop(0, (count + 63) // 64, step, none)

            for turn in range(steps):
                lax.fori_loop(0, 4, functools.partial(one_unit, turn), 0)
            end = kstart[item] + klen[item]

            def clear(part, none):
                tail = pl.ds(pl.multiple_of(end + 64 * part, 16), 64)
                ns_ref[tail, :] = jnp.zeros((64, width), BF16)
                return none

            lax.fori_loop(0, (kstart[item + 1] - end + 63) // 64 + 1, clear, 0)

        for_items(items, klen, one_item)

        def clear(part, none):
            tail = pl.ds(pl.multiple_of(used + 64 * part, 16), 64)
            ns_ref[tail, :] = jnp.zeros((64, width), BF16)
            return none

        lax.fori_loop(0, (ns_ref.shape[0] - used) // 64, clear, 0)

    def project(block, none):
        here = pl.ds(pl.multiple_of(block * ROWS, ROWS), ROWS)
        rows = ns_ref[here, :]
        ks_ref[here, :] = jnp.dot(rows, wk_ref[...], preferred_element_type=F32).astype(BF16)
        vs_ref[here, :] = jnp.dot(rows, wv_ref[...], preferred_element_type=F32).astype(BF16)
        return none

    lax.fori_loop(0, (used + ROWS - 1) // ROWS, project, 0)

    def one_item(item, size, blocks):
        def some_queries(place, count):
            wide = count * cols
            rows = pl.ds(pl.multiple_of(place * QROWS, QROWS), count * QROWS)
            block = q_ref[rows, :]
            queries = jnp.concatenate(
                [spread(block[n * QROWS : (n + 1) * QROWS], heads) for n in range(count)], axis=0
            )
            top, total, acc = top_ref.at[:, :wide], total_ref.at[:, :wide], acc_ref.at[:wide]
            top[...] = jnp.full((8, wide), NEG, F32)
            total[...] = jnp.zeros((8, wide), F32)
            acc[...] = jnp.zeros((wide, heads * HEAD), F32)

            def step(number, none):
                here = pl.ds(pl.multiple_of(kstart[item] + number * size, 16), size)
                scores = lax.dot_general(
                    ks_ref[here, :], queries, NT, preferred_element_type=F32
                ) + lanes(bias_ref[here, :], wide)
                best = jnp.max(jnp.max(scores.reshape(size // 8, 8, wide), axis=0), axis=0)
                old = top[...]
                best = jnp.maximum(old, jnp.broadcast_to(best[None], (8, wide)))
                top[...] = best
                shrink = jnp.exp(old - best)
                weights = jnp.exp(scores - best[:1])
                total[...] = total[...] * shrink + jnp.sum(
                    weights.reshape(size // 8, 8, wide), axis=0
                )
                acc[...] = acc[...] * as_column(shrink) + lax.dot_general(
                    weights.astype(BF16),
                    vs_ref[here, :],
                    (((0,), (0,)), ((), ())),
                    preferred_element_type=F32,
                )
                return none

            lax.fori_loop(0, blocks, step, 0)
            summed = jnp.broadcast_to(jnp.sum(total[...], axis=0, keepdims=True), (8, wide))
            lse = top[...] + jnp.log(summed)
            out = acc[...] * as_column(1.0 / summed)
            for n in range(count):
                part = slice(n * cols, (n + 1) * cols)
                lse_ref[pl.ds(place + n, 1), :] = lse[:1, part]
                o_ref[pl.ds(pl.multiple_of((place + n) * QROWS, QROWS), QROWS), :] = gathered(
                    out[part], heads
                )

        query_blocks(qfirst[item], qcount[item], some_queries)

    for_items(items, klen, one_item)


def attend_back_kernel(
    heads, units, items,
    koff, kcnt, kdst, kstart, klen, qfirst, qcount,
    q_ref, do_ref, o_ref, lse_ref, ks_ref, vs_ref, wk_ref, wv_ref, ns_ref, bias_ref,
    dq_ref, gk_ref, gv_ref, dn_ref,
    spread_q, spread_do, delta, dq_acc, dk_acc, dv_acc, gk_acc, gv_acc, dn_acc,
):
    feats = heads * HEAD
    cols = heads * QROWS
    flip = (((0,), (0,)), ((), ()))
    dq_ref[...] = jnp.zeros_like(dq_ref)
    gk_acc[...] = jnp.zeros_like(gk_acc)
    gv_acc[...] = jnp.zeros_like(gv_acc)
    used = qfirst[items - 1] + qcount[items - 1]

    @pl.when(pl.program_id(0) == 0)
    def _():
        dn_acc[...] = jnp.zeros_like(dn_acc)

    def prepare(place, none):
        rows = pl.ds(pl.multiple_of(place * QROWS, QROWS), QROWS)
        grads = do_ref[rows, :]
        spread_q[place] = spread(q_ref[rows, :], heads)
        spread_do[place] = spread(grads, heads)
        product = spread(grads.astype(F32) * o_ref[rows, :], heads)
        delta[place] = lax.dot_general(
            jnp.ones((8, feats), F32), product, NT, precision=HIGH, preferred_element_type=F32
        )
        dq_acc[place] = jnp.zeros((cols, feats), F32)
        return none

    lax.fori_loop(0, used, prepare, 0)

    def one_item(item, size, blocks):
        def one_block(number, none):
            here = pl.ds(pl.multiple_of(kstart[item] + number * size, 16), size)
            dk_acc[:size] = jnp.zeros((size, feats), F32)
            dv_acc[:size] = jnp.zeros((size, feats), F32)

            def some_queries(place, count):
                wide = count * cols
                spot = pl.ds(place, count)
                queries = spread_q[spot].reshape(wide, feats)
                grads = spread_do[spot].reshape(wide, feats)
                row = [lse_ref[pl.ds(place + n, 1), :] for n in range(count)]
                log_total = jnp.concatenate(row, axis=1)
                shift = jnp.concatenate([delta[place + n, :1, :] for n in range(count)], axis=1)
                keys = ks_ref[here, :]
                scores = lax.dot_general(keys, queries, NT, preferred_element_type=F32)
                weights = jnp.exp(scores + lanes(bias_ref[here, :], wide) - log_total)
                slopes = lax.dot_general(vs_ref[here, :], grads, NT, preferred_element_type=F32)
                score_grads = (weights * (slopes - shift)).astype(BF16)
                dv_acc[:size] += jnp.dot(weights.astype(BF16), grads, preferred_element_type=F32)
                dk_acc[:size] += jnp.dot(score_grads, queries, preferred_element_type=F32)
                part = lax.dot_general(score_grads, keys, flip, preferred_element_type=F32)
                dq_acc[spot] += part.reshape(count, cols, feats)

            query_blocks(qfirst[item], qcount[item], some_queries)
            dk = dk_acc[:size].astype(BF16)
            dv = dv_acc[:size].astype(BF16)
            dn_acc[here, :] += (
                lax.dot_general(dk, wk_ref[...], NT, preferred_element_type=F32)
                + lax.dot_general(dv, wv_ref[...], NT, preferred_element_type=F32)
            ).astype(dn_acc.dtype)
            rows = ns_ref[here, :]
            gk_acc[...] += lax.dot_general(rows, dk, flip, preferred_element_type=F32)
            gv_acc[...] += lax.dot_general(rows, dv, flip, preferred_element_type=F32)
            return none

        lax.fori_loop(0, jnp.where(qcount[item] > 0, blocks, 0), one_block, 0)

    for_items(items, klen, one_item)

    def finish(place, none):
        rows = pl.ds(pl.multiple_of(place * QROWS, QROWS), QROWS)
        scale = 1.0 / math.sqrt(HEAD)
        dq_ref[rows, :] = (gathered(dq_acc[place], heads) * scale).astype(BF16)
        return none

    lax.fori_loop(0, used, finish, 0)
    gk_ref[...] = gk_acc[...].astype(BF16)
    gv_ref[...] = gv_acc[...].astype(BF16)

    @pl.when(pl.program_id(0) == pl.num_programs(0) - 1)
    def _():
        dn_ref[...] = jnp.zeros_like(dn_ref)

        def one_unit(unit, none):
            def one_item(item, none):
                entry = unit * items + item
                count, source, target = kcnt[entry], koff[entry], kdst[entry]

                def step(part, none):
                    src = pl.ds(pl.multiple_of(source + 64 * part, 16), 64)
                    dst = pl.ds(pl.multiple_of(target + 64 * part, 16), 64)
                    dn_ref[src, :] = dn_acc[dst, :].astype(BF16)
                    return none

                return lax.fori_loop(0, (count + 63) // 64, step, none)

            return lax.fori_loop(0, items, one_item, none)

        lax.fori_loop(0, units, one_unit, 0)


def attend(tables, query, bias, key_weight, value_weight, norms, units, items, heads):
    feats = heads * HEAD
    cols = heads * QROWS
    width = query.shape[1]
    groups = width // feats
    blocks8 = (query.shape[0] // QROWS + 7) // 8 * 8
    sorted_keys = bias.shape[0]
    once = pl.Buffered(1) if units > 16 else None

    def part(rows, columns=feats):
        return pl.BlockSpec((rows, columns), lambda group, *_: (0, group), pipeline_mode=once)

    def whole(rows, columns):
        return pl.BlockSpec(
            (rows, columns), lambda group, *_: (0, 0), pipeline_mode=pl.Buffered(1)
        )

    return pl.pallas_call(
        functools.partial(attend_kernel, heads, units, items),
        grid_spec=pltpu.PrefetchScalarGridSpec(
            num_scalar_prefetch=7,
            grid=(groups,),
            in_specs=[part(query.shape[0]), whole(sorted_keys, 128), part(width), part(width)]
            + [whole(*norm.shape) for norm in norms],
            out_specs=[
                part(query.shape[0]),
                part(blocks8, cols),
                whole(sorted_keys, width),
                part(sorted_keys),
                part(sorted_keys),
            ],
            scratch_shapes=[
                pltpu.VMEM((2 * cols, feats), F32),
                pltpu.VMEM((8, 2 * cols), F32),
                pltpu.VMEM((8, 2 * cols), F32),
            ],
        ),
        out_shape=[
            jax.ShapeDtypeStruct(query.shape, F32),
            jax.ShapeDtypeStruct((blocks8, groups * cols), F32),
            jax.ShapeDtypeStruct((sorted_keys, width), BF16),
            jax.ShapeDtypeStruct((sorted_keys, width), BF16),
            jax.ShapeDtypeStruct((sorted_keys, width), BF16),
        ],
        compiler_params=pltpu.CompilerParams(vmem_limit_bytes=VMEM),
        name="attend",
    )(*tables, query, bias, key_weight, value_weight, *norms)


def attend_back(
    tables, query, grads, outputs, lse, ks, vs, key_weight, value_weight, ns, bias,
    key_rows, units, items, heads,
):
    feats = heads * HEAD
    cols = heads * QROWS
    rows, width = query.shape
    groups = width // feats
    blocks = rows // QROWS
    once = pl.Buffered(1) if units > 16 else None

    def part(rows, columns=feats):
        return pl.BlockSpec((rows, columns), lambda group, *_: (0, group), pipeline_mode=once)

    def whole(rows, columns):
        return pl.BlockSpec(
            (rows, columns), lambda group, *_: (0, 0), pipeline_mode=pl.Buffered(1)
        )

    return pl.pallas_call(
        functools.partial(attend_back_kernel, heads, units, items),
        grid_spec=pltpu.PrefetchScalarGridSpec(
            num_scalar_prefetch=7,
            grid=(groups,),
            in_specs=[
                part(rows),
                part(rows),
                part(rows),
                part(lse.shape[0], cols),
                part(ks.shape[0]),
                part(ks.shape[0]),
                part(width),
                part(width),
                whole(*ns.shape),
                whole(*bias.shape),
            ],
            out_specs=[part(rows), part(width), part(width), whole(key_rows, width)],
            scratch_shapes=[
                pltpu.VMEM((blocks, cols, feats), BF16),
                pltpu.VMEM((blocks, cols, feats), BF16),
                pltpu.VMEM((blocks, 8, cols), F32),
                pltpu.VMEM((blocks, cols, feats), F32),
                pltpu.VMEM((SPARE_KEYS, feats), F32),
                pltpu.VMEM((SPARE_KEYS, feats), F32),
                pltpu.VMEM((width, feats), F32),
                pltpu.VMEM((width, feats), F32),
                pltpu.VMEM(ns.shape, BF16),
            ],
        ),
        out_shape=[
            jax.ShapeDtypeStruct(query.shape, BF16),
            jax.ShapeDtypeStruct((width, width), BF16),
            jax.ShapeDtypeStruct((width, width), BF16),
            jax.ShapeDtypeStruct((key_rows, width), BF16),
        ],
        compiler_params=pltpu.CompilerParams(vmem_limit_bytes=VMEM),
        name="attend_back",
    )(*tables, query, grads, outputs, lse, ks, vs, key_weight, value_weight, ns, bias)


@functools.cache
def most_rows(cycle_size, item_count):
    rows = np.arange(SLOTS)[:, None] * cycle_size + np.arange(cycle_size)
    most_keys = most_unit = most_queries = 0
    lists = [()]
    while lists:
        heights = lists.pop()
        if len(heights) < item_count:
            for height in (24, 30):
                if sum(heights) + height <= SLOTS * cycle_size:
                    lists.append(heights + (height,))
        if not heights:
            continue
        ends = np.cumsum(heights)
        number = np.searchsorted(ends, rows, side="right")
        wide = np.array([24 if height == 24 else ROWW for height in heights] + [0])[number]
        kinds = np.arange(len(heights))
        counts = [((number == kind) * wide) for kind in kinds] + [ROWW - wide]
        counts = np.stack(counts)

        def rounded(values, align):
            return -(-values // align) * align

        units = rounded(counts.reshape(len(counts), 2, HALF, cycle_size).sum(2), 16)
        most_unit = max(most_unit, units.sum(0).max())
        keys = units.sum((1, 2))
        keys = rounded(keys[:-1], KEYS).sum() + rounded(keys[-1], SPARE_KEYS)
        most_keys = max(most_keys, keys)
        most_queries = max(most_queries, rounded(counts.sum(1), QROWS).sum(0).max())
    return int(most_keys), int(most_unit), int(most_queries)


def passed(value, axis, target):
    pairs = [(source, target(source)) for source in range(lax.axis_size(axis))]
    return lax.ppermute(value, axis, pairs)


def passed_along(value, axis, steps):
    count = lax.axis_size(axis)
    return passed(value, axis, lambda source: (source + steps) % count)


def to_sibling(value):
    return passed(value, "blk", lambda source: source ^ 1)


def gelu_tanh(values):
    return (
        0.5
        * values
        * (1.0 + jnp.tanh(0.7978845608028654 * (values + 0.044715 * values * values * values)))
    )


def gelu_back(values, gradient):
    return jax.vjp(gelu_tanh, values)[1](gradient)[0]


def layer_norm(hidden, norm_gain, norm_bias):
    centred = hidden - jnp.mean(hidden, axis=-1, keepdims=True)
    spread_now = jnp.mean(centred * centred, axis=-1, keepdims=True)
    return centred * lax.rsqrt(spread_now + EPS) * norm_gain + norm_bias


def row_facts(lengths, row_ids):
    item_count = lengths.shape[0]
    heights = jnp.where(lengths == 1200, 30, jnp.where(lengths == 576, 24, 0)).astype(jnp.int32)
    widths = jnp.where(lengths == 1200, 40, 24).astype(jnp.int32)
    upto = jnp.arange(item_count)[None, :] <= jnp.arange(item_count)[:, None]
    ends = jnp.sum(jnp.where(upto, heights[None, :], 0), axis=1)
    number = jnp.sum((ends <= row_ids[..., None]).astype(jnp.int32), axis=-1)
    number = jnp.where(row_ids < 0, item_count, number)
    pick = number[..., None] == jnp.arange(item_count, dtype=jnp.int32)
    start = jnp.sum(jnp.where(pick, ends - heights, 0), axis=-1)
    height = jnp.sum(jnp.where(pick, heights, 0), axis=-1)
    width = jnp.sum(jnp.where(pick, widths, 0), axis=-1)
    return number, pick, row_ids - start, height, width


def tap_masks(local_row, height, width):
    column = jnp.arange(ROWW, dtype=jnp.int32)
    is_real = column[None, :] < width[:, None]
    all_masks = []
    for row_step in (-1, 0, 1):
        rows_fine = (local_row + row_step >= 0) & (local_row + row_step < height)
        for col_step in (-1, 0, 1):
            cols_fine = (column + col_step >= 0)[None, :] & (
                column[None, :] + col_step < width[:, None]
            )
            all_masks.append(is_real & rows_fine[:, None] & cols_fine)
    return is_real, all_masks


def segments(number, width, item_count, align):
    slots = number.shape[1]
    kinds = jnp.arange(item_count + 1, dtype=jnp.int32)
    here = number[:, :, None] == kinds
    counts = jnp.sum(jnp.where(here, width[:, :, None], 0), axis=1)
    spare = jnp.sum(ROWW - width, axis=1)
    counts = jnp.where(kinds == item_count, spare[:, None], counts)
    rounded = (counts + align - 1) // align * align
    before = kinds[:, None] < kinds[None, :]
    offsets = jnp.sum(jnp.where(before, rounded[:, :, None], 0), axis=1)
    own_offset = jnp.sum(jnp.where(here, offsets[:, None, :], 0), axis=2)
    earlier = jnp.arange(slots)[None, :] < jnp.arange(slots)[:, None]
    same = earlier & (number[:, :, None] == number[:, None, :])
    rank = jnp.sum(jnp.where(same, width[:, None, :], 0), axis=2)
    spare_rank = jnp.sum(jnp.where(earlier, ROWW - width[:, None, :], 0), axis=2)
    column = jnp.arange(ROWW, dtype=jnp.int32)
    place = jnp.where(
        column < width[:, :, None],
        (own_offset + rank)[:, :, None] + column,
        (offsets[:, -1:] + spare_rank - width)[:, :, None] + column,
    )
    return counts, rounded, offsets, place


def one_hot_rows(place, rows):
    flat = place.reshape(place.shape[0], 1, -1)
    return (flat == jnp.arange(rows, dtype=jnp.int32)[None, :, None]).astype(BF16)


def side_shift(values, col_step):
    if col_step == 0:
        return values
    empty_col = jnp.zeros_like(values[:, :1])
    if col_step < 0:
        return jnp.concatenate([empty_col, values[:, :-1]], axis=1)
    return jnp.concatenate([values[:, 1:], empty_col], axis=1)


def row_shift(values, row_step):
    empty_row = jnp.zeros_like(values[:1])
    if row_step == 0:
        return values
    if row_step < 0:
        return jnp.concatenate([empty_row, values[:-1]], axis=0)
    return jnp.concatenate([values[1:], empty_row], axis=0)


def tap_matrix(values, all_masks):
    tap_parts = []
    for row_step in (-1, 0, 1):
        for col_step in (-1, 0, 1):
            tap_parts.append(
                jnp.where(
                    all_masks[len(tap_parts)][:, :, None],
                    side_shift(row_shift(values, row_step), col_step),
                    jnp.zeros((), values.dtype),
                )
            )
    joined = jnp.concatenate(tap_parts, axis=2)
    return joined.reshape(-1, joined.shape[2])


def flipped(kernel):
    channels = kernel.shape[1]
    return jnp.transpose(kernel.reshape(9, channels, channels)[::-1], (0, 2, 1)).reshape(
        9 * channels, channels
    )


def from_above(values, cycle_pos):
    got = passed_along(values, "blk", 1)
    empty_row = jnp.zeros_like(values[:1])
    return jnp.where(cycle_pos == 0, jnp.concatenate([empty_row, got[:-1]], axis=0), got)


def from_below(values, cycle_pos, cycle_size):
    got = passed_along(values, "blk", -1)
    empty_row = jnp.zeros_like(values[:1])
    return jnp.where(
        cycle_pos == cycle_size - 1, jnp.concatenate([got[1:], empty_row], axis=0), got
    )


def upsample_forward(values, all_masks, cycle_pos, cycle_size):
    center = values.astype(F32)
    row_above = from_above(values, cycle_pos)
    row_below = from_below(values, cycle_pos, cycle_size)
    upper_value = jnp.where(all_masks[1][:, :, None], row_above, values).astype(F32)
    lower_value = jnp.where(all_masks[7][:, :, None], row_below, values).astype(F32)
    pieces = []
    for half_rows in (0.75 * center + 0.25 * upper_value, 0.75 * center + 0.25 * lower_value):
        left_value = jnp.where(all_masks[3][:, :, None], side_shift(half_rows, -1), half_rows)
        right_value = jnp.where(all_masks[5][:, :, None], side_shift(half_rows, 1), half_rows)
        pieces.append(0.75 * half_rows + 0.25 * left_value)
        pieces.append(0.75 * half_rows + 0.25 * right_value)
    joined = jnp.concatenate(pieces, axis=2)
    return joined.reshape(-1, joined.shape[2])


def upsample_back(gradient, all_masks, cycle_pos, cycle_size):
    channels = gradient.shape[2] // 4
    left_fine = all_masks[3][:, :, None]
    right_fine = all_masks[5][:, :, None]
    up_fine = all_masks[1][:, :, None]
    down_fine = all_masks[7][:, :, None]
    halves = []
    for half in (0, 1):
        left_part = gradient[:, :, 2 * half * channels : (2 * half + 1) * channels].astype(F32)
        right_part = gradient[:, :, (2 * half + 1) * channels : (2 * half + 2) * channels].astype(
            F32
        )
        side = jnp.where(right_fine, side_shift(left_part, 1), 0.0)
        side = side + jnp.where(left_fine, 0.0, left_part)
        side = side + jnp.where(left_fine, side_shift(right_part, -1), 0.0)
        side = side + jnp.where(right_fine, 0.0, right_part)
        halves.append(0.75 * (left_part + right_part) + 0.25 * side)
    upper, lower = halves
    upper_next = from_below(upper.astype(BF16), cycle_pos, cycle_size).astype(F32)
    lower_prev = from_above(lower.astype(BF16), cycle_pos).astype(F32)
    rows = jnp.where(down_fine, upper_next, lower) + jnp.where(up_fine, lower_prev, upper)
    return 0.75 * (upper + lower) + 0.25 * rows


def first_slot(begin, device, cycle_size):
    return -((device - begin) // cycle_size)


def to_windows(values, cycle_pos, cycle_size):
    window = SLOTS + 2 * REACH
    many = -(-window // cycle_size)
    spare = many + 1
    padded = jnp.pad(values, ((spare, spare), (0, 0), (0, 0)))
    sends = []
    for target in range(cycle_size):
        slot = first_slot(SLOTS * target - REACH, cycle_pos, cycle_size) + spare
        sends.append(lax.dynamic_slice_in_dim(padded, slot, many, axis=0))
    got = lax.all_to_all(jnp.stack(sends), "blk", 0, 0)
    got = jnp.swapaxes(got, 0, 1)
    begin = SLOTS * cycle_pos - REACH
    turn = begin - (begin // cycle_size) * cycle_size
    got = lax.dynamic_slice_in_dim(jnp.concatenate([got, got], axis=1), turn, cycle_size, axis=1)
    return got.reshape((many * cycle_size,) + values.shape[1:])[:window]


def from_windows(values, cycle_pos, cycle_size):
    many = -(-SLOTS // cycle_size)
    padded = jnp.pad(values, ((0, many * cycle_size), (0, 0), (0, 0)))
    begin = SLOTS * cycle_pos
    sends = []
    for target in range(cycle_size):
        slot = first_slot(begin, target, cycle_size)
        for extra in range(many):
            row = (slot + extra) * cycle_size + target - begin
            sends.append(lax.dynamic_slice_in_dim(padded, row, 1, axis=0))
    sends = jnp.concatenate(sends, axis=0).reshape((cycle_size, many) + values.shape[1:])
    got = lax.all_to_all(sends, "blk", 0, 0).reshape((cycle_size * many,) + values.shape[1:])
    rows = []
    for slot in range(SLOTS):
        row = slot * cycle_size + cycle_pos
        source = row // SLOTS
        extra = slot - first_slot(source * SLOTS, cycle_pos, cycle_size)
        rows.append(lax.dynamic_slice_in_dim(got, source * many + extra, 1, axis=0))
    return jnp.concatenate(rows, axis=0)


def dot32(left, right, **more):
    return jnp.dot(left, right, preferred_element_type=F32, **more)


def dot_t(left, right):
    return lax.dot_general(left, right, NT, preferred_element_type=F32)


def t_dot(left, right):
    return lax.dot_general(left, right, (((0,), (0,)), ((), ())), preferred_element_type=F32)


def halved(values, device, bit, axis, pairs_axis):
    half = values.shape[axis] // 2
    mine = (device >> bit) & 1
    keep = lax.dynamic_slice_in_dim(values, mine * half, half, axis=axis)
    send = lax.dynamic_slice_in_dim(values, (1 - mine) * half, half, axis=axis)
    got = passed(send, pairs_axis, lambda source: source ^ (1 << bit))
    return (keep.astype(F32) + got.astype(F32)).astype(BF16)


def added_over_group(shares, order, cycle_pos, dp_pos):
    cycle_size, rows, width = shares.shape
    chips = cycle_size // 2
    core = cycle_pos % 2
    paired = shares.reshape(chips, 2, rows, width)
    keep = lax.dynamic_index_in_dim(paired, core, 1, keepdims=False)
    send = lax.dynamic_index_in_dim(paired, 1 - core, 1, keepdims=False)
    values = (keep.astype(F32) + to_sibling(send).astype(F32)).astype(BF16)
    for bit in order:
        values = halved(values, dp_pos, bit, 1, "dp")
    return values


def added_over_chips(values, chip):
    chips = values.shape[0]

    def block(offset):
        return lax.dynamic_index_in_dim(
            values, (chip + offset) % chips, 0, keepdims=False
        ).astype(F32)

    moving = block(-1)
    for step in range(2, chips + 1):
        moving = passed_along(moving.astype(BF16), "blk", 2).astype(F32) + block(-step)
    return moving.astype(BF16)


def gathered_over_groups(values, dp_pos):
    groups = lax.axis_size("dp")
    bits = groups.bit_length() - 1
    half = values.shape[0] // 2
    both = []
    for part, order in ((values[:half], range(bits)), (values[half:], range(bits - 1, -1, -1))):
        held = part[(None,) * bits]
        for bit in order:
            axis = bits - 1 - bit
            got = passed(held, "dp", lambda source, bit=bit: source ^ (1 << bit))
            mine = (dp_pos >> bit) & 1
            held = jnp.where(
                mine == 0,
                jnp.concatenate([held, got], axis=axis),
                jnp.concatenate([got, held], axis=axis),
            )
        both.append(held.reshape((groups,) + part.shape))
    return jnp.concatenate(both, axis=1)


def reduced(gradients, cycle_size, cycle_pos, dp_pos):
    groups = lax.axis_size("dp")
    bits = groups.bit_length() - 1
    orders, parts = [], []
    for number, gradient in enumerate(gradients):
        order = list(range(bits))
        if number % 2:
            order.reverse()
        orders.append(order)
        parts.append(added_over_group(gradient, order, cycle_pos, dp_pos))
    chips = cycle_size // 2
    joined = jnp.concatenate([part.reshape(chips, -1, 256) for part in parts], axis=1)
    whole = gathered_over_groups(added_over_chips(joined, cycle_pos // 2), dp_pos)
    out, place = [], 0
    for gradient, order in zip(gradients, orders):
        rows, width = gradient.shape[1:]
        size = rows * width // groups // 256
        pieces = []
        for turn in range(groups):
            device = sum(((turn >> (bits - 1 - index)) & 1) << bit for index, bit in enumerate(order))
            pieces.append(whole[device, place : place + size].reshape(rows // groups, width))
        out.append(jnp.concatenate(pieces, axis=0).astype(F32))
        place += size
    return out


def shards(
    tokens,
    item_lengths,
    dataset_ids,
    dataset_table,
    norm1_gain,
    norm1_bias,
    query_weight,
    key_weight,
    value_weight,
    out_weight,
    norm2_gain,
    norm2_bias,
    fc1_weight,
    fc2_weight,
    project_weight,
    unit1_first,
    unit1_second,
    unit2_first,
    unit2_second,
    output_weight,
    block_cotangent,
    merged_cotangent,
):
    cycle_size = lax.axis_size("blk")
    cycle_pos = lax.axis_index("blk")
    chips = cycle_size // 2
    chip, core = cycle_pos // 2, cycle_pos % 2
    lengths = item_lengths[0]
    item_count = lengths.shape[0]
    kinds = item_count + 1
    width_model = tokens.shape[1]
    heads = 4 if cycle_size <= 8 else 2
    half_tokens = HALF * ROWW
    token_count = tokens.shape[0]

    ahead, behind = tokens[:half_tokens], tokens[half_tokens:]
    arrivals = []
    for step in range(chips):
        if step:
            ahead = passed_along(ahead, "blk", 2)
            behind = passed_along(behind, "blk", -2)
        mine = jnp.concatenate([ahead, behind], axis=0)
        arrivals.append((mine, to_sibling(mine)))

    slots = jnp.arange(SLOTS, dtype=jnp.int32)
    number, item_pick, local_row, height, width = row_facts(lengths, slots * cycle_size + cycle_pos)
    is_real, all_masks = tap_masks(local_row, height, width)
    unit_rows = []
    for step in range(chips):
        for other in (0, 1):
            for half, turn in ((0, -step), (1, step)):
                source = 2 * ((chip + turn) % chips) + (core ^ other)
                unit_rows.append(slots[half * HALF : (half + 1) * HALF] * cycle_size + source)
    unit_rows = jnp.stack(unit_rows)
    units = 4 * chips
    unit_number, unit_pick, _, _, unit_width = row_facts(lengths, unit_rows)
    most_keys, unit_size, query_rows = most_rows(cycle_size, item_count)
    kcnt, krounded, koff, kplace = segments(unit_number, unit_width, item_count, 16)
    unit_spots = jnp.arange(units, dtype=jnp.int32)
    step_rows = 4 * unit_size + 64
    koff = koff + (unit_spots // 4 * step_rows + unit_spots % 4 * unit_size)[:, None]
    klen = jnp.sum(krounded, axis=0)
    size = jnp.where(jnp.arange(kinds) == kinds - 1, SPARE_KEYS, KEYS)
    klen_up = (klen + size - 1) // size * size
    before = jnp.arange(kinds)[:, None] < jnp.arange(kinds + 1)[None, :]
    kstart = jnp.sum(jnp.where(before, klen_up[:, None], 0), axis=0)
    unit_before = jnp.arange(units)[:, None] < jnp.arange(units)[None, :]
    kdst = kstart[None, :kinds] + jnp.sum(
        jnp.where(unit_before[:, :, None], krounded[:, None, :], 0), axis=0
    )
    key_rows = chips * step_rows
    sorted_keys = (most_keys + 128 + ROWS - 1) // ROWS * ROWS
    spot = jnp.arange(sorted_keys, dtype=jnp.int32)[:, None]
    filled = (spot >= kdst.reshape(1, -1)) & (spot < (kdst + kcnt).reshape(1, -1))
    bias = jnp.where(jnp.any(filled, axis=1), 0.0, NEG)
    bias = jnp.broadcast_to(bias[:, None], (sorted_keys, 128)).astype(F32)
    _, qrounded, qoff, qplace = segments(number[None], width[None], item_count, QROWS)
    tables = (
        koff.reshape(-1),
        kcnt.reshape(-1),
        kdst.reshape(-1),
        kstart,
        klen,
        qoff[0] // QROWS,
        qrounded[0] // QROWS,
    )
    sort_units = one_hot_rows(kplace, unit_size)
    sort_queries = one_hot_rows(qplace, query_rows)[0]
    table_rows = dataset_table.shape[0]

    def dataset_one_hot(pick, widths):
        dataset = jnp.sum(jnp.where(pick, dataset_ids[0], 0), axis=-1)
        real = jnp.arange(ROWW, dtype=jnp.int32) < widths[..., None]
        hot = real[..., None] & (
            dataset[..., None, None] == jnp.arange(table_rows, dtype=jnp.int32)
        )
        return hot.astype(F32).reshape(-1, table_rows)

    def with_dataset(values, hot):
        return values.astype(F32) + jnp.dot(hot, dataset_table, precision=HIGH)

    onehot = dataset_one_hot(item_pick, width)

    sorted_norms = []
    for step in range(chips):
        here = slice(4 * step, 4 * step + 4)
        hot = dataset_one_hot(unit_pick[here], unit_width[here])
        values = with_dataset(jnp.concatenate(arrivals[step], axis=0), hot)
        normed = layer_norm(values, norm1_gain, norm1_bias).astype(BF16)
        normed = jnp.einsum(
            "upt,utd->upd",
            sort_units[here],
            normed.reshape(4, half_tokens, width_model),
            preferred_element_type=F32,
        ).astype(BF16)
        normed = jnp.pad(normed.reshape(4 * unit_size, width_model), ((0, 64), (0, 0)))
        sorted_norms.append(normed)

    stream_start = with_dataset(tokens, onehot)
    normed_one = layer_norm(stream_start, norm1_gain, norm1_bias).astype(BF16)
    query_norm = dot32(sort_queries, normed_one).astype(BF16)
    query = (dot32(query_norm, query_weight) * (1.0 / math.sqrt(HEAD))).astype(BF16)
    outputs, lse, sorted_norm, ks, vs = attend(
        tables, query, bias, key_weight, value_weight, sorted_norms, units, kinds, heads
    )
    attended = t_dot(sort_queries, outputs.astype(BF16)).astype(BF16)

    def as_cells(flattened):
        return flattened.reshape(SLOTS, ROWW, flattened.shape[-1])

    after_attn = stream_start + dot32(attended, out_weight)
    normed_two = layer_norm(after_attn, norm2_gain, norm2_bias).astype(BF16)
    pre_act = dot32(normed_two, fc1_weight)
    hidden = gelu_tanh(pre_act).astype(BF16)
    block_out = (after_attn + dot32(hidden, fc2_weight)).astype(BF16)
    reassembled_own = dot32(block_out, project_weight).astype(BF16)

    mapped_grad_own = upsample_back(
        as_cells(merged_cotangent), all_masks, cycle_pos, cycle_size
    ).astype(BF16)
    channels = mapped_grad_own.shape[-1]
    arrived = to_windows(
        jnp.concatenate([as_cells(reassembled_own), mapped_grad_own], axis=2), cycle_pos, cycle_size
    )
    window = SLOTS + 2 * REACH
    _, _, w_row, w_height, w_width = row_facts(
        lengths, SLOTS * cycle_pos - REACH + jnp.arange(window, dtype=jnp.int32)
    )
    _, w_masks = tap_masks(w_row, w_height, w_width)
    reassembled = arrived[:, :, :channels].reshape(-1, channels).astype(F32)
    mapped_grad = arrived[:, :, channels:].reshape(-1, channels)
    middle = slice(REACH * ROWW, (REACH + SLOTS) * ROWW)

    def grid(flattened):
        return flattened.reshape(window, ROWW, channels)

    def stencil(values, kernel):
        taps_now = tap_matrix(grid(values), w_masks)
        return taps_now[middle], dot32(taps_now, kernel)

    def stencil_back(gradient, kernel):
        return dot32(tap_matrix(grid(gradient), w_masks), flipped(kernel))

    taps_one, conv_one = stencil(gelu_tanh(reassembled).astype(BF16), unit1_first)
    taps_two, conv_two = stencil(gelu_tanh(conv_one).astype(BF16), unit1_second)
    merged_one = reassembled + conv_two
    taps_three, conv_three = stencil(gelu_tanh(merged_one).astype(BF16), unit2_first)
    taps_four, conv_four = stencil(gelu_tanh(conv_three).astype(BF16), unit2_second)
    merged_low = (merged_one + conv_four).astype(BF16)[middle]
    mapped = dot32(merged_low, output_weight).astype(BF16)
    output_grad = t_dot(merged_low, mapped_grad[middle])
    merged_two_grad = dot_t(mapped_grad, output_weight)
    conv_four_grad = merged_two_grad.astype(BF16)
    unit2_second_grad = t_dot(taps_four, conv_four_grad[middle])
    conv_three_grad = gelu_back(conv_three, stencil_back(conv_four_grad, unit2_second)).astype(BF16)
    unit2_first_grad = t_dot(taps_three, conv_three_grad[middle])
    merged_one_grad = merged_two_grad + gelu_back(
        merged_one, stencil_back(conv_three_grad, unit2_first)
    )
    conv_two_grad = merged_one_grad.astype(BF16)
    unit1_second_grad = t_dot(taps_two, conv_two_grad[middle])
    conv_one_grad = gelu_back(conv_one, stencil_back(conv_two_grad, unit1_second)).astype(BF16)
    unit1_first_grad = t_dot(taps_one, conv_one_grad[middle])
    reassembled_grad = (
        merged_one_grad + gelu_back(reassembled, stencil_back(conv_one_grad, unit1_first))
    ).astype(BF16)[middle]

    returned = from_windows(
        jnp.concatenate([as_cells(reassembled_grad), as_cells(mapped)], axis=2),
        cycle_pos,
        cycle_size,
    )
    reassembled_grad = returned[:, :, :channels].reshape(-1, channels)
    merged = upsample_forward(returned[:, :, channels:], all_masks, cycle_pos, cycle_size).astype(
        BF16
    )

    project_grad = t_dot(block_out, reassembled_grad)
    block_grad = block_cotangent.astype(F32) + dot_t(reassembled_grad, project_weight)
    mlp_grad = block_grad.astype(BF16)
    fc2_grad = t_dot(hidden, mlp_grad)
    pre_grad = gelu_back(pre_act, dot_t(mlp_grad, fc2_weight)).astype(BF16)
    fc1_grad = t_dot(normed_two, pre_grad)
    normed_two_grad = dot_t(pre_grad, fc1_weight)
    norm_two_pull = jax.vjp(layer_norm, after_attn, norm2_gain, norm2_bias)[1]
    attn_side, norm2_gain_grad, norm2_bias_grad = norm_two_pull(normed_two_grad)
    after_grad = block_grad + attn_side
    branch_grad = after_grad.astype(BF16)
    out_proj_grad = t_dot(attended, branch_grad)
    attended_grad = dot_t(branch_grad, out_weight).astype(BF16)

    rows = width_model // cycle_size
    dp_pos = lax.axis_index("dp")

    def shared_out(*gradients):
        parts = []
        for gradient in gradients:
            parts.append(gradient.astype(BF16).reshape(cycle_size, -1, gradient.shape[-1]))
        return jnp.concatenate(parts, axis=1)

    early = reduced(
        [
            shared_out(
                unit1_first_grad,
                unit1_second_grad,
                unit2_first_grad,
                unit2_second_grad,
                output_grad,
                project_grad,
            ),
            shared_out(fc2_grad, out_proj_grad),
            shared_out(fc1_grad),
        ],
        cycle_size,
        cycle_pos,
        dp_pos,
    )
    unit_share = 9 * channels // cycle_size
    fc2_share = fc2_weight.shape[0] // cycle_size

    sorted_grad = dot32(sort_queries, attended_grad).astype(BF16)
    dq, key_grad, value_grad, unit_grad = attend_back(
        tables, query, sorted_grad, outputs, lse, ks, vs, key_weight, value_weight, sorted_norm,
        bias, key_rows, units, kinds, heads,
    )
    query_low = t_dot(sort_queries, dq).astype(BF16)
    query_grad = t_dot(normed_one, query_low)

    def unit_part(step):
        here = slice(step_rows * step, step_rows * step + 4 * unit_size)
        part = jnp.einsum(
            "upt,upd->utd",
            sort_units[4 * step : 4 * step + 4],
            unit_grad[here].reshape(4, unit_size, width_model),
            preferred_element_type=F32,
        )
        mine, other = part[:2], part[2:].astype(BF16)
        return mine + to_sibling(other).astype(F32)

    ahead = behind = None
    for step in range(chips - 1, -1, -1):
        part = unit_part(step)
        if ahead is None:
            ahead, behind = part[0], part[1]
        else:
            ahead = passed_along(ahead.astype(BF16), "blk", -2).astype(F32) + part[0]
            behind = passed_along(behind.astype(BF16), "blk", 2).astype(F32) + part[1]
    normed_one_grad = jnp.concatenate([ahead, behind], axis=0) + dot_t(query_low, query_weight)

    norm_one_pull = jax.vjp(layer_norm, stream_start, norm1_gain, norm1_bias)[1]
    start_side, norm1_gain_grad, norm1_bias_grad = norm_one_pull(normed_one_grad)
    tokens_grad = after_grad + start_side
    table_grad = jnp.dot(onehot.T, tokens_grad, precision=HIGH)
    table_split = jnp.swapaxes(table_grad.reshape(table_rows, cycle_size, rows), 0, 1)
    small = [table_split.reshape(cycle_size, -1)] + [
        gradient.reshape(cycle_size, -1)
        for gradient in (norm1_gain_grad, norm1_bias_grad, norm2_gain_grad, norm2_bias_grad)
    ]
    small = jnp.concatenate(small, axis=1).astype(BF16)
    small = jnp.pad(small, ((0, 0), (0, 32 * width_model - small.shape[1])))
    late = reduced(
        [
            jnp.concatenate(
                [
                    shared_out(query_grad, key_grad, value_grad),
                    small.reshape(cycle_size, 32, width_model),
                ],
                axis=1,
            )
        ],
        cycle_size,
        cycle_pos,
        dp_pos,
    )[0]
    small = late[3 * rows :].reshape(-1)
    table_size = table_rows * rows
    norms = [small[table_size + index * rows :][:rows] for index in range(4)]
    convs = early[0]
    return (
        block_out,
        merged,
        tokens_grad,
        small[:table_size].reshape(table_rows, rows),
        norms[0],
        norms[1],
        late[:rows],
        late[rows : 2 * rows],
        late[2 * rows : 3 * rows],
        early[1][fc2_share:],
        norms[2],
        norms[3],
        early[2],
        early[1][:fc2_share],
        convs[4 * unit_share + channels // cycle_size :],
        convs[:unit_share],
        convs[unit_share : 2 * unit_share],
        convs[2 * unit_share : 3 * unit_share],
        convs[3 * unit_share : 4 * unit_share],
        convs[4 * unit_share : 4 * unit_share + channels // cycle_size],
    )


def solution(mesh):
    split = P(("dp", "blk"), None)
    placed = (split, P("dp", None), P("dp", None)) + (P(),) * 17 + (split, split)
    rows, line = P("blk", None), P("blk")
    return jax.shard_map(
        shards,
        mesh=mesh,
        in_specs=placed,
        out_specs=(
            split, split, split, P(None, "blk"), line, line, rows, rows, rows, rows, line, line,
            rows, rows, rows, rows, rows, rows, rows, rows,
        ),
        check_vma=False,
    )
```

```python
import functools
import math
import typing

import jax
import jax.numpy as jnp
from jax import lax
from jax.experimental import pallas as pl
from jax.experimental.pallas import tpu as pltpu
from jax.sharding import PartitionSpec as P
import numpy as np

HEADS = 12
HEAD = 64
ROWW = 40
SLOTS = 12
HALF = SLOTS // 2
REACH = 6
PITCH = 48
CH = 256

NEG = -1e30
EPS = 1e-06
HIGH = lax.Precision.HIGHEST
KEYS = 672
SPARE_KEYS = 768
QROWS = 64
ROWS = 512
VMEM = 60 * 1024 * 1024
NT = (((1,), (1,)), ((), ()))
FLIP = (((0,), (0,)), ((), ()))
F32 = jnp.float32
BF16 = jnp.bfloat16


def cost(microseconds):
    return pl.CostEstimate(flops=microseconds * 10**9, bytes_accessed=10**6, transcendentals=0)


def own_blocks(heads, feats):
    row = lax.broadcasted_iota(jnp.int32, (heads * QROWS, feats), 0) // QROWS
    col = lax.broadcasted_iota(jnp.int32, (heads * QROWS, feats), 1) // HEAD
    return row == col


def spread(block, heads):
    wide = jnp.concatenate([block] * heads, axis=0)
    return jnp.where(own_blocks(heads, block.shape[1]), wide, jnp.zeros((), block.dtype))


def gathered(wide, heads):
    kept = jnp.where(own_blocks(heads, wide.shape[1]), wide, 0.0)
    total = kept[:QROWS]
    for head in range(1, heads):
        total = total + kept[head * QROWS : (head + 1) * QROWS]
    return total


def lanes(column, width):
    return jnp.concatenate([column] * (width // 128), axis=1)


class Tables(typing.NamedTuple):
    koff: jax.Array
    kcnt: jax.Array
    kdst: jax.Array
    kstart: jax.Array
    klen: jax.Array
    qfirst: jax.Array
    qcount: jax.Array
    ubase: jax.Array
    uspare: jax.Array
    uwidth: jax.Array
    uitem: jax.Array
    qbase: jax.Array
    qspare: jax.Array
    qwidth: jax.Array
    qitem: jax.Array
    wwidth: jax.Array
    wup: jax.Array
    wdown: jax.Array


TABLES = len(Tables._fields)


def geometry_kernel(cycle_size, unit_size, lengths, place, *refs):
    tab = Tables(*refs)
    item_count = lengths.shape[0]
    items = item_count + 1
    chips = cycle_size // 2
    units = 4 * chips
    me = place[0]
    chip, core = lax.div(me, 2), lax.rem(me, 2)
    facts, start = [], 0
    for item in range(item_count):
        length = lengths[item]
        height = jnp.where(length == 1200, 30, jnp.where(length == 576, 24, 0))
        facts.append((start, start + height, jnp.where(length == 1200, 40, 24)))
        start = start + height

    def fact(row):
        number, width = item_count, 0
        for item, (begin, end, item_width) in enumerate(facts):
            inside = (row >= begin) & (row < end)
            number = jnp.where(inside, item, number)
            width = jnp.where(inside, item_width, width)
        return number, width

    def up(value, align):
        return lax.div(value + (align - 1), align) * align

    def sort(rows, align, base, spare_base, widths, numbers, first):
        known = [fact(row) for row in rows]
        counts = [
            sum(jnp.where(number == item, width, 0) for number, width in known)
            for item in range(item_count)
        ]
        counts.append(sum(ROWW - width for _, width in known))
        offsets, total = [], 0
        for count in counts:
            offsets.append(total)
            total = total + up(count, align)
        spare = offsets[-1]
        for slot, (number, width) in enumerate(known):
            begin = sum(jnp.where(number == item, offsets[item], 0) for item in range(item_count))
            for other, other_width in known[:slot]:
                begin = begin + jnp.where(other == number, other_width, 0)
            base[first + slot] = begin
            spare_base[first + slot] = spare - width
            widths[first + slot] = width
            numbers[first + slot] = number
            spare = spare + ROWW - width
        return counts, offsets

    def one_unit(unit, lens):
        turn, half = lax.div(unit, 4), lax.rem(unit, 2)
        other = lax.rem(lax.div(unit, 2), 2)
        turn = jnp.where(half == 0, -turn, turn)
        source = 2 * lax.rem(chip + turn + chips, chips) + jnp.where(other == 0, core, 1 - core)
        rows = [(half * HALF + slot) * cycle_size + source for slot in range(HALF)]
        counts, offsets = sort(
            rows, 16, tab.ubase, tab.uspare, tab.uwidth, tab.uitem, unit * HALF
        )
        for item in range(items):
            tab.koff[unit * items + item] = offsets[item] + unit * unit_size
            tab.kcnt[unit * items + item] = counts[item]
        return tuple(length + up(count, 16) for length, count in zip(lens, counts))

    lens = lax.fori_loop(0, units, one_unit, (jnp.int32(0),) * items)
    starts = [jnp.int32(0)]
    for item in range(items):
        size = SPARE_KEYS if item == items - 1 else KEYS
        tab.klen[item] = lens[item]
        tab.kstart[item] = starts[item]
        starts.append(starts[item] + up(lens[item], size))
    tab.kstart[items] = starts[items]

    def place_unit(unit, at):
        for item in range(items):
            tab.kdst[unit * items + item] = at[item]
        return tuple(
            spot + up(tab.kcnt[unit * items + item], 16) for item, spot in enumerate(at)
        )

    lax.fori_loop(0, units, place_unit, tuple(starts[:items]))
    for index in range(SLOTS + 2 * REACH):
        row = SLOTS * me - REACH + index
        width, above, below = 0, 0, 0
        for begin, end, item_width in facts:
            inside = (row >= begin) & (row < end)
            width = jnp.where(inside, item_width, width)
            above = jnp.where(inside & (row > begin), 1, above)
            below = jnp.where(inside & (row + 1 < end), 1, below)
        tab.wwidth[index] = width
        tab.wup[index] = above
        tab.wdown[index] = below
    rows = [slot * cycle_size + me for slot in range(SLOTS)]
    counts, offsets = sort(rows, QROWS, tab.qbase, tab.qspare, tab.qwidth, tab.qitem, 0)
    for item in range(items):
        tab.qfirst[item] = lax.div(offsets[item], QROWS)
        tab.qcount[item] = lax.div(counts[item] + (QROWS - 1), QROWS)


def geometry(lengths, cycle_pos, cycle_size, unit_size):
    items = lengths.shape[0] + 1
    units = 2 * cycle_size
    sizes = [units * items] * 3 + [items + 1] + [items] * 3 + [units * HALF] * 4 + [SLOTS] * 4
    sizes += [SLOTS + 2 * REACH] * 3
    smem = pl.BlockSpec(memory_space=pltpu.SMEM)
    return Tables(
        *pl.pallas_call(
            functools.partial(geometry_kernel, cycle_size, unit_size),
            in_specs=[smem, smem],
            out_specs=[smem] * TABLES,
            out_shape=[jax.ShapeDtypeStruct((size,), jnp.int32) for size in sizes],
            name="geometry",
        )(lengths, cycle_pos.reshape(1))
    )


def places(base, spare, width, first, slots):
    token = lax.broadcasted_iota(jnp.int32, (1, slots * ROWW), 1)
    place = jnp.zeros_like(token)
    for slot in range(slots):
        column = token - slot * ROWW
        here = jnp.where(column < width[first + slot], base[first + slot], spare[first + slot])
        place = jnp.where((column >= 0) & (column < ROWW), here + column, place)
    return place


def sorter(place, rows):
    spot = lax.broadcasted_iota(jnp.int32, (rows, place.shape[1]), 0)
    return jnp.where(spot == place, 1.0, 0.0).astype(BF16)


def query_sorter(tab, rows):
    return sorter(places(tab.qbase, tab.qspare, tab.qwidth, 0, SLOTS), rows)


def with_dataset(values, width, item, first, ids, table_ref):
    column = lax.broadcasted_iota(jnp.int32, (ROWW, 1), 0)
    parts = []
    for slot in range(values.shape[0] // ROWW):
        number = jnp.minimum(item[first + slot], ids.shape[0] - 1)
        added = table_ref[pl.ds(ids[number], 1), :]
        real = column < width[first + slot]
        parts.append(values[slot * ROWW : (slot + 1) * ROWW] + jnp.where(real, added, 0.0))
    return jnp.concatenate(parts, axis=0)


def layer_norm(hidden, norm_gain, norm_bias):
    centred = hidden - jnp.mean(hidden, axis=-1, keepdims=True)
    variance = jnp.mean(centred * centred, axis=-1, keepdims=True)
    return centred * lax.rsqrt(variance + EPS) * norm_gain + norm_bias


def sort_step_kernel(step, ubase, uspare, uwidth, uitem, ids, *refs):
    mine_ref, other_ref, table_ref, gain_ref, bias_ref, out_ref = refs
    unit_size = out_ref.shape[0] // 4
    count = HALF * ROWW
    for unit in range(4):
        source = (mine_ref, other_ref)[unit // 2]
        first = (4 * step + unit) * HALF
        values = source[unit % 2 * count : (unit % 2 + 1) * count, :].astype(F32)
        values = with_dataset(values, uwidth, uitem, first, ids, table_ref)
        normed = layer_norm(values, gain_ref[...], bias_ref[...]).astype(BF16)
        matrix = sorter(places(ubase, uspare, uwidth, first, HALF), unit_size)
        out_ref[unit * unit_size : (unit + 1) * unit_size, :] = jnp.dot(
            matrix, normed, preferred_element_type=F32
        ).astype(BF16)


def sort_step(step, tab, ids, mine, other, table, gain, bias, unit_size):
    return pl.pallas_call(
        functools.partial(sort_step_kernel, step),
        grid_spec=pltpu.PrefetchScalarGridSpec(
            num_scalar_prefetch=5,
            in_specs=[pl.BlockSpec(memory_space=pltpu.VMEM)] * 5,
            out_specs=pl.BlockSpec(memory_space=pltpu.VMEM),
        ),
        out_shape=jax.ShapeDtypeStruct((4 * unit_size, mine.shape[1]), BF16),
        cost_estimate=cost(3),
        compiler_params=pltpu.CompilerParams(vmem_limit_bytes=VMEM),
        name="sort_step",
    )(tab.ubase, tab.uspare, tab.uwidth, tab.uitem, ids, mine, other, table, gain, bias)


def own_start_kernel(qbase, qspare, qwidth, qitem, ids, *refs):
    tokens_ref, table_ref, gain_ref, bias_ref, weight_ref, start_ref, normed_ref, query_ref = refs
    values = tokens_ref[...].astype(F32)
    values = with_dataset(values, qwidth, qitem, 0, ids, table_ref)
    start_ref[...] = values
    normed = layer_norm(values, gain_ref[...], bias_ref[...]).astype(BF16)
    normed_ref[...] = normed
    matrix = sorter(places(qbase, qspare, qwidth, 0, SLOTS), query_ref.shape[0])
    sorted_norm = jnp.dot(matrix, normed, preferred_element_type=F32).astype(BF16)
    query = jnp.dot(sorted_norm, weight_ref[...], preferred_element_type=F32)
    query_ref[...] = (query * (1.0 / math.sqrt(HEAD))).astype(BF16)


def own_start(tab, ids, tokens, table, gain, bias, weight, query_rows):
    vmem = pl.BlockSpec(memory_space=pltpu.VMEM)
    return pl.pallas_call(
        own_start_kernel,
        grid_spec=pltpu.PrefetchScalarGridSpec(
            num_scalar_prefetch=5, in_specs=[vmem] * 5, out_specs=[vmem] * 3
        ),
        out_shape=[
            jax.ShapeDtypeStruct(tokens.shape, F32),
            jax.ShapeDtypeStruct(tokens.shape, BF16),
            jax.ShapeDtypeStruct((query_rows, tokens.shape[1]), BF16),
        ],
        cost_estimate=cost(5),
        compiler_params=pltpu.CompilerParams(vmem_limit_bytes=VMEM),
        name="own_start",
    )(tab.qbase, tab.qspare, tab.qwidth, tab.qitem, ids, tokens, table, gain, bias, weight)


def query_blocks(first, many, body):
    def pair(number, none):
        body(first + 2 * number, 2)
        return none

    lax.fori_loop(0, many // 2, pair, 0)

    @pl.when(many % 2 == 1)
    def _():
        body(first + many - 1, 1)


def for_items(items, klen, body):
    def one(item, none):
        body(item, KEYS, (klen[item] + KEYS - 1) // KEYS)
        return none

    lax.fori_loop(0, items - 1, one, 0)
    last = items - 1
    body(last, SPARE_KEYS, (klen[last] + SPARE_KEYS - 1) // SPARE_KEYS)


def as_column(row):
    return row.T[:, :1]


def attend_kernel(heads, units, items, *refs):
    tab, refs = Tables(*refs[:TABLES]), refs[TABLES:]
    koff, kcnt, kdst, kstart, klen, qfirst, qcount = tab[:7]
    steps = units // 4
    q_ref, wk_ref, wv_ref = refs[:3]
    n_refs, refs = refs[3 : 3 + steps], refs[3 + steps :]
    att_ref, o_ref, lse_ref, ns_ref, bias_ref, ks_ref, vs_ref = refs[:7]
    acc_ref, top_ref, total_ref, matrix = refs[7:]
    stride = n_refs[0].shape[0]
    cols = heads * QROWS
    width = ns_ref.shape[1]
    o_ref[...] = jnp.zeros_like(o_ref)
    lse_ref[...] = jnp.zeros_like(lse_ref)
    used = kstart[items]

    @pl.when(pl.program_id(0) == 0)
    def _():
        matrix[...] = query_sorter(tab, o_ref.shape[0])

        def one_item(item, size, blocks):
            def one_unit(turn, unit, none):
                entry = (4 * turn + unit) * items + item
                count, source, target = kcnt[entry], koff[entry] - turn * stride, kdst[entry]

                def step(part, none):
                    src = pl.ds(pl.multiple_of(source + 64 * part, 16), 64)
                    dst = pl.ds(pl.multiple_of(target + 64 * part, 16), 64)
                    ns_ref[dst, :] = n_refs[turn][src, :]
                    row = lax.broadcasted_iota(jnp.int32, (64, 128), 0) + 64 * part
                    bias_ref[dst, :] = jnp.where(row < count, 0.0, NEG).astype(BF16)
                    return none

                return lax.fori_loop(0, (count + 63) // 64, step, none)

            for turn in range(steps):
                lax.fori_loop(0, 4, functools.partial(one_unit, turn), 0)
            end = kstart[item] + klen[item]

            def clear(part, none):
                tail = pl.ds(pl.multiple_of(end + 64 * part, 16), 64)
                ns_ref[tail, :] = jnp.zeros((64, width), BF16)
                bias_ref[tail, :] = jnp.full((64, 128), NEG, BF16)
                return none

            lax.fori_loop(0, (kstart[item + 1] - end + 63) // 64 + 1, clear, 0)

        for_items(items, klen, one_item)

        def clear(part, none):
            tail = pl.ds(pl.multiple_of(used + 64 * part, 16), 64)
            ns_ref[tail, :] = jnp.zeros((64, width), BF16)
            return none

        lax.fori_loop(0, (ns_ref.shape[0] - used) // 64, clear, 0)

    def project(block, none):
        here = pl.ds(pl.multiple_of(block * ROWS, ROWS), ROWS)
        rows = ns_ref[here, :]
        ks_ref[here, :] = jnp.dot(rows, wk_ref[...], preferred_element_type=F32).astype(BF16)
        vs_ref[here, :] = jnp.dot(rows, wv_ref[...], preferred_element_type=F32).astype(BF16)
        return none

    lax.fori_loop(0, (used + ROWS - 1) // ROWS, project, 0)

    def one_item(item, size, blocks):
        def some_queries(place, count):
            wide = count * cols
            rows = pl.ds(pl.multiple_of(place * QROWS, QROWS), count * QROWS)
            block = q_ref[rows, :]
            queries = jnp.concatenate(
                [spread(block[n * QROWS : (n + 1) * QROWS], heads) for n in range(count)], axis=0
            )
            top, total, acc = top_ref.at[:, :wide], total_ref.at[:, :wide], acc_ref.at[:wide]
            top[...] = jnp.full((8, wide), NEG, F32)
            total[...] = jnp.zeros((8, wide), F32)
            acc[...] = jnp.zeros((wide, heads * HEAD), F32)

            def step(number, none):
                here = pl.ds(pl.multiple_of(kstart[item] + number * size, 16), size)
                scores = lax.dot_general(
                    ks_ref[here, :], queries, NT, preferred_element_type=F32
                ) + lanes(bias_ref[here, :].astype(F32), wide)
                best = jnp.max(jnp.max(scores.reshape(size // 8, 8, wide), axis=0), axis=0)
                old = top[...]
                best = jnp.maximum(old, jnp.broadcast_to(best[None], (8, wide)))
                top[...] = best
                shrink = jnp.exp(old - best)
                weights = jnp.exp(scores - best[:1])
                total[...] = total[...] * shrink + jnp.sum(
                    weights.reshape(size // 8, 8, wide), axis=0
                )
                acc[...] = acc[...] * as_column(shrink) + lax.dot_general(
                    weights.astype(BF16),
                    vs_ref[here, :],
                    (((0,), (0,)), ((), ())),
                    preferred_element_type=F32,
                )
                return none

            lax.fori_loop(0, blocks, step, 0)
            summed = jnp.broadcast_to(jnp.sum(total[...], axis=0, keepdims=True), (8, wide))
            lse = top[...] + jnp.log(summed)
            out = acc[...] * as_column(1.0 / summed)
            for n in range(count):
                part = slice(n * cols, (n + 1) * cols)
                lse_ref[pl.ds(place + n, 1), :] = lse[:1, part]
                o_ref[pl.ds(pl.multiple_of((place + n) * QROWS, QROWS), QROWS), :] = gathered(
                    out[part], heads
                )

        query_blocks(qfirst[item], qcount[item], some_queries)

    for_items(items, klen, one_item)
    att_ref[...] = lax.dot_general(
        matrix[...], o_ref[...].astype(BF16), FLIP, preferred_element_type=F32
    ).astype(BF16)


def attend_back_kernel(heads, units, items, unit_size, *refs):
    tab, refs = Tables(*refs[:TABLES]), refs[TABLES:]
    koff, kcnt, kdst, kstart, klen, qfirst, qcount = tab[:7]
    q_ref, grad_ref, o_ref, lse_ref, ks_ref, vs_ref, wk_ref, wv_ref, ns_ref, bias_ref = refs[:10]
    dq_ref, gk_ref, gv_ref, dn_ref = refs[10:14]
    (
        spread_q, spread_do, delta, dq_acc, dk_acc, dv_acc, gk_acc, gv_acc, dn_acc,
        matrix, do_ref, dqs, unit_rows,
    ) = refs[14:]
    feats = heads * HEAD
    cols = heads * QROWS
    flip = FLIP
    dqs[...] = jnp.zeros_like(dqs)
    gk_acc[...] = jnp.zeros_like(gk_acc)
    gv_acc[...] = jnp.zeros_like(gv_acc)
    used = qfirst[items - 1] + qcount[items - 1]

    @pl.when(pl.program_id(0) == 0)
    def _():
        dn_acc[...] = jnp.zeros_like(dn_acc)
        matrix[...] = query_sorter(tab, q_ref.shape[0])

    do_ref[...] = jnp.dot(matrix[...], grad_ref[...], preferred_element_type=F32).astype(BF16)

    def prepare(place, none):
        rows = pl.ds(pl.multiple_of(place * QROWS, QROWS), QROWS)
        grads = do_ref[rows, :]
        spread_q[place] = spread(q_ref[rows, :], heads)
        spread_do[place] = spread(grads, heads)
        product = spread(grads.astype(F32) * o_ref[rows, :], heads)
        delta[place] = lax.dot_general(
            jnp.ones((8, feats), F32), product, NT, precision=HIGH, preferred_element_type=F32
        )
        dq_acc[place] = jnp.zeros((cols, feats), F32)
        return none

    lax.fori_loop(0, used, prepare, 0)

    def one_item(item, size, blocks):
        def one_block(number, none):
            here = pl.ds(pl.multiple_of(kstart[item] + number * size, 16), size)
            dk_acc[:size] = jnp.zeros((size, feats), F32)
            dv_acc[:size] = jnp.zeros((size, feats), F32)

            def some_queries(place, count):
                wide = count * cols
                spot = pl.ds(place, count)
                queries = spread_q[spot].reshape(wide, feats)
                grads = spread_do[spot].reshape(wide, feats)
                row = [lse_ref[pl.ds(place + n, 1), :] for n in range(count)]
                log_total = jnp.concatenate(row, axis=1)
                shift = jnp.concatenate([delta[place + n, :1, :] for n in range(count)], axis=1)
                keys = ks_ref[here, :]
                scores = lax.dot_general(keys, queries, NT, preferred_element_type=F32)
                weights = jnp.exp(scores + lanes(bias_ref[here, :].astype(F32), wide) - log_total)
                slopes = lax.dot_general(vs_ref[here, :], grads, NT, preferred_element_type=F32)
                score_grads = (weights * (slopes - shift)).astype(BF16)
                dv_acc[:size] += jnp.dot(weights.astype(BF16), grads, preferred_element_type=F32)
                dk_acc[:size] += jnp.dot(score_grads, queries, preferred_element_type=F32)
                part = lax.dot_general(score_grads, keys, flip, preferred_element_type=F32)
                dq_acc[spot] += part.reshape(count, cols, feats)

            query_blocks(qfirst[item], qcount[item], some_queries)
            dk = dk_acc[:size].astype(BF16)
            dv = dv_acc[:size].astype(BF16)
            dn_acc[here, :] += (
                lax.dot_general(dk, wk_ref[...], NT, preferred_element_type=F32)
                + lax.dot_general(dv, wv_ref[...], NT, preferred_element_type=F32)
            ).astype(dn_acc.dtype)
            rows = ns_ref[here, :]
            gk_acc[...] += lax.dot_general(rows, dk, flip, preferred_element_type=F32)
            gv_acc[...] += lax.dot_general(rows, dv, flip, preferred_element_type=F32)
            return none

        lax.fori_loop(0, jnp.where(qcount[item] > 0, blocks, 0), one_block, 0)

    for_items(items, klen, one_item)

    def finish(place, none):
        rows = pl.ds(pl.multiple_of(place * QROWS, QROWS), QROWS)
        scale = 1.0 / math.sqrt(HEAD)
        dqs[rows, :] = (gathered(dq_acc[place], heads) * scale).astype(BF16)
        return none

    lax.fori_loop(0, used, finish, 0)
    dq_ref[...] = lax.dot_general(
        matrix[...], dqs[...], flip, preferred_element_type=F32
    ).astype(BF16)
    gk_ref[...] = gk_acc[...].astype(BF16)
    gv_ref[...] = gv_acc[...].astype(BF16)

    @pl.when(pl.program_id(0) == pl.num_programs(0) - 1)
    def _():
        unit_rows[...] = jnp.zeros_like(unit_rows)
        count = HALF * ROWW

        def one_unit(unit, none):
            def one_item(item, none):
                entry = unit * items + item
                source, target = koff[entry] - unit * unit_size, kdst[entry]

                def step(part, none):
                    src = pl.ds(pl.multiple_of(source + 64 * part, 16), 64)
                    dst = pl.ds(pl.multiple_of(target + 64 * part, 16), 64)
                    unit_rows[src, :] = dn_acc[dst, :]
                    return none

                return lax.fori_loop(0, (kcnt[entry] + 63) // 64, step, none)

            lax.fori_loop(0, items, one_item, 0)
            place = places(tab.ubase, tab.uspare, tab.uwidth, unit * HALF, HALF)
            dn_ref[pl.ds(pl.multiple_of(unit * count, 16), count), :] = lax.dot_general(
                sorter(place, unit_size), unit_rows[...], flip, preferred_element_type=F32
            ).astype(BF16)
            return none

        lax.fori_loop(0, units, one_unit, 0)


def gelu_parts(values):
    slope = 0.7978845608028654
    bent = jnp.tanh(slope * (values + 0.044715 * values * values * values))
    return bent, slope * (1.0 + 3.0 * 0.044715 * values * values)


def gelu(values):
    return 0.5 * values * (1.0 + gelu_parts(values)[0])


def gelu_slope(values):
    bent, inner = gelu_parts(values)
    return 0.5 * (1.0 + bent) + 0.5 * values * (1.0 - bent * bent) * inner


def merge_kernel(
    cycle_size, wwidth, wup, wdown,
    win_ref, k11, k12, k21, k22, out_weight, grad_ref, mapped_ref, shares_ref,
    x1, x2, x3, x4, g3, real_ref, up_ref, down_ref, c1, m1, c3, m2g, m1g,
):
    window = SLOTS + 2 * REACH
    column = lax.broadcasted_iota(jnp.int32, (PITCH, 128), 0)
    for row in range(window):
        spots = pl.ds(row * PITCH, PITCH)
        real = jnp.where(column < wwidth[row], 1.0, 0.0)
        real_ref[spots, :] = real
        up_ref[spots, :] = real * wup[row].astype(F32)
        down_ref[spots, :] = real * wdown[row].astype(F32)

    def at(low, high):
        return slice(low * PITCH, high * PITCH)

    def masked(ref, values, low, high):
        return values * lanes(ref[at(low, high), :], CH)

    def fill(taps, values, low, high):
        spots = at(low + 1, high + 1)
        size = values.shape[0]
        taps[spots, :CH] = pltpu.roll(values, 1, 0).astype(BF16)
        taps[spots, CH : 2 * CH] = values.astype(BF16)
        taps[spots, 2 * CH :] = pltpu.roll(values, size - 1, 0).astype(BF16)

    def conv(taps, kernel, low, high):
        def part(row_step):
            rows = taps[at(low + 1 + row_step, high + 1 + row_step), :]
            first = (row_step + 1) * 3 * CH
            return jnp.dot(rows, kernel[first : first + 3 * CH, :], preferred_element_type=F32)

        total = masked(real_ref, part(0), low, high)
        total = total + masked(up_ref, part(-1), low, high)
        return total + masked(down_ref, part(1), low, high)

    def conv_back(kernel, low, high):
        def part(row_step):
            rows = at(low + 1 + row_step, high + 1 + row_step)
            total = None
            for col_step in (-1, 0, 1):
                first = (8 - (3 * (row_step + 1) + col_step + 1)) * CH
                side = (col_step + 1) * CH
                now = lax.dot_general(
                    g3[rows, side : side + CH],
                    kernel[first : first + CH, :],
                    NT,
                    preferred_element_type=F32,
                )
                total = now if total is None else total + now
            return total

        total = masked(real_ref, part(0), low, high)
        total = total + masked(up_ref, part(-1), low, high)
        return total + masked(down_ref, part(1), low, high)

    own, last = REACH, REACH + SLOTS
    unit_share = 9 * CH // cycle_size
    out_share = CH // cycle_size
    share_rows = 4 * unit_share + out_share

    def weight_grad(taps, gradient, tensor):
        piece = math.gcd(3 * CH, unit_share)
        for row_step, mask in ((-1, up_ref), (0, real_ref), (1, down_ref)):
            now = masked(mask, gradient, own, last).astype(BF16)
            rows = taps[at(own + 1 + row_step, last + 1 + row_step), :]
            block = lax.dot_general(rows, now, FLIP, preferred_element_type=F32).astype(BF16)
            for part in range(3 * CH // piece):
                spot = (row_step + 1) * 3 * CH + part * piece
                share, offset = divmod(spot, unit_share)
                first = share * share_rows + tensor * unit_share + offset
                shares_ref[first : first + piece, :] = block[part * piece : (part + 1) * piece]

    def start(low, high):
        return win_ref[at(low, high), :CH].astype(F32)

    fill(x1, masked(real_ref, gelu(start(0, 24)), 0, 24), 0, 24)
    c1[at(1, 23), :] = conv(x1, k11, 1, 23)
    fill(x2, masked(real_ref, gelu(c1[at(1, 23), :]), 1, 23), 1, 23)
    m1[at(2, 22), :] = start(2, 22) + conv(x2, k12, 2, 22)
    fill(x3, masked(real_ref, gelu(m1[at(2, 22), :]), 2, 22), 2, 22)
    c3[at(3, 21), :] = conv(x3, k21, 3, 21)
    fill(x4, masked(real_ref, gelu(c3[at(3, 21), :]), 3, 21), 3, 21)
    merged = (m1[at(own, last), :] + conv(x4, k22, own, last)).astype(BF16)
    mapped_ref[...] = jnp.dot(merged, out_weight[...], preferred_element_type=F32).astype(BF16)
    block = lax.dot_general(
        merged, win_ref[at(own, last), CH:], FLIP, preferred_element_type=F32
    ).astype(BF16)
    for share in range(cycle_size):
        first = share * share_rows + 4 * unit_share
        shares_ref[first : first + out_share, :] = block[share * out_share : (share + 1) * out_share]

    m2g[at(2, 22), :] = lax.dot_general(
        win_ref[at(2, 22), CH:], out_weight[...], NT, preferred_element_type=F32
    )
    fill(g3, masked(real_ref, m2g[at(2, 22), :], 2, 22), 2, 22)
    weight_grad(x4, m2g[at(own, last), :], 3)
    now = gelu_slope(c3[at(3, 21), :]) * conv_back(k22, 3, 21)
    fill(g3, now, 3, 21)
    weight_grad(x3, now[at(own - 3, last - 3)], 2)
    m1g[at(4, 20), :] = m2g[at(4, 20), :] + gelu_slope(m1[at(4, 20), :]) * conv_back(k21, 4, 20)
    fill(g3, masked(real_ref, m1g[at(4, 20), :], 4, 20), 4, 20)
    weight_grad(x2, m1g[at(own, last), :], 1)
    now = gelu_slope(c1[at(5, 19), :]) * conv_back(k12, 5, 19)
    fill(g3, now, 5, 19)
    weight_grad(x1, now[at(own - 5, last - 5)], 0)
    now = gelu_slope(start(own, last)) * conv_back(k11, own, last)
    grad_ref[...] = (m1g[at(own, last), :] + now).astype(BF16)


def merge(tab, windows, kernels, out_weight, cycle_size):
    window = SLOTS + 2 * REACH
    vmem = pl.BlockSpec(memory_space=pltpu.VMEM)
    padded = (window + 2) * PITCH
    share_rows = 4 * (9 * CH // cycle_size) + CH // cycle_size
    small = pltpu.VMEM((window * PITCH, 128), F32)
    large = pltpu.VMEM((window * PITCH, CH), F32)
    return pl.pallas_call(
        functools.partial(merge_kernel, cycle_size),
        grid_spec=pltpu.PrefetchScalarGridSpec(
            num_scalar_prefetch=3,
            in_specs=[vmem] * 6,
            out_specs=[vmem] * 3,
            scratch_shapes=[pltpu.VMEM((padded, 3 * CH), BF16)] * 5 + [small] * 3 + [large] * 5,
        ),
        out_shape=[
            jax.ShapeDtypeStruct((SLOTS * PITCH, CH), BF16),
            jax.ShapeDtypeStruct((SLOTS * PITCH, CH), BF16),
            jax.ShapeDtypeStruct((cycle_size * share_rows, CH), BF16),
        ],
        cost_estimate=cost(25),
        compiler_params=pltpu.CompilerParams(vmem_limit_bytes=VMEM),
        name="merge",
    )(tab.wwidth, tab.wup, tab.wdown, windows, *kernels, out_weight)


def attend(tab, query, key_weight, value_weight, norms, sorted_keys, units, items, heads):
    feats = heads * HEAD
    cols = heads * QROWS
    width = query.shape[1]
    groups = width // feats
    blocks8 = (query.shape[0] // QROWS + 7) // 8 * 8
    once = pl.Buffered(1) if units > 16 else None

    def part(rows, columns=feats):
        return pl.BlockSpec((rows, columns), lambda group, *_: (0, group), pipeline_mode=once)

    def whole(rows, columns):
        return pl.BlockSpec(
            (rows, columns), lambda group, *_: (0, 0), pipeline_mode=pl.Buffered(1)
        )

    return pl.pallas_call(
        functools.partial(attend_kernel, heads, units, items),
        grid_spec=pltpu.PrefetchScalarGridSpec(
            num_scalar_prefetch=TABLES,
            grid=(groups,),
            in_specs=[part(query.shape[0]), part(width), part(width)]
            + [whole(*norm.shape) for norm in norms],
            out_specs=[
                part(SLOTS * ROWW),
                part(query.shape[0]),
                part(blocks8, cols),
                whole(sorted_keys, width),
                whole(sorted_keys, 128),
                part(sorted_keys),
                part(sorted_keys),
            ],
            scratch_shapes=[
                pltpu.VMEM((2 * cols, feats), F32),
                pltpu.VMEM((8, 2 * cols), F32),
                pltpu.VMEM((8, 2 * cols), F32),
                pltpu.VMEM((query.shape[0], SLOTS * ROWW), BF16),
            ],
        ),
        out_shape=[
            jax.ShapeDtypeStruct((SLOTS * ROWW, width), BF16),
            jax.ShapeDtypeStruct(query.shape, F32),
            jax.ShapeDtypeStruct((blocks8, groups * cols), F32),
            jax.ShapeDtypeStruct((sorted_keys, width), BF16),
            jax.ShapeDtypeStruct((sorted_keys, 128), BF16),
            jax.ShapeDtypeStruct((sorted_keys, width), BF16),
            jax.ShapeDtypeStruct((sorted_keys, width), BF16),
        ],
        cost_estimate=cost(70),
        compiler_params=pltpu.CompilerParams(vmem_limit_bytes=VMEM),
        name="attend",
    )(*tab, query, key_weight, value_weight, *norms)


def attend_back(
    tab, query, grads, outputs, lse, ks, vs, key_weight, value_weight, ns, bias,
    unit_size, units, items, heads,
):
    feats = heads * HEAD
    cols = heads * QROWS
    rows, width = query.shape
    groups = width // feats
    blocks = rows // QROWS
    once = pl.Buffered(1) if units > 16 else None

    def part(rows, columns=feats):
        return pl.BlockSpec((rows, columns), lambda group, *_: (0, group), pipeline_mode=once)

    def whole(rows, columns):
        return pl.BlockSpec(
            (rows, columns), lambda group, *_: (0, 0), pipeline_mode=pl.Buffered(1)
        )

    return pl.pallas_call(
        functools.partial(attend_back_kernel, heads, units, items, unit_size),
        grid_spec=pltpu.PrefetchScalarGridSpec(
            num_scalar_prefetch=TABLES,
            grid=(groups,),
            in_specs=[
                part(rows),
                part(grads.shape[0]),
                part(rows),
                part(lse.shape[0], cols),
                part(ks.shape[0]),
                part(ks.shape[0]),
                part(width),
                part(width),
                whole(*ns.shape),
                whole(*bias.shape),
            ],
            out_specs=[
                part(grads.shape[0]),
                part(width),
                part(width),
                whole(units * HALF * ROWW, width),
            ],
            scratch_shapes=[
                pltpu.VMEM((blocks, cols, feats), BF16),
                pltpu.VMEM((blocks, cols, feats), BF16),
                pltpu.VMEM((blocks, 8, cols), F32),
                pltpu.VMEM((blocks, cols, feats), F32),
                pltpu.VMEM((SPARE_KEYS, feats), F32),
                pltpu.VMEM((SPARE_KEYS, feats), F32),
                pltpu.VMEM((width, feats), F32),
                pltpu.VMEM((width, feats), F32),
                pltpu.VMEM(ns.shape, BF16),
                pltpu.VMEM((rows, grads.shape[0]), BF16),
                pltpu.VMEM((rows, feats), BF16),
                pltpu.VMEM((rows, feats), BF16),
                pltpu.VMEM((unit_size, width), BF16),
            ],
        ),
        out_shape=[
            jax.ShapeDtypeStruct(grads.shape, BF16),
            jax.ShapeDtypeStruct((width, width), BF16),
            jax.ShapeDtypeStruct((width, width), BF16),
            jax.ShapeDtypeStruct((units * HALF * ROWW, width), BF16),
        ],
        cost_estimate=cost(90),
        compiler_params=pltpu.CompilerParams(vmem_limit_bytes=VMEM),
        name="attend_back",
    )(*tab, query, grads, outputs, lse, ks, vs, key_weight, value_weight, ns, bias)


@functools.cache
def most_rows(cycle_size, item_count):
    rows = np.arange(SLOTS)[:, None] * cycle_size + np.arange(cycle_size)
    most_keys = most_unit = most_queries = 0
    lists = [()]
    while lists:
        heights = lists.pop()
        if len(heights) < item_count:
            for height in (24, 30):
                if sum(heights) + height <= SLOTS * cycle_size:
                    lists.append(heights + (height,))
        if not heights:
            continue
        ends = np.cumsum(heights)
        number = np.searchsorted(ends, rows, side="right")
        wide = np.array([24 if height == 24 else ROWW for height in heights] + [0])[number]
        kinds = np.arange(len(heights))
        counts = [((number == kind) * wide) for kind in kinds] + [ROWW - wide]
        counts = np.stack(counts)

        def rounded(values, align):
            return -(-values // align) * align

        units = rounded(counts.reshape(len(counts), 2, HALF, cycle_size).sum(2), 16)
        most_unit = max(most_unit, units.sum(0).max())
        keys = units.sum((1, 2))
        keys = rounded(keys[:-1], KEYS).sum() + rounded(keys[-1], SPARE_KEYS)
        most_keys = max(most_keys, keys)
        most_queries = max(most_queries, rounded(counts.sum(1), QROWS).sum(0).max())
    return int(most_keys), int(most_unit), int(most_queries)


def passed(value, axis, target):
    pairs = [(source, target(source)) for source in range(lax.axis_size(axis))]
    return lax.ppermute(value, axis, pairs)


def passed_along(value, axis, steps):
    count = lax.axis_size(axis)
    return passed(value, axis, lambda source: (source + steps) % count)


def tied(*values):
    return lax.optimization_barrier(values)


def to_sibling(value):
    return passed(value, "blk", lambda source: source ^ 1)


def gelu_tanh(values):
    return (
        0.5
        * values
        * (1.0 + jnp.tanh(0.7978845608028654 * (values + 0.044715 * values * values * values)))
    )


def gelu_back(values, gradient):
    return jax.vjp(gelu_tanh, values)[1](gradient)[0]


def item_facts(lengths):
    facts, start = [], 0
    for item in range(lengths.shape[0]):
        length = lengths[item]
        height = jnp.where(length == 1200, 30, jnp.where(length == 576, 24, 0))
        width = jnp.where(length == 1200, 40, 24)
        facts.append((start, start + height, height, width))
        start = start + height
    return facts


def row_facts(facts, rows):
    number = jnp.full_like(rows, len(facts))
    local, height, width = rows, jnp.zeros_like(rows), jnp.zeros_like(rows)
    for item, (start, end, item_height, item_width) in enumerate(facts):
        inside = (rows >= start) & (rows < end)
        number = jnp.where(inside, item, number)
        local = jnp.where(inside, rows - start, local)
        height = jnp.where(inside, item_height, height)
        width = jnp.where(inside, item_width, width)
    return number, local, height, width


def tap_masks(local_row, height, width):
    column = lax.broadcasted_iota(jnp.int32, (1, ROWW), 1)
    is_real = column < width
    all_masks = []
    for row_step in (-1, 0, 1):
        rows_fine = (local_row + row_step >= 0) & (local_row + row_step < height)
        for col_step in (-1, 0, 1):
            cols_fine = (column + col_step >= 0) & (column + col_step < width)
            all_masks.append(is_real & rows_fine & cols_fine)
    return is_real, all_masks


def side_shift(values, col_step):
    if col_step == 0:
        return values
    empty_col = jnp.zeros_like(values[:, :1])
    if col_step < 0:
        return jnp.concatenate([empty_col, values[:, :-1]], axis=1)
    return jnp.concatenate([values[:, 1:], empty_col], axis=1)


def from_above(values, cycle_pos):
    got = passed_along(values, "blk", 1)
    empty_row = jnp.zeros_like(values[:1])
    return jnp.where(cycle_pos == 0, jnp.concatenate([empty_row, got[:-1]], axis=0), got)


def from_below(values, cycle_pos, cycle_size):
    got = passed_along(values, "blk", -1)
    empty_row = jnp.zeros_like(values[:1])
    return jnp.where(
        cycle_pos == cycle_size - 1, jnp.concatenate([got[1:], empty_row], axis=0), got
    )


def upsample_forward(values, all_masks, cycle_pos, cycle_size):
    center = values.astype(F32)
    row_above = from_above(values, cycle_pos)
    row_below = from_below(values, cycle_pos, cycle_size)
    upper_value = jnp.where(all_masks[1][:, :, None], row_above, values).astype(F32)
    lower_value = jnp.where(all_masks[7][:, :, None], row_below, values).astype(F32)
    pieces = []
    for half_rows in (0.75 * center + 0.25 * upper_value, 0.75 * center + 0.25 * lower_value):
        left_value = jnp.where(all_masks[3][:, :, None], side_shift(half_rows, -1), half_rows)
        right_value = jnp.where(all_masks[5][:, :, None], side_shift(half_rows, 1), half_rows)
        pieces.append(0.75 * half_rows + 0.25 * left_value)
        pieces.append(0.75 * half_rows + 0.25 * right_value)
    joined = jnp.concatenate(pieces, axis=2)
    return joined.reshape(-1, joined.shape[2])


def upsample_back_columns(gradient, all_masks):
    channels = gradient.shape[2] // 4
    left_fine = all_masks[3][:, :, None]
    right_fine = all_masks[5][:, :, None]
    halves = []
    for half in (0, 1):
        left_part = gradient[:, :, 2 * half * channels : (2 * half + 1) * channels].astype(F32)
        right_part = gradient[:, :, (2 * half + 1) * channels : (2 * half + 2) * channels].astype(
            F32
        )
        side = jnp.where(right_fine, side_shift(left_part, 1), 0.0)
        side = side + jnp.where(left_fine, 0.0, left_part)
        side = side + jnp.where(left_fine, side_shift(right_part, -1), 0.0)
        side = side + jnp.where(right_fine, 0.0, right_part)
        halves.append(0.75 * (left_part + right_part) + 0.25 * side)
    return [half.astype(BF16) for half in halves]


def upsample_back_rows(upper, lower, upper_next, lower_prev, all_masks):
    up_fine = all_masks[1][:, :, None]
    down_fine = all_masks[7][:, :, None]
    rows = jnp.where(down_fine, upper_next, lower).astype(F32)
    rows = rows + jnp.where(up_fine, lower_prev, upper).astype(F32)
    return 0.75 * (upper.astype(F32) + lower.astype(F32)) + 0.25 * rows


def first_slot(begin, device, cycle_size):
    return -((device - begin) // cycle_size)


def to_windows(values, cycle_pos, cycle_size):
    window = SLOTS + 2 * REACH
    many = -(-window // cycle_size)
    spare = many + 1
    padded = jnp.pad(values, ((spare, spare), (0, 0), (0, 0)))
    sends = []
    for target in range(cycle_size):
        slot = first_slot(SLOTS * target - REACH, cycle_pos, cycle_size) + spare
        sends.append(lax.dynamic_slice_in_dim(padded, slot, many, axis=0))
    got = lax.all_to_all(jnp.stack(sends), "blk", 0, 0)
    got = jnp.swapaxes(got, 0, 1)
    begin = SLOTS * cycle_pos - REACH
    turn = begin - (begin // cycle_size) * cycle_size
    got = lax.dynamic_slice_in_dim(jnp.concatenate([got, got], axis=1), turn, cycle_size, axis=1)
    return got.reshape((many * cycle_size,) + values.shape[1:])[:window]


def from_windows(values, cycle_pos, cycle_size):
    many = -(-SLOTS // cycle_size)
    padded = jnp.pad(values, ((0, many * cycle_size), (0, 0), (0, 0)))
    begin = SLOTS * cycle_pos
    sends = []
    for target in range(cycle_size):
        slot = first_slot(begin, target, cycle_size)
        for extra in range(many):
            row = (slot + extra) * cycle_size + target - begin
            sends.append(lax.dynamic_slice_in_dim(padded, row, 1, axis=0))
    sends = jnp.concatenate(sends, axis=0).reshape((cycle_size, many) + values.shape[1:])
    got = lax.all_to_all(sends, "blk", 0, 0).reshape((cycle_size * many,) + values.shape[1:])
    rows = []
    for slot in range(SLOTS):
        row = slot * cycle_size + cycle_pos
        source = row // SLOTS
        extra = slot - first_slot(source * SLOTS, cycle_pos, cycle_size)
        rows.append(lax.dynamic_slice_in_dim(got, source * many + extra, 1, axis=0))
    return jnp.concatenate(rows, axis=0)


def dot32(left, right, **more):
    return jnp.dot(left, right, preferred_element_type=F32, **more)


def dot_t(left, right):
    return lax.dot_general(left, right, NT, preferred_element_type=F32)


def t_dot(left, right):
    return lax.dot_general(left, right, (((0,), (0,)), ((), ())), preferred_element_type=F32)


def halved(values, device, bit, axis, pairs_axis):
    half = values.shape[axis] // 2
    mine = (device >> bit) & 1
    keep = lax.dynamic_slice_in_dim(values, mine * half, half, axis=axis)
    send = lax.dynamic_slice_in_dim(values, (1 - mine) * half, half, axis=axis)
    got = passed(send, pairs_axis, lambda source: source ^ (1 << bit))
    return (keep.astype(F32) + got.astype(F32)).astype(BF16)


def core_summed(shares, core):
    cycle_size, rows, width = shares.shape
    paired = shares.reshape(cycle_size // 2, 2, rows, width)
    keep = lax.dynamic_index_in_dim(paired, core, 1, keepdims=False)
    send = lax.dynamic_index_in_dim(paired, 1 - core, 1, keepdims=False)
    return (keep.astype(F32) + to_sibling(send).astype(F32)).astype(BF16)


def added_over_chips(values, chip):
    chips, rows, _ = values.shape
    half = rows // 2
    both = []
    for part, way in ((values[:, :half], 1), (values[:, half:], -1)):

        def block(offset, part=part, way=way):
            return lax.dynamic_index_in_dim(
                part, (chip - way * offset) % chips, 0, keepdims=False
            ).astype(F32)

        moving = block(1)
        for step in range(2, chips + 1):
            moving = passed_along(moving.astype(BF16), "blk", 2 * way).astype(F32) + block(step)
        both.append(moving.astype(BF16))
    return jnp.concatenate(both, axis=0)


def gathered_over_groups(values, dp_pos):
    groups = lax.axis_size("dp")
    bits = groups.bit_length() - 1
    half = values.shape[0] // 2
    both = []
    for part, order in ((values[:half], range(bits)), (values[half:], range(bits - 1, -1, -1))):
        held = part[(None,) * bits]
        for bit in order:
            axis = bits - 1 - bit
            got = passed(held, "dp", lambda source, bit=bit: source ^ (1 << bit))
            mine = (dp_pos >> bit) & 1
            held = jnp.where(
                mine == 0,
                jnp.concatenate([held, got], axis=axis),
                jnp.concatenate([got, held], axis=axis),
            )
        both.append(held.reshape((groups,) + part.shape))
    return jnp.concatenate(both, axis=1)


def small_sums(values, core, chip, dp_pos):
    values = core_summed(values, core)
    for bit in range(lax.axis_size("dp").bit_length() - 1):
        got = passed(values, "dp", lambda source, bit=bit: source ^ (1 << bit))
        values = (values.astype(F32) + got.astype(F32)).astype(BF16)
    chips = values.shape[0]
    total = lax.dynamic_index_in_dim(values, chip, 0, keepdims=False).astype(F32)
    for step in range(1, chips):
        send = lax.dynamic_index_in_dim(values, (chip + step) % chips, 0, keepdims=False)
        total = total + passed_along(send, "blk", 2 * step).astype(F32)
    return total


def finished(late, orders, chip, dp_pos):
    groups = lax.axis_size("dp")
    bits = groups.bit_length() - 1
    chips = late[0].shape[0]
    joined = jnp.concatenate([part.reshape(chips, -1, 256) for part in late], axis=1)
    whole = gathered_over_groups(added_over_chips(joined, chip), dp_pos)
    out, place = [], 0
    for part, order in zip(late, orders):
        rows, width = part.shape[1:]
        size = rows * width // 256
        pieces = []
        for turn in range(groups):
            device = sum(((turn >> (bits - 1 - index)) & 1) << bit for index, bit in enumerate(order))
            pieces.append(whole[device, place : place + size].reshape(rows, width))
        out.append(jnp.concatenate(pieces, axis=0).astype(F32))
        place += size
    return out


def shards(
    tokens,
    item_lengths,
    dataset_ids,
    dataset_table,
    norm1_gain,
    norm1_bias,
    query_weight,
    key_weight,
    value_weight,
    out_weight,
    norm2_gain,
    norm2_bias,
    fc1_weight,
    fc2_weight,
    project_weight,
    unit1_first,
    unit1_second,
    unit2_first,
    unit2_second,
    output_weight,
    block_cotangent,
    merged_cotangent,
):
    cycle_size = lax.axis_size("blk")
    cycle_pos = lax.axis_index("blk")
    chips = cycle_size // 2
    chip, core = cycle_pos // 2, cycle_pos % 2
    lengths = item_lengths[0]
    item_count = lengths.shape[0]
    kinds = item_count + 1
    width_model = tokens.shape[1]
    heads = 4 if cycle_size <= 8 else 2
    half_tokens = HALF * ROWW
    token_count = tokens.shape[0]

    facts = item_facts(lengths)
    own_rows = lax.broadcasted_iota(jnp.int32, (SLOTS, 1), 0) * cycle_size + cycle_pos
    number, local_row, height, width = row_facts(facts, own_rows)
    is_real, all_masks = tap_masks(local_row, height, width)
    units = 4 * chips
    most_keys, most_unit, query_rows = most_rows(cycle_size, item_count)
    unit_size = most_unit + 48
    sorted_keys = (most_keys + 128 + ROWS - 1) // ROWS * ROWS
    tab = geometry(lengths, cycle_pos, cycle_size, unit_size)
    ids = dataset_ids[0]
    gain_one, bias_one = norm1_gain.reshape(1, -1), norm1_bias.reshape(1, -1)

    stream_start, normed_one, query = own_start(
        tab, ids, tokens, dataset_table, gain_one, bias_one, query_weight, query_rows
    )
    ahead, behind = tokens[:half_tokens], tokens[half_tokens:]
    sorted_norms = []
    for step in range(chips):
        if step:
            ahead = passed_along(ahead, "blk", 2)
            behind = passed_along(behind, "blk", -2)
            ahead, behind, sorted_norms[-1] = tied(ahead, behind, sorted_norms[-1])
        if step == 1:
            ahead, behind, merged_cotangent, stream_start, normed_one, query = tied(
                ahead, behind, merged_cotangent, stream_start, normed_one, query
            )
        mine = jnp.concatenate([ahead, behind], axis=0)
        sorted_norms.append(
            sort_step(
                step, tab, ids, mine, to_sibling(mine), dataset_table, gain_one, bias_one, unit_size
            )
        )
    upper, lower = upsample_back_columns(
        merged_cotangent.reshape(SLOTS, ROWW, -1), all_masks
    )
    sorted_norms[-1], upper, lower = tied(sorted_norms[-1], upper, lower)
    upper_next = from_below(upper, cycle_pos, cycle_size)
    lower_prev = from_above(lower, cycle_pos)
    attended, outputs, lse, sorted_norm, bias, ks, vs = attend(
        tab, query, key_weight, value_weight, sorted_norms, sorted_keys, units, kinds, heads
    )

    attended, upper_next, lower_prev = tied(attended, upper_next, lower_prev)

    def as_cells(flattened):
        return flattened.reshape(SLOTS, ROWW, flattened.shape[-1])

    after_attn = stream_start + dot32(attended, out_weight)
    normed_two = layer_norm(after_attn, norm2_gain, norm2_bias).astype(BF16)
    pre_act = dot32(normed_two, fc1_weight)
    hidden = gelu_tanh(pre_act).astype(BF16)
    block_out = (after_attn + dot32(hidden, fc2_weight)).astype(BF16)
    reassembled_own = dot32(block_out, project_weight).astype(BF16)

    mapped_grad_own = upsample_back_rows(
        upper, lower, upper_next, lower_prev, all_masks
    ).astype(BF16)
    channels = mapped_grad_own.shape[-1]
    arrived = to_windows(
        jnp.concatenate([as_cells(reassembled_own), mapped_grad_own], axis=2), cycle_pos, cycle_size
    )
    windows = jnp.pad(arrived, ((0, 0), (0, PITCH - ROWW), (0, 0))).reshape(-1, 2 * channels)
    reassembled_grad, mapped, conv_shares = merge(
        tab, windows, (unit1_first, unit1_second, unit2_first, unit2_second), output_weight, cycle_size
    )
    conv_shares = conv_shares.reshape(cycle_size, -1, channels)

    def own_window(values):
        return values.reshape(SLOTS, PITCH, channels)[:, :ROWW]

    def shared_out(*gradients):
        parts = []
        for gradient in gradients:
            parts.append(gradient.astype(BF16).reshape(cycle_size, -1, gradient.shape[-1]))
        return jnp.concatenate(parts, axis=1) if len(parts) > 1 else parts[0]

    dp_pos = lax.axis_index("dp")
    groups = lax.axis_size("dp")
    bits = groups.bit_length() - 1
    one_way = list(range(bits))
    other_way = one_way[::-1]

    def wide(gradient):
        return gradient.reshape(cycle_size, -1, width_model)

    def scattered(shares):
        count, share_rows, share_width = shares.shape
        parts = shares.reshape(count, groups, share_rows // groups, share_width)
        parts = jnp.swapaxes(parts, 0, 1).reshape(-1, share_width)
        part = lax.psum_scatter(parts, "dp", scatter_dimension=0, tiled=True)
        return part.reshape(count, -1, 256)

    def dp_halved(values, order, index):
        return halved(values, dp_pos, order[index], 1, "dp")

    returned = from_windows(
        jnp.concatenate([own_window(reassembled_grad), own_window(mapped)], axis=2),
        cycle_pos,
        cycle_size,
    )
    reassembled_grad = returned[:, :, :channels].reshape(-1, channels)
    merged = upsample_forward(returned[:, :, channels:], all_masks, cycle_pos, cycle_size).astype(
        BF16
    )

    project_grad = t_dot(block_out, reassembled_grad)
    block_grad = block_cotangent.astype(F32) + dot_t(reassembled_grad, project_weight)
    mlp_grad = block_grad.astype(BF16)
    fc2_grad = t_dot(hidden, mlp_grad)
    conv_sums = core_summed(conv_shares, core)
    pre_grad = gelu_back(pre_act, dot_t(mlp_grad, fc2_weight)).astype(BF16)
    fc1_grad = t_dot(normed_two, pre_grad)
    normed_two_grad = dot_t(pre_grad, fc1_weight)
    norm_two_pull = jax.vjp(layer_norm, after_attn, norm2_gain, norm2_bias)[1]
    attn_side, norm2_gain_grad, norm2_bias_grad = norm_two_pull(normed_two_grad)
    after_grad = block_grad + attn_side
    branch_grad = after_grad.astype(BF16)
    out_proj_grad = t_dot(attended, branch_grad)
    attended_grad = dot_t(branch_grad, out_weight).astype(BF16)

    rows = width_model // cycle_size
    rows = width_model // cycle_size
    model_sums = scattered(shared_out(fc2_grad, out_proj_grad, wide(project_grad)))
    fc1_sums = scattered(shared_out(fc1_grad))
    early = [model_sums, fc1_sums]
    early_sums = jnp.concatenate(early, axis=1)
    attended_grad, conv_sums = tied(attended_grad, conv_sums)
    conv_sums = dp_halved(conv_sums, one_way, 0)
    query_low, key_grad, value_grad, unit_grad = attend_back(
        tab, query, attended_grad, outputs, lse, ks, vs, key_weight, value_weight, sorted_norm,
        bias, unit_size, units, kinds, heads,
    )
    query_low, key_grad, value_grad, unit_grad, conv_sums = tied(
        query_low, key_grad, value_grad, unit_grad, conv_sums
    )
    query_grad = t_dot(normed_one, query_low)
    key_sums = core_summed(shared_out(key_grad, value_grad), core)
    query_sums = core_summed(shared_out(query_grad), core)

    def unit_part(step):
        part = unit_grad[4 * step * half_tokens : 4 * (step + 1) * half_tokens]
        part = part.reshape(4, half_tokens, width_model)
        return part[:2].astype(F32) + to_sibling(part[2:]).astype(F32)

    ahead = behind = None
    for step in range(chips - 1, -1, -1):
        part = unit_part(step)
        if ahead is None:
            ahead, behind = part[0], part[1]
        else:
            ahead = passed_along(ahead.astype(BF16), "blk", -2).astype(F32) + part[0]
            behind = passed_along(behind.astype(BF16), "blk", 2).astype(F32) + part[1]
            turn = chips - 1 - step
            if turn < bits:
                conv_sums = dp_halved(conv_sums, one_way, turn)
            if turn <= bits:
                key_sums = dp_halved(key_sums, one_way, turn - 1)
                query_sums = dp_halved(query_sums, other_way, turn - 1)
                ahead, behind, key_sums, query_sums, conv_sums = tied(
                    ahead, behind, key_sums, query_sums, conv_sums
                )
                if turn == 1:
                    early_sums = lax.psum_scatter(
                        early_sums.reshape(-1, 256), "blk", scatter_dimension=0, tiled=True
                    )
    normed_one_grad = jnp.concatenate([ahead, behind], axis=0) + dot_t(query_low, query_weight)

    norm_one_pull = jax.vjp(layer_norm, stream_start, norm1_gain, norm1_bias)[1]
    start_side, norm1_gain_grad, norm1_bias_grad = norm_one_pull(normed_one_grad)
    tokens_grad = after_grad + start_side
    table_rows = dataset_table.shape[0]
    dataset = jnp.full_like(number, -1)
    for item in range(item_count):
        dataset = jnp.where(number == item, ids[item], dataset)
    dataset = jnp.where(is_real, dataset, -1).reshape(1, -1)
    onehot = (dataset == lax.broadcasted_iota(jnp.int32, (table_rows, 1), 0)).astype(F32)
    table_grad = jnp.dot(onehot, tokens_grad, precision=HIGH)
    table_split = jnp.swapaxes(table_grad.reshape(table_rows, cycle_size, rows), 0, 1)
    small = [table_split.reshape(cycle_size, -1)] + [
        gradient.reshape(cycle_size, -1)
        for gradient in (norm1_gain_grad, norm1_bias_grad, norm2_gain_grad, norm2_bias_grad)
    ]
    small = jnp.concatenate(small, axis=1).astype(BF16)
    small_rows = -(-small.shape[1] // 1024) * 8
    small = jnp.pad(small, ((0, 0), (0, small_rows * 128 - small.shape[1])))
    small = small_sums(small.reshape(cycle_size, small_rows, 128), core, chip, dp_pos).reshape(-1)
    table_size = table_rows * rows
    norms = [small[table_size + index * rows :][:rows] for index in range(4)]

    unit_share = 9 * channels // cycle_size
    out_share = channels // cycle_size
    fc2_share = fc2_weight.shape[0] // cycle_size
    convs, keys_values, query_share = finished(
        [conv_sums, key_sums, query_sums], [one_way, one_way, other_way], chip, dp_pos
    )
    whole = gathered_over_groups(early_sums, dp_pos)
    shares, spot = [], 0
    for part, columns in zip(early, (width_model, fc1_weight.shape[1])):
        size = part.shape[1]
        shares.append(whole[:, spot : spot + size].reshape(-1, columns).astype(F32))
        spot += size
    models, fc1_share = shares
    return (
        block_out,
        merged,
        tokens_grad,
        small[:table_size].reshape(table_rows, rows),
        norms[0],
        norms[1],
        query_share,
        keys_values[:rows],
        keys_values[rows:],
        models[fc2_share : fc2_share + rows],
        norms[2],
        norms[3],
        fc1_share,
        models[:fc2_share],
        models[fc2_share + rows :].reshape(rows, channels),
        convs[:unit_share],
        convs[unit_share : 2 * unit_share],
        convs[2 * unit_share : 3 * unit_share],
        convs[3 * unit_share : 4 * unit_share],
        convs[4 * unit_share :],
    )


def solution(mesh):
    split = P(("dp", "blk"), None)
    placed = (split, P("dp", None), P("dp", None)) + (P(),) * 17 + (split, split)
    rows, line = P("blk", None), P("blk")
    return jax.shard_map(
        shards,
        mesh=mesh,
        in_specs=placed,
        out_specs=(
            split, split, split, P(None, "blk"), line, line, rows, rows, rows, rows, line, line,
            rows, rows, rows, rows, rows, rows, rows, rows,
        ),
        check_vma=False,
    )
```

```python
import functools
import math
import typing

import jax
import jax.numpy as jnp
from jax import lax
from jax.experimental import pallas as pl
from jax.experimental.pallas import tpu as pltpu
from jax.sharding import PartitionSpec as P
import numpy as np

HEADS = 12
HEAD = 64
ROWW = 40
SLOTS = 12
HALF = SLOTS // 2
REACH = 6
PITCH = 48
CH = 256

NEG = -1e30
EPS = 1e-06
HIGH = lax.Precision.HIGHEST
KEYS = 672
SPARE_KEYS = 768
QROWS = 64
ROWS = 1024
VMEM = 60 * 1024 * 1024
NT = (((1,), (1,)), ((), ()))
FLIP = (((0,), (0,)), ((), ()))
F32 = jnp.float32
BF16 = jnp.bfloat16


def cost(microseconds):
    return pl.CostEstimate(flops=microseconds * 10**9, bytes_accessed=10**6, transcendentals=0)


def own_blocks(heads, feats):
    row = lax.broadcasted_iota(jnp.int32, (heads * QROWS, feats), 0) // QROWS
    col = lax.broadcasted_iota(jnp.int32, (heads * QROWS, feats), 1) // HEAD
    return row == col


def spread(block, heads):
    wide = jnp.concatenate([block] * heads, axis=0)
    return jnp.where(own_blocks(heads, block.shape[1]), wide, jnp.zeros((), block.dtype))


def gathered(wide, heads):
    kept = jnp.where(own_blocks(heads, wide.shape[1]), wide, 0.0)
    total = kept[:QROWS]
    for head in range(1, heads):
        total = total + kept[head * QROWS : (head + 1) * QROWS]
    return total


def lanes(column, width):
    return jnp.concatenate([column] * (width // 128), axis=1)


class Tables(typing.NamedTuple):
    koff: jax.Array
    kcnt: jax.Array
    kdst: jax.Array
    kstart: jax.Array
    klen: jax.Array
    qfirst: jax.Array
    qcount: jax.Array
    ubase: jax.Array
    uspare: jax.Array
    uwidth: jax.Array
    uitem: jax.Array
    qbase: jax.Array
    qspare: jax.Array
    qwidth: jax.Array
    qitem: jax.Array
    wwidth: jax.Array
    wup: jax.Array
    wdown: jax.Array
    wgroup: jax.Array
    wcame: jax.Array
    sent: jax.Array
    back: jax.Array
    came: jax.Array
    around: jax.Array


TABLES = len(Tables._fields)


def pieces(cycle_size):
    return -(-(SLOTS + 2 * REACH) // cycle_size), -(-SLOTS // cycle_size)


def floor_div(value, by):
    return lax.div(value + 16 * by, by) - 16


def first_slot(begin, device, cycle_size):
    return -floor_div(device - begin, cycle_size)


def unit_source(unit, me, chips):
    chip, core = lax.div(me, 2), lax.rem(me, 2)
    turn, half = lax.div(unit, 4), lax.rem(unit, 2)
    other = lax.rem(lax.div(unit, 2), 2)
    turn = jnp.where(half == 0, -turn, turn)
    source = 2 * lax.rem(chip + turn + chips, chips) + jnp.where(other == 0, core, 1 - core)
    return source, half


def geometry_kernel(cycle_size, unit_size, lengths, place, *refs):
    tab = Tables(*refs)
    item_count = lengths.shape[0]
    items = item_count + 1
    chips = cycle_size // 2
    units = 4 * chips
    me = place[0]
    many, few = pieces(cycle_size)
    facts, start = [], 0
    for item in range(item_count):
        length = lengths[item]
        height = jnp.where(length == 1200, 30, jnp.where(length == 576, 24, 0))
        facts.append((start, start + height, jnp.where(length == 1200, 40, 24)))
        start = start + height

    def fact(row):
        number, width = item_count, 0
        for item, (begin, end, item_width) in enumerate(facts):
            inside = (row >= begin) & (row < end)
            number = jnp.where(inside, item, number)
            width = jnp.where(inside, item_width, width)
        return number, width

    def up(value, align):
        return lax.div(value + (align - 1), align) * align

    def sort(rows, align, base, spare_base, widths, numbers, first):
        known = [fact(row) for row in rows]
        counts = [
            sum(jnp.where(number == item, width, 0) for number, width in known)
            for item in range(item_count)
        ]
        counts.append(sum(ROWW - width for _, width in known))
        offsets, total = [], 0
        for count in counts:
            offsets.append(total)
            total = total + up(count, align)
        spare = offsets[-1]
        for slot, (number, width) in enumerate(known):
            begin = sum(jnp.where(number == item, offsets[item], 0) for item in range(item_count))
            for other, other_width in known[:slot]:
                begin = begin + jnp.where(other == number, other_width, 0)
            base[first + slot] = begin
            spare_base[first + slot] = spare - width
            widths[first + slot] = width
            numbers[first + slot] = number
            spare = spare + ROWW - width
        return counts, offsets

    def one_unit(unit, lens):
        source, half = unit_source(unit, me, chips)
        rows = [(half * HALF + slot) * cycle_size + source for slot in range(HALF)]
        counts, offsets = sort(
            rows, 16, tab.ubase, tab.uspare, tab.uwidth, tab.uitem, unit * HALF
        )
        for item in range(items):
            tab.koff[unit * items + item] = offsets[item] + unit * unit_size
            tab.kcnt[unit * items + item] = counts[item]
        return tuple(length + up(count, 16) for length, count in zip(lens, counts))

    lens = lax.fori_loop(0, units, one_unit, (jnp.int32(0),) * items)
    starts = [jnp.int32(0)]
    for item in range(items):
        size = SPARE_KEYS if item == items - 1 else KEYS
        tab.klen[item] = lens[item]
        tab.kstart[item] = starts[item]
        starts.append(starts[item] + up(lens[item], size))
    tab.kstart[items] = starts[items]

    def place_unit(unit, at):
        for item in range(items):
            tab.kdst[unit * items + item] = at[item]
        return tuple(
            spot + up(tab.kcnt[unit * items + item], 16) for item, spot in enumerate(at)
        )

    lax.fori_loop(0, units, place_unit, tuple(starts[:items]))
    for index in range(SLOTS + 2 * REACH):
        row = SLOTS * me - REACH + index
        width, above, below = 0, 0, 0
        for begin, end, item_width in facts:
            inside = (row >= begin) & (row < end)
            width = jnp.where(inside, item_width, width)
            above = jnp.where(inside & (row > begin), 1, above)
            below = jnp.where(inside & (row + 1 < end), 1, below)
        tab.wwidth[index] = width
        tab.wup[index] = above
        tab.wdown[index] = below
        inner = jnp.clip(row, 0, SLOTS * cycle_size - 1)
        slot = lax.div(inner, cycle_size)
        device = inner - slot * cycle_size
        tab.wgroup[index] = (device * SLOTS + slot) * PITCH
        slot = floor_div(row, cycle_size)
        device = row - slot * cycle_size
        turn = slot - first_slot(SLOTS * me - REACH, device, cycle_size)
        tab.wcame[index] = (device * many + turn) * PITCH
    for device in range(cycle_size):
        first = first_slot(SLOTS * device - REACH, me, cycle_size)
        for turn in range(many):
            tab.sent[device * many + turn] = first + turn
        first = first_slot(SLOTS * me, device, cycle_size)
        for turn in range(few):
            tab.back[device * few + turn] = (first + turn) * cycle_size + device - SLOTS * me
    for slot in range(SLOTS):
        row = slot * cycle_size + me
        source = lax.div(row, SLOTS)
        turn = slot - first_slot(source * SLOTS, me, cycle_size)
        tab.came[slot] = (source * few + turn) * PITCH
        for turn in range(3):
            near = jnp.clip(row + turn - 1, 0, SLOTS * cycle_size - 1)
            tab.around[turn * SLOTS + slot] = near * PITCH
    rows = [slot * cycle_size + me for slot in range(SLOTS)]
    counts, offsets = sort(rows, QROWS, tab.qbase, tab.qspare, tab.qwidth, tab.qitem, 0)
    for item in range(items):
        tab.qfirst[item] = lax.div(offsets[item], QROWS)
        tab.qcount[item] = lax.div(counts[item] + (QROWS - 1), QROWS)


def geometry(lengths, cycle_pos, cycle_size, unit_size):
    items = lengths.shape[0] + 1
    units = 2 * cycle_size
    sizes = [units * items] * 3 + [items + 1] + [items] * 3 + [units * HALF] * 4 + [SLOTS] * 4
    sizes += [SLOTS + 2 * REACH] * 5
    many, few = pieces(cycle_size)
    sizes += [cycle_size * many, cycle_size * few, SLOTS, 3 * SLOTS]
    smem = pl.BlockSpec(memory_space=pltpu.SMEM)
    return Tables(
        *pl.pallas_call(
            functools.partial(geometry_kernel, cycle_size, unit_size),
            in_specs=[smem, smem],
            out_specs=[smem] * TABLES,
            out_shape=[jax.ShapeDtypeStruct((size,), jnp.int32) for size in sizes],
            name="geometry",
        )(lengths, cycle_pos.reshape(1))
    )


def places(base, spare, width, first, slots):
    token = lax.broadcasted_iota(jnp.int32, (1, slots * ROWW), 1)
    place = jnp.zeros_like(token)
    for slot in range(slots):
        column = token - slot * ROWW
        here = jnp.where(column < width[first + slot], base[first + slot], spare[first + slot])
        place = jnp.where((column >= 0) & (column < ROWW), here + column, place)
    return place


def sorter(place, rows):
    spot = lax.broadcasted_iota(jnp.int32, (rows, place.shape[1]), 0)
    return jnp.where(spot == place, 1.0, 0.0).astype(BF16)


def query_sorter(tab, rows):
    return sorter(places(tab.qbase, tab.qspare, tab.qwidth, 0, SLOTS), rows)


def with_dataset(values, width, item, first, ids, table_ref):
    column = lax.broadcasted_iota(jnp.int32, (ROWW, 1), 0)
    parts = []
    for slot in range(values.shape[0] // ROWW):
        number = jnp.minimum(item[first + slot], ids.shape[0] - 1)
        added = table_ref[pl.ds(ids[number], 1), :]
        real = column < width[first + slot]
        parts.append(values[slot * ROWW : (slot + 1) * ROWW] + jnp.where(real, added, 0.0))
    return jnp.concatenate(parts, axis=0)


def layer_norm(hidden, norm_gain, norm_bias):
    centred = hidden - jnp.mean(hidden, axis=-1, keepdims=True)
    variance = jnp.mean(centred * centred, axis=-1, keepdims=True)
    return centred * lax.rsqrt(variance + EPS) * norm_gain + norm_bias


def sort_step_kernel(step, ubase, uspare, uwidth, uitem, ids, *refs):
    mine_ref, other_ref, table_ref, gain_ref, bias_ref, out_ref = refs
    unit_size = out_ref.shape[0] // 4
    count = HALF * ROWW
    for unit in range(4):
        source = (mine_ref, other_ref)[unit // 2]
        first = (4 * step + unit) * HALF
        values = source[unit % 2 * count : (unit % 2 + 1) * count, :].astype(F32)
        values = with_dataset(values, uwidth, uitem, first, ids, table_ref)
        normed = layer_norm(values, gain_ref[...], bias_ref[...]).astype(BF16)
        matrix = sorter(places(ubase, uspare, uwidth, first, HALF), unit_size)
        out_ref[unit * unit_size : (unit + 1) * unit_size, :] = jnp.dot(
            matrix, normed, preferred_element_type=F32
        ).astype(BF16)


def sort_step(step, tab, ids, mine, other, table, gain, bias, unit_size):
    return pl.pallas_call(
        functools.partial(sort_step_kernel, step),
        grid_spec=pltpu.PrefetchScalarGridSpec(
            num_scalar_prefetch=5,
            in_specs=[pl.BlockSpec(memory_space=pltpu.VMEM)] * 5,
            out_specs=pl.BlockSpec(memory_space=pltpu.VMEM),
        ),
        out_shape=jax.ShapeDtypeStruct((4 * unit_size, mine.shape[1]), BF16),
        cost_estimate=cost(3),
        compiler_params=pltpu.CompilerParams(vmem_limit_bytes=VMEM),
        name="sort_step",
    )(tab.ubase, tab.uspare, tab.uwidth, tab.uitem, ids, mine, other, table, gain, bias)


def own_start_kernel(qbase, qspare, qwidth, qitem, ids, *refs):
    tokens_ref, table_ref, gain_ref, bias_ref, weight_ref, start_ref, normed_ref, query_ref = refs
    values = tokens_ref[...].astype(F32)
    values = with_dataset(values, qwidth, qitem, 0, ids, table_ref)
    start_ref[...] = values
    normed = layer_norm(values, gain_ref[...], bias_ref[...]).astype(BF16)
    normed_ref[...] = normed
    matrix = sorter(places(qbase, qspare, qwidth, 0, SLOTS), query_ref.shape[0])
    sorted_norm = jnp.dot(matrix, normed, preferred_element_type=F32).astype(BF16)
    query = jnp.dot(sorted_norm, weight_ref[...], preferred_element_type=F32)
    query_ref[...] = (query * (1.0 / math.sqrt(HEAD))).astype(BF16)


def own_start(tab, ids, tokens, table, gain, bias, weight, query_rows):
    vmem = pl.BlockSpec(memory_space=pltpu.VMEM)
    return pl.pallas_call(
        own_start_kernel,
        grid_spec=pltpu.PrefetchScalarGridSpec(
            num_scalar_prefetch=5, in_specs=[vmem] * 5, out_specs=[vmem] * 3
        ),
        out_shape=[
            jax.ShapeDtypeStruct(tokens.shape, F32),
            jax.ShapeDtypeStruct(tokens.shape, BF16),
            jax.ShapeDtypeStruct((query_rows, tokens.shape[1]), BF16),
        ],
        cost_estimate=cost(5),
        compiler_params=pltpu.CompilerParams(vmem_limit_bytes=VMEM),
        name="own_start",
    )(tab.qbase, tab.qspare, tab.qwidth, tab.qitem, ids, tokens, table, gain, bias, weight)


def query_blocks(first, many, body):
    def pair(number, none):
        body(first + 2 * number, 2)
        return none

    lax.fori_loop(0, many // 2, pair, 0)

    @pl.when(many % 2 == 1)
    def _():
        body(first + many - 1, 1)


def for_items(items, klen, body):
    def one(item, none):
        body(item, KEYS, (klen[item] + KEYS - 1) // KEYS)
        return none

    lax.fori_loop(0, items - 1, one, 0)
    last = items - 1
    body(last, SPARE_KEYS, (klen[last] + SPARE_KEYS - 1) // SPARE_KEYS)


def as_column(row):
    return row.T[:, :1]


def attend_kernel(heads, units, items, *refs):
    tab, refs = Tables(*refs[:TABLES]), refs[TABLES:]
    koff, kcnt, kdst, kstart, klen, qfirst, qcount = tab[:7]
    steps = units // 4
    q_ref, wk_ref, wv_ref = refs[:3]
    n_refs, refs = refs[3 : 3 + steps], refs[3 + steps :]
    att_ref, o_ref, lse_ref, ns_ref, bias_ref, ks_ref, vs_ref = refs[:7]
    acc_ref, top_ref, total_ref, matrix = refs[7:]
    stride = n_refs[0].shape[0]
    cols = heads * QROWS
    width = ns_ref.shape[1]
    o_ref[...] = jnp.zeros_like(o_ref)
    lse_ref[...] = jnp.zeros_like(lse_ref)
    used = kstart[items]

    @pl.when(pl.program_id(0) == 0)
    def _():
        matrix[...] = query_sorter(tab, o_ref.shape[0])

        def one_item(item, size, blocks):
            def one_unit(turn, unit, none):
                entry = (4 * turn + unit) * items + item
                count, source, target = kcnt[entry], koff[entry] - turn * stride, kdst[entry]

                def step(part, none):
                    src = pl.ds(pl.multiple_of(source + 64 * part, 16), 64)
                    dst = pl.ds(pl.multiple_of(target + 64 * part, 16), 64)
                    ns_ref[dst, :] = n_refs[turn][src, :]
                    row = lax.broadcasted_iota(jnp.int32, (64, 128), 0) + 64 * part
                    bias_ref[dst, :] = jnp.where(row < count, 0.0, NEG).astype(BF16)
                    return none

                return lax.fori_loop(0, (count + 63) // 64, step, none)

            for turn in range(steps):
                lax.fori_loop(0, 4, functools.partial(one_unit, turn), 0)
            end = kstart[item] + klen[item]

            def clear(part, none):
                tail = pl.ds(pl.multiple_of(end + 64 * part, 16), 64)
                ns_ref[tail, :] = jnp.zeros((64, width), BF16)
                bias_ref[tail, :] = jnp.full((64, 128), NEG, BF16)
                return none

            lax.fori_loop(0, (kstart[item + 1] - end + 63) // 64 + 1, clear, 0)

        for_items(items, klen, one_item)

        def clear(part, none):
            tail = pl.ds(pl.multiple_of(used + 64 * part, 16), 64)
            ns_ref[tail, :] = jnp.zeros((64, width), BF16)
            return none

        lax.fori_loop(0, (ns_ref.shape[0] - used) // 64, clear, 0)

    def project(block, none):
        here = pl.ds(pl.multiple_of(block * ROWS, ROWS), ROWS)
        rows = ns_ref[here, :]
        ks_ref[here, :] = jnp.dot(rows, wk_ref[...], preferred_element_type=F32).astype(BF16)
        vs_ref[here, :] = jnp.dot(rows, wv_ref[...], preferred_element_type=F32).astype(BF16)
        return none

    lax.fori_loop(0, (used + ROWS - 1) // ROWS, project, 0)

    def one_item(item, size, blocks):
        def some_queries(place, count):
            wide = count * cols
            rows = pl.ds(pl.multiple_of(place * QROWS, QROWS), count * QROWS)
            block = q_ref[rows, :]
            queries = jnp.concatenate(
                [spread(block[n * QROWS : (n + 1) * QROWS], heads) for n in range(count)], axis=0
            )
            top, total, acc = top_ref.at[:, :wide], total_ref.at[:, :wide], acc_ref.at[:wide]
            top[...] = jnp.full((8, wide), NEG, F32)
            total[...] = jnp.zeros((8, wide), F32)
            acc[...] = jnp.zeros((wide, heads * HEAD), F32)

            def step(number, none):
                here = pl.ds(pl.multiple_of(kstart[item] + number * size, 16), size)
                scores = lax.dot_general(
                    ks_ref[here, :], queries, NT, preferred_element_type=F32
                ) + lanes(bias_ref[here, :].astype(F32), wide)
                best = jnp.max(jnp.max(scores.reshape(size // 8, 8, wide), axis=0), axis=0)
                old = top[...]
                best = jnp.maximum(old, jnp.broadcast_to(best[None], (8, wide)))
                top[...] = best
                shrink = jnp.exp(old - best)
                weights = jnp.exp(scores - best[:1])
                total[...] = total[...] * shrink + jnp.sum(
                    weights.reshape(size // 8, 8, wide), axis=0
                )
                acc[...] = acc[...] * as_column(shrink) + lax.dot_general(
                    weights.astype(BF16),
                    vs_ref[here, :],
                    (((0,), (0,)), ((), ())),
                    preferred_element_type=F32,
                )
                return none

            lax.fori_loop(0, blocks, step, 0)
            summed = jnp.broadcast_to(jnp.sum(total[...], axis=0, keepdims=True), (8, wide))
            lse = top[...] + jnp.log(summed)
            out = acc[...] * as_column(1.0 / summed)
            for n in range(count):
                part = slice(n * cols, (n + 1) * cols)
                lse_ref[pl.ds(place + n, 1), :] = lse[:1, part]
                o_ref[pl.ds(pl.multiple_of((place + n) * QROWS, QROWS), QROWS), :] = gathered(
                    out[part], heads
                )

        query_blocks(qfirst[item], qcount[item], some_queries)

    for_items(items, klen, one_item)
    att_ref[...] = lax.dot_general(
        matrix[...], o_ref[...].astype(BF16), FLIP, preferred_element_type=F32
    ).astype(BF16)


def attend_back_kernel(heads, units, items, unit_size, me, *refs):
    tab, refs = Tables(*refs[:TABLES]), refs[TABLES:]
    koff, kcnt, kdst, kstart, klen, qfirst, qcount = tab[:7]
    q_ref, grad_ref, o_ref, lse_ref, ks_ref, vs_ref, wk_ref, wv_ref, ns_ref, bias_ref = refs[:10]
    dq_ref, gk_ref, gv_ref, dn_ref = refs[10:14]
    (
        spread_q, spread_do, delta, dq_acc, dk_acc, dv_acc, gk_acc, gv_acc, dn_acc,
        matrix, do_ref, dqs, unit_rows,
    ) = refs[14:]
    feats = heads * HEAD
    cols = heads * QROWS
    flip = FLIP
    dqs[...] = jnp.zeros_like(dqs)
    gk_acc[...] = jnp.zeros_like(gk_acc)
    gv_acc[...] = jnp.zeros_like(gv_acc)
    used = qfirst[items - 1] + qcount[items - 1]

    @pl.when(pl.program_id(0) == 0)
    def _():
        dn_acc[...] = jnp.zeros_like(dn_acc)
        matrix[...] = query_sorter(tab, q_ref.shape[0])

    do_ref[...] = jnp.dot(matrix[...], grad_ref[...], preferred_element_type=F32).astype(BF16)

    def prepare(place, none):
        rows = pl.ds(pl.multiple_of(place * QROWS, QROWS), QROWS)
        grads = do_ref[rows, :]
        spread_q[place] = spread(q_ref[rows, :], heads)
        spread_do[place] = spread(grads, heads)
        product = spread(grads.astype(F32) * o_ref[rows, :], heads)
        delta[place] = lax.dot_general(
            jnp.ones((8, feats), F32), product, NT, precision=HIGH, preferred_element_type=F32
        )
        dq_acc[place] = jnp.zeros((cols, feats), F32)
        return none

    lax.fori_loop(0, used, prepare, 0)

    def one_item(item, size, blocks):
        def one_block(number, none):
            here = pl.ds(pl.multiple_of(kstart[item] + number * size, 16), size)
            dk_acc[:size] = jnp.zeros((size, feats), F32)
            dv_acc[:size] = jnp.zeros((size, feats), F32)

            def some_queries(place, count):
                wide = count * cols
                spot = pl.ds(place, count)
                queries = spread_q[spot].reshape(wide, feats)
                grads = spread_do[spot].reshape(wide, feats)
                row = [lse_ref[pl.ds(place + n, 1), :] for n in range(count)]
                log_total = jnp.concatenate(row, axis=1)
                shift = jnp.concatenate([delta[place + n, :1, :] for n in range(count)], axis=1)
                keys = ks_ref[here, :]
                scores = lax.dot_general(keys, queries, NT, preferred_element_type=F32)
                weights = jnp.exp(scores + lanes(bias_ref[here, :].astype(F32), wide) - log_total)
                slopes = lax.dot_general(vs_ref[here, :], grads, NT, preferred_element_type=F32)
                score_grads = (weights * (slopes - shift)).astype(BF16)
                dv_acc[:size] += jnp.dot(weights.astype(BF16), grads, preferred_element_type=F32)
                dk_acc[:size] += jnp.dot(score_grads, queries, preferred_element_type=F32)
                part = lax.dot_general(score_grads, keys, flip, preferred_element_type=F32)
                dq_acc[spot] += part.reshape(count, cols, feats)

            query_blocks(qfirst[item], qcount[item], some_queries)
            dk = dk_acc[:size].astype(BF16)
            dv = dv_acc[:size].astype(BF16)
            dn_acc[here, :] += (
                lax.dot_general(dk, wk_ref[...], NT, preferred_element_type=F32)
                + lax.dot_general(dv, wv_ref[...], NT, preferred_element_type=F32)
            ).astype(dn_acc.dtype)
            rows = ns_ref[here, :]
            gk_acc[...] += lax.dot_general(rows, dk, flip, preferred_element_type=F32)
            gv_acc[...] += lax.dot_general(rows, dv, flip, preferred_element_type=F32)
            return none

        lax.fori_loop(0, jnp.where(qcount[item] > 0, blocks, 0), one_block, 0)

    for_items(items, klen, one_item)

    def finish(place, none):
        rows = pl.ds(pl.multiple_of(place * QROWS, QROWS), QROWS)
        scale = 1.0 / math.sqrt(HEAD)
        dqs[rows, :] = (gathered(dq_acc[place], heads) * scale).astype(BF16)
        return none

    lax.fori_loop(0, used, finish, 0)
    dq_ref[...] = lax.dot_general(
        matrix[...], dqs[...], flip, preferred_element_type=F32
    ).astype(BF16)
    gk_ref[...] = gk_acc[...].astype(BF16)
    gv_ref[...] = gv_acc[...].astype(BF16)

    @pl.when(pl.program_id(0) == pl.num_programs(0) - 1)
    def _():
        unit_rows[...] = jnp.zeros_like(unit_rows)
        count = HALF * ROWW

        def one_unit(unit, none):
            def one_item(item, none):
                entry = unit * items + item
                source, target = koff[entry] - unit * unit_size, kdst[entry]

                def step(part, none):
                    src = pl.ds(pl.multiple_of(source + 64 * part, 16), 64)
                    dst = pl.ds(pl.multiple_of(target + 64 * part, 16), 64)
                    unit_rows[src, :] = dn_acc[dst, :]
                    return none

                return lax.fori_loop(0, (kcnt[entry] + 63) // 64, step, none)

            lax.fori_loop(0, items, one_item, 0)
            place = places(tab.ubase, tab.uspare, tab.uwidth, unit * HALF, HALF)
            source, half = unit_source(unit, me[0], units // 4)
            spot = (2 * source + half) * count
            dn_ref[pl.ds(pl.multiple_of(spot, 16), count), :] = lax.dot_general(
                sorter(place, unit_size), unit_rows[...], flip, preferred_element_type=F32
            ).astype(BF16)
            return none

        lax.fori_loop(0, units, one_unit, 0)


def gelu_parts(values):
    slope = 0.7978845608028654
    bent = jnp.tanh(slope * (values + 0.044715 * values * values * values))
    return bent, slope * (1.0 + 3.0 * 0.044715 * values * values)


def gelu(values):
    return 0.5 * values * (1.0 + gelu_parts(values)[0])


def gelu_slope(values):
    bent, inner = gelu_parts(values)
    return 0.5 * (1.0 + bent) + 0.5 * values * (1.0 - bent * bent) * inner


def merge_kernel(
    cycle_size, wwidth, wup, wdown, wgroup, wcame, back,
    came_ref, group_ref, k11, k12, k21, k22, out_weight, grad_ref, mapped_ref, shares_ref,
    x1, x2, x3, x4, g3, real_ref, up_ref, down_ref, c1, m1, c3, m2g, m1g, win_ref, rows_ref,
):
    window = SLOTS + 2 * REACH
    column = lax.broadcasted_iota(jnp.int32, (PITCH, 128), 0)
    for row in range(window):
        spots = pl.ds(row * PITCH, PITCH)
        win_ref[spots, :CH] = came_ref[pl.ds(pl.multiple_of(wcame[row], 16), PITCH), :]
        win_ref[spots, CH:] = group_ref[pl.ds(pl.multiple_of(wgroup[row], 16), PITCH), :]
        real = jnp.where(column < wwidth[row], 1.0, 0.0)
        real_ref[spots, :] = real
        up_ref[spots, :] = real * wup[row].astype(F32)
        down_ref[spots, :] = real * wdown[row].astype(F32)

    def at(low, high):
        return slice(low * PITCH, high * PITCH)

    def masked(ref, values, low, high):
        return values * lanes(ref[at(low, high), :], CH)

    def fill(taps, values, low, high):
        spots = at(low + 1, high + 1)
        size = values.shape[0]
        taps[spots, :CH] = pltpu.roll(values, 1, 0).astype(BF16)
        taps[spots, CH : 2 * CH] = values.astype(BF16)
        taps[spots, 2 * CH :] = pltpu.roll(values, size - 1, 0).astype(BF16)

    def conv(taps, kernel, low, high):
        def part(row_step):
            rows = taps[at(low + 1 + row_step, high + 1 + row_step), :]
            first = (row_step + 1) * 3 * CH
            return jnp.dot(rows, kernel[first : first + 3 * CH, :], preferred_element_type=F32)

        total = masked(real_ref, part(0), low, high)
        total = total + masked(up_ref, part(-1), low, high)
        return total + masked(down_ref, part(1), low, high)

    def conv_back(kernel, low, high):
        def part(row_step):
            rows = at(low + 1 + row_step, high + 1 + row_step)
            total = None
            for col_step in (-1, 0, 1):
                first = (8 - (3 * (row_step + 1) + col_step + 1)) * CH
                side = (col_step + 1) * CH
                now = lax.dot_general(
                    g3[rows, side : side + CH],
                    kernel[first : first + CH, :],
                    NT,
                    preferred_element_type=F32,
                )
                total = now if total is None else total + now
            return total

        total = masked(real_ref, part(0), low, high)
        total = total + masked(up_ref, part(-1), low, high)
        return total + masked(down_ref, part(1), low, high)

    own, last = REACH, REACH + SLOTS
    unit_share = 9 * CH // cycle_size
    out_share = CH // cycle_size
    share_rows = 4 * unit_share + out_share

    def weight_grad(taps, gradient, tensor):
        piece = math.gcd(3 * CH, unit_share)
        for row_step, mask in ((-1, up_ref), (0, real_ref), (1, down_ref)):
            now = masked(mask, gradient, own, last).astype(BF16)
            rows = taps[at(own + 1 + row_step, last + 1 + row_step), :]
            block = lax.dot_general(rows, now, FLIP, preferred_element_type=F32).astype(BF16)
            for part in range(3 * CH // piece):
                spot = (row_step + 1) * 3 * CH + part * piece
                share, offset = divmod(spot, unit_share)
                first = share * share_rows + tensor * unit_share + offset
                shares_ref[first : first + piece, :] = block[part * piece : (part + 1) * piece]

    def start(low, high):
        return win_ref[at(low, high), :CH].astype(F32)

    fill(x1, masked(real_ref, gelu(start(0, 24)), 0, 24), 0, 24)
    c1[at(1, 23), :] = conv(x1, k11, 1, 23)
    fill(x2, masked(real_ref, gelu(c1[at(1, 23), :]), 1, 23), 1, 23)
    m1[at(2, 22), :] = start(2, 22) + conv(x2, k12, 2, 22)
    fill(x3, masked(real_ref, gelu(m1[at(2, 22), :]), 2, 22), 2, 22)
    c3[at(3, 21), :] = conv(x3, k21, 3, 21)
    fill(x4, masked(real_ref, gelu(c3[at(3, 21), :]), 3, 21), 3, 21)
    merged = (m1[at(own, last), :] + conv(x4, k22, own, last)).astype(BF16)

    def send(values, ref):
        rows_ref[...] = values
        for piece in range(back.shape[0]):
            row = jnp.minimum(back[piece], SLOTS - 1)
            block = rows_ref[pl.ds(pl.multiple_of(row * PITCH, PITCH), PITCH), :]
            ref[piece * PITCH : (piece + 1) * PITCH, :] = block.astype(BF16)

    mapped_ref[...] = jnp.dot(merged, out_weight[...], preferred_element_type=F32).astype(BF16)
    block = lax.dot_general(
        merged, win_ref[at(own, last), CH:], FLIP, preferred_element_type=F32
    ).astype(BF16)
    for share in range(cycle_size):
        first = share * share_rows + 4 * unit_share
        shares_ref[first : first + out_share, :] = block[share * out_share : (share + 1) * out_share]

    m2g[at(2, 22), :] = lax.dot_general(
        win_ref[at(2, 22), CH:], out_weight[...], NT, preferred_element_type=F32
    )
    fill(g3, masked(real_ref, m2g[at(2, 22), :], 2, 22), 2, 22)
    weight_grad(x4, m2g[at(own, last), :], 3)
    now = gelu_slope(c3[at(3, 21), :]) * conv_back(k22, 3, 21)
    fill(g3, now, 3, 21)
    weight_grad(x3, now[at(own - 3, last - 3)], 2)
    m1g[at(4, 20), :] = m2g[at(4, 20), :] + gelu_slope(m1[at(4, 20), :]) * conv_back(k21, 4, 20)
    fill(g3, masked(real_ref, m1g[at(4, 20), :], 4, 20), 4, 20)
    weight_grad(x2, m1g[at(own, last), :], 1)
    now = gelu_slope(c1[at(5, 19), :]) * conv_back(k12, 5, 19)
    fill(g3, now, 5, 19)
    weight_grad(x1, now[at(own - 5, last - 5)], 0)
    now = gelu_slope(start(own, last)) * conv_back(k11, own, last)
    send(m1g[at(own, last), :] + now, grad_ref)


def pack_kernel(sent, block_ref, weight_ref, out_ref, rows_ref):
    rows_ref[...] = jnp.dot(block_ref[...], weight_ref[...], preferred_element_type=F32)
    blank = jnp.zeros((PITCH - ROWW, CH), F32)
    for piece in range(sent.shape[0]):
        slot = jnp.clip(sent[piece], 0, SLOTS - 1)
        block = rows_ref[pl.ds(pl.multiple_of(slot * ROWW, 8), ROWW), :]
        out_ref[piece * PITCH : (piece + 1) * PITCH, :] = jnp.concatenate(
            [block, blank], axis=0
        ).astype(BF16)


def pack(tab, block_out, weight):
    vmem = pl.BlockSpec(memory_space=pltpu.VMEM)
    return pl.pallas_call(
        pack_kernel,
        grid_spec=pltpu.PrefetchScalarGridSpec(
            num_scalar_prefetch=1,
            in_specs=[vmem] * 2,
            out_specs=vmem,
            scratch_shapes=[pltpu.VMEM((block_out.shape[0], CH), F32)],
        ),
        out_shape=jax.ShapeDtypeStruct((tab.sent.shape[0] * PITCH, CH), BF16),
        cost_estimate=cost(2),
        compiler_params=pltpu.CompilerParams(vmem_limit_bytes=VMEM),
        name="pack",
    )(tab.sent, block_out, weight)


def unpack_kernel(came, rows_ref, out_ref):
    parts = []
    for slot in range(came.shape[0]):
        block = rows_ref[pl.ds(pl.multiple_of(came[slot], 16), PITCH), :].astype(F32)
        parts.append(block[:ROWW])
    out_ref[...] = jnp.concatenate(parts, axis=0).astype(BF16)


def unpack(came, rows):
    vmem = pl.BlockSpec(memory_space=pltpu.VMEM)
    return pl.pallas_call(
        unpack_kernel,
        grid_spec=pltpu.PrefetchScalarGridSpec(
            num_scalar_prefetch=1, in_specs=[vmem], out_specs=vmem
        ),
        out_shape=jax.ShapeDtypeStruct((came.shape[0] * ROWW, CH), BF16),
        cost_estimate=cost(1),
        compiler_params=pltpu.CompilerParams(vmem_limit_bytes=VMEM),
        name="unpack",
    )(came, rows)


def merge(tab, came, group, kernels, out_weight, cycle_size):
    window = SLOTS + 2 * REACH
    vmem = pl.BlockSpec(memory_space=pltpu.VMEM)
    padded = (window + 2) * PITCH
    share_rows = 4 * (9 * CH // cycle_size) + CH // cycle_size
    small = pltpu.VMEM((window * PITCH, 128), F32)
    large = pltpu.VMEM((window * PITCH, CH), F32)
    return pl.pallas_call(
        functools.partial(merge_kernel, cycle_size),
        grid_spec=pltpu.PrefetchScalarGridSpec(
            num_scalar_prefetch=6,
            in_specs=[vmem] * 7,
            out_specs=[vmem] * 3,
            scratch_shapes=[pltpu.VMEM((padded, 3 * CH), BF16)] * 5
            + [small] * 3
            + [large] * 5
            + [
                pltpu.VMEM((window * PITCH, 2 * CH), BF16),
                pltpu.VMEM((SLOTS * PITCH, CH), F32),
            ],
        ),
        out_shape=[
            jax.ShapeDtypeStruct((tab.back.shape[0] * PITCH, CH), BF16),
            jax.ShapeDtypeStruct((SLOTS * PITCH, CH), BF16),
            jax.ShapeDtypeStruct((cycle_size * share_rows, CH), BF16),
        ],
        cost_estimate=cost(25),
        compiler_params=pltpu.CompilerParams(vmem_limit_bytes=VMEM),
        name="merge",
    )(
        tab.wwidth, tab.wup, tab.wdown, tab.wgroup, tab.wcame, tab.back,
        came, group, *kernels, out_weight,
    )


def attend(tab, query, key_weight, value_weight, norms, sorted_keys, units, items, heads):
    feats = heads * HEAD
    cols = heads * QROWS
    width = query.shape[1]
    groups = width // feats
    blocks8 = (query.shape[0] // QROWS + 7) // 8 * 8
    once = pl.Buffered(1) if units > 16 else None

    def part(rows, columns=feats):
        return pl.BlockSpec((rows, columns), lambda group, *_: (0, group), pipeline_mode=once)

    def whole(rows, columns):
        return pl.BlockSpec(
            (rows, columns), lambda group, *_: (0, 0), pipeline_mode=pl.Buffered(1)
        )

    return pl.pallas_call(
        functools.partial(attend_kernel, heads, units, items),
        grid_spec=pltpu.PrefetchScalarGridSpec(
            num_scalar_prefetch=TABLES,
            grid=(groups,),
            in_specs=[part(query.shape[0]), part(width), part(width)]
            + [whole(*norm.shape) for norm in norms],
            out_specs=[
                part(SLOTS * ROWW),
                part(query.shape[0]),
                part(blocks8, cols),
                whole(sorted_keys, width),
                whole(sorted_keys, 128),
                part(sorted_keys),
                part(sorted_keys),
            ],
            scratch_shapes=[
                pltpu.VMEM((2 * cols, feats), F32),
                pltpu.VMEM((8, 2 * cols), F32),
                pltpu.VMEM((8, 2 * cols), F32),
                pltpu.VMEM((query.shape[0], SLOTS * ROWW), BF16),
            ],
        ),
        out_shape=[
            jax.ShapeDtypeStruct((SLOTS * ROWW, width), BF16),
            jax.ShapeDtypeStruct(query.shape, F32),
            jax.ShapeDtypeStruct((blocks8, groups * cols), F32),
            jax.ShapeDtypeStruct((sorted_keys, width), BF16),
            jax.ShapeDtypeStruct((sorted_keys, 128), BF16),
            jax.ShapeDtypeStruct((sorted_keys, width), BF16),
            jax.ShapeDtypeStruct((sorted_keys, width), BF16),
        ],
        cost_estimate=cost(70),
        compiler_params=pltpu.CompilerParams(vmem_limit_bytes=VMEM),
        name="attend",
    )(*tab, query, key_weight, value_weight, *norms)


def attend_back(
    tab, cycle_pos, query, grads, outputs, lse, ks, vs, key_weight, value_weight, ns, bias,
    unit_size, units, items, heads,
):
    feats = heads * HEAD
    cols = heads * QROWS
    rows, width = query.shape
    groups = width // feats
    blocks = rows // QROWS
    once = pl.Buffered(1) if units > 16 else None

    def part(rows, columns=feats):
        return pl.BlockSpec((rows, columns), lambda group, *_: (0, group), pipeline_mode=once)

    def whole(rows, columns):
        return pl.BlockSpec(
            (rows, columns), lambda group, *_: (0, 0), pipeline_mode=pl.Buffered(1)
        )

    return pl.pallas_call(
        functools.partial(attend_back_kernel, heads, units, items, unit_size),
        grid_spec=pltpu.PrefetchScalarGridSpec(
            num_scalar_prefetch=TABLES + 1,
            grid=(groups,),
            in_specs=[
                part(rows),
                part(grads.shape[0]),
                part(rows),
                part(lse.shape[0], cols),
                part(ks.shape[0]),
                part(ks.shape[0]),
                part(width),
                part(width),
                whole(*ns.shape),
                whole(*bias.shape),
            ],
            out_specs=[
                part(grads.shape[0]),
                part(width),
                part(width),
                whole(units * HALF * ROWW, width),
            ],
            scratch_shapes=[
                pltpu.VMEM((blocks, cols, feats), BF16),
                pltpu.VMEM((blocks, cols, feats), BF16),
                pltpu.VMEM((blocks, 8, cols), F32),
                pltpu.VMEM((blocks, cols, feats), F32),
                pltpu.VMEM((SPARE_KEYS, feats), F32),
                pltpu.VMEM((SPARE_KEYS, feats), F32),
                pltpu.VMEM((width, feats), F32),
                pltpu.VMEM((width, feats), F32),
                pltpu.VMEM(ns.shape, BF16),
                pltpu.VMEM((rows, grads.shape[0]), BF16),
                pltpu.VMEM((rows, feats), BF16),
                pltpu.VMEM((rows, feats), BF16),
                pltpu.VMEM((unit_size, width), BF16),
            ],
        ),
        out_shape=[
            jax.ShapeDtypeStruct(grads.shape, BF16),
            jax.ShapeDtypeStruct((width, width), BF16),
            jax.ShapeDtypeStruct((width, width), BF16),
            jax.ShapeDtypeStruct((units * HALF * ROWW, width), BF16),
        ],
        cost_estimate=cost(90),
        compiler_params=pltpu.CompilerParams(vmem_limit_bytes=VMEM),
        name="attend_back",
    )(cycle_pos.reshape(1), *tab, query, grads, outputs, lse, ks, vs, key_weight, value_weight, ns, bias)


@functools.cache
def most_rows(cycle_size, item_count):
    rows = np.arange(SLOTS)[:, None] * cycle_size + np.arange(cycle_size)
    most_keys = most_unit = most_queries = 0
    lists = [()]
    while lists:
        heights = lists.pop()
        if len(heights) < item_count:
            for height in (24, 30):
                if sum(heights) + height <= SLOTS * cycle_size:
                    lists.append(heights + (height,))
        if not heights:
            continue
        ends = np.cumsum(heights)
        number = np.searchsorted(ends, rows, side="right")
        wide = np.array([24 if height == 24 else ROWW for height in heights] + [0])[number]
        kinds = np.arange(len(heights))
        counts = [((number == kind) * wide) for kind in kinds] + [ROWW - wide]
        counts = np.stack(counts)

        def rounded(values, align):
            return -(-values // align) * align

        units = rounded(counts.reshape(len(counts), 2, HALF, cycle_size).sum(2), 16)
        most_unit = max(most_unit, units.sum(0).max())
        keys = units.sum((1, 2))
        keys = rounded(keys[:-1], KEYS).sum() + rounded(keys[-1], SPARE_KEYS)
        most_keys = max(most_keys, keys)
        most_queries = max(most_queries, rounded(counts.sum(1), QROWS).sum(0).max())
    return int(most_keys), int(most_unit), int(most_queries)


def passed(value, axis, target):
    pairs = [(source, target(source)) for source in range(lax.axis_size(axis))]
    return lax.ppermute(value, axis, pairs)


def passed_along(value, axis, steps):
    count = lax.axis_size(axis)
    return passed(value, axis, lambda source: (source + steps) % count)


def tied(*values):
    return lax.optimization_barrier(values)


def to_sibling(value):
    return passed(value, "blk", lambda source: source ^ 1)


def gelu_tanh(values):
    return (
        0.5
        * values
        * (1.0 + jnp.tanh(0.7978845608028654 * (values + 0.044715 * values * values * values)))
    )


def gelu_back(values, gradient):
    return jax.vjp(gelu_tanh, values)[1](gradient)[0]


def item_facts(lengths):
    facts, start = [], 0
    for item in range(lengths.shape[0]):
        length = lengths[item]
        height = jnp.where(length == 1200, 30, jnp.where(length == 576, 24, 0))
        width = jnp.where(length == 1200, 40, 24)
        facts.append((start, start + height, height, width))
        start = start + height
    return facts


def row_facts(facts, rows):
    number = jnp.full_like(rows, len(facts))
    local, height, width = rows, jnp.zeros_like(rows), jnp.zeros_like(rows)
    for item, (start, end, item_height, item_width) in enumerate(facts):
        inside = (rows >= start) & (rows < end)
        number = jnp.where(inside, item, number)
        local = jnp.where(inside, rows - start, local)
        height = jnp.where(inside, item_height, height)
        width = jnp.where(inside, item_width, width)
    return number, local, height, width


def tap_masks(local_row, height, width):
    column = lax.broadcasted_iota(jnp.int32, (1, ROWW), 1)
    is_real = column < width
    all_masks = []
    for row_step in (-1, 0, 1):
        rows_fine = (local_row + row_step >= 0) & (local_row + row_step < height)
        for col_step in (-1, 0, 1):
            cols_fine = (column + col_step >= 0) & (column + col_step < width)
            all_masks.append(is_real & rows_fine & cols_fine)
    return is_real, all_masks


def side_shift(values, col_step):
    if col_step == 0:
        return values
    empty_col = jnp.zeros_like(values[:, :1])
    if col_step < 0:
        return jnp.concatenate([empty_col, values[:, :-1]], axis=1)
    return jnp.concatenate([values[:, 1:], empty_col], axis=1)


def from_above(values, cycle_pos):
    got = passed_along(values, "blk", 1)
    empty_row = jnp.zeros_like(values[:1])
    return jnp.where(cycle_pos == 0, jnp.concatenate([empty_row, got[:-1]], axis=0), got)


def from_below(values, cycle_pos, cycle_size):
    got = passed_along(values, "blk", -1)
    empty_row = jnp.zeros_like(values[:1])
    return jnp.where(
        cycle_pos == cycle_size - 1, jnp.concatenate([got[1:], empty_row], axis=0), got
    )


def upsample_forward(row_above, values, row_below, all_masks):
    center = values.astype(F32)
    upper_value = jnp.where(all_masks[1][:, :, None], row_above, values).astype(F32)
    lower_value = jnp.where(all_masks[7][:, :, None], row_below, values).astype(F32)
    pieces = []
    for half_rows in (0.75 * center + 0.25 * upper_value, 0.75 * center + 0.25 * lower_value):
        left_value = jnp.where(all_masks[3][:, :, None], side_shift(half_rows, -1), half_rows)
        right_value = jnp.where(all_masks[5][:, :, None], side_shift(half_rows, 1), half_rows)
        pieces.append(0.75 * half_rows + 0.25 * left_value)
        pieces.append(0.75 * half_rows + 0.25 * right_value)
    joined = jnp.concatenate(pieces, axis=2)
    return joined.reshape(-1, joined.shape[2])


def upsample_back_columns(gradient, all_masks):
    channels = gradient.shape[2] // 4
    left_fine = all_masks[3][:, :, None]
    right_fine = all_masks[5][:, :, None]
    halves = []
    for half in (0, 1):
        left_part = gradient[:, :, 2 * half * channels : (2 * half + 1) * channels].astype(F32)
        right_part = gradient[:, :, (2 * half + 1) * channels : (2 * half + 2) * channels].astype(
            F32
        )
        side = jnp.where(right_fine, side_shift(left_part, 1), 0.0)
        side = side + jnp.where(left_fine, 0.0, left_part)
        side = side + jnp.where(left_fine, side_shift(right_part, -1), 0.0)
        side = side + jnp.where(right_fine, 0.0, right_part)
        halves.append(0.75 * (left_part + right_part) + 0.25 * side)
    return [half.astype(BF16) for half in halves]


def upsample_back_rows(upper, lower, upper_next, lower_prev, all_masks):
    up_fine = all_masks[1][:, :, None]
    down_fine = all_masks[7][:, :, None]
    rows = jnp.where(down_fine, upper_next, lower).astype(F32)
    rows = rows + jnp.where(up_fine, lower_prev, upper).astype(F32)
    return 0.75 * (upper.astype(F32) + lower.astype(F32)) + 0.25 * rows


def dot32(left, right, **more):
    return jnp.dot(left, right, preferred_element_type=F32, **more)


def dot_t(left, right):
    return lax.dot_general(left, right, NT, preferred_element_type=F32)


def t_dot(left, right):
    return lax.dot_general(left, right, (((0,), (0,)), ((), ())), preferred_element_type=F32)


def halving(values, device, bit, axis, pairs_axis):
    half = values.shape[axis] // 2
    mine = (device >> bit) & 1
    keep = lax.dynamic_slice_in_dim(values, mine * half, half, axis=axis)
    send = lax.dynamic_slice_in_dim(values, (1 - mine) * half, half, axis=axis)
    return keep, passed(send, pairs_axis, lambda source: source ^ (1 << bit))


def summed(keep, got):
    return (keep.astype(F32) + got.astype(F32)).astype(BF16)


def core_summed(shares, core):
    cycle_size, rows, width = shares.shape
    paired = shares.reshape(cycle_size // 2, 2, rows, width)
    keep = lax.dynamic_index_in_dim(paired, core, 1, keepdims=False)
    send = lax.dynamic_index_in_dim(paired, 1 - core, 1, keepdims=False)
    return (keep.astype(F32) + to_sibling(send).astype(F32)).astype(BF16)


class ChipSums:
    def __init__(self, values, chip):
        half = values.shape[1] // 2
        self.chip, self.chips = chip, values.shape[0]
        self.parts = [(values[:, :half], 1), (values[:, half:], -1)]
        self.moving = [self.block(part, way, 1).astype(BF16) for part, way in self.parts]

    def block(self, part, way, offset):
        spot = (self.chip - way * offset) % self.chips
        return lax.dynamic_index_in_dim(part, spot, 0, keepdims=False).astype(F32)

    def step(self, number):
        moved = []
        for value, (part, way) in zip(self.moving, self.parts):
            got = passed_along(value, "blk", 2 * way).astype(F32)
            moved.append((got + self.block(part, way, number + 1)).astype(BF16))
        self.moving = moved

    def result(self):
        return jnp.concatenate(self.moving, axis=0)


class GroupGather:
    def __init__(self, values, dp_pos):
        self.dp_pos, self.bits = dp_pos, lax.axis_size("dp").bit_length() - 1
        half = values.shape[0] // 2
        self.held = [part[(None,) * self.bits] for part in (values[:half], values[half:])]

    def step(self, number):
        held = []
        for value, bit in zip(self.held, (number, self.bits - 1 - number)):
            axis = self.bits - 1 - bit
            got = passed(value, "dp", lambda source, bit=bit: source ^ (1 << bit))
            mine = (self.dp_pos >> bit) & 1
            held.append(
                jnp.where(
                    mine == 0,
                    jnp.concatenate([value, got], axis=axis),
                    jnp.concatenate([got, value], axis=axis),
                )
            )
        self.held = held

    def result(self):
        shape = (1 << self.bits,)
        return jnp.concatenate(
            [value.reshape(shape + value.shape[self.bits :]) for value in self.held], axis=1
        )


def gathered_over_groups(values, dp_pos):
    gather = GroupGather(values, dp_pos)
    for number in range(gather.bits):
        gather.step(number)
    return gather.result()


def over_groups(values, bit):
    got = passed(values, "dp", lambda source: source ^ (1 << bit))
    return (values.astype(F32) + got.astype(F32)).astype(BF16)


def sum_over_chips(values, chip):
    chips = values.shape[0]
    total = lax.dynamic_index_in_dim(values, chip, 0, keepdims=False).astype(F32)
    for step in range(1, chips):
        send = lax.dynamic_index_in_dim(values, (chip + step) % chips, 0, keepdims=False)
        total = total + passed_along(send, "blk", 2 * step).astype(F32)
    return total


def whole_shares(whole, parts, orders):
    groups = whole.shape[0]
    bits = groups.bit_length() - 1
    out, place = [], 0
    for part, order in zip(parts, orders):
        rows, width = part.shape[1:]
        size = rows * width // 256
        pieces = []
        for turn in range(groups):
            device = sum(((turn >> (bits - 1 - index)) & 1) << bit for index, bit in enumerate(order))
            pieces.append(whole[device, place : place + size].reshape(rows, width))
        out.append(jnp.concatenate(pieces, axis=0).astype(F32))
        place += size
    return out


def shards(
    tokens,
    item_lengths,
    dataset_ids,
    dataset_table,
    norm1_gain,
    norm1_bias,
    query_weight,
    key_weight,
    value_weight,
    out_weight,
    norm2_gain,
    norm2_bias,
    fc1_weight,
    fc2_weight,
    project_weight,
    unit1_first,
    unit1_second,
    unit2_first,
    unit2_second,
    output_weight,
    block_cotangent,
    merged_cotangent,
):
    cycle_size = lax.axis_size("blk")
    cycle_pos = lax.axis_index("blk")
    chips = cycle_size // 2
    chip, core = cycle_pos // 2, cycle_pos % 2
    lengths = item_lengths[0]
    item_count = lengths.shape[0]
    kinds = item_count + 1
    width_model = tokens.shape[1]
    heads = 4 if cycle_size <= 8 else 2
    half_tokens = HALF * ROWW
    token_count = tokens.shape[0]

    facts = item_facts(lengths)
    own_rows = lax.broadcasted_iota(jnp.int32, (SLOTS, 1), 0) * cycle_size + cycle_pos
    number, local_row, height, width = row_facts(facts, own_rows)
    is_real, all_masks = tap_masks(local_row, height, width)
    units = 4 * chips
    most_keys, most_unit, query_rows = most_rows(cycle_size, item_count)
    unit_size = most_unit + 48
    sorted_keys = (most_keys + 128 + ROWS - 1) // ROWS * ROWS
    tab = geometry(lengths, cycle_pos, cycle_size, unit_size)
    ids = dataset_ids[0]
    gain_one, bias_one = norm1_gain.reshape(1, -1), norm1_bias.reshape(1, -1)

    stream_start, normed_one, query = own_start(
        tab, ids, tokens, dataset_table, gain_one, bias_one, query_weight, query_rows
    )
    ahead, behind = tokens[:half_tokens], tokens[half_tokens:]
    sorted_norms = []
    for step in range(chips):
        if step:
            ahead = passed_along(ahead, "blk", 2)
            behind = passed_along(behind, "blk", -2)
            ahead, behind, sorted_norms[-1] = tied(ahead, behind, sorted_norms[-1])
        if step == 1:
            ahead, behind, stream_start, normed_one, query = tied(
                ahead, behind, stream_start, normed_one, query
            )
            ahead, behind, merged_cotangent = tied(ahead, behind, merged_cotangent)
            upper, lower = upsample_back_columns(
                merged_cotangent.reshape(SLOTS, ROWW, -1), all_masks
            )
        if step == 2:
            ahead, behind, upper, lower = tied(ahead, behind, upper, lower)
            upper_next = from_below(upper, cycle_pos, cycle_size)
            lower_prev = from_above(lower, cycle_pos)
        if step == chips - 1:
            ahead, behind, upper_next, lower_prev = tied(ahead, behind, upper_next, lower_prev)
            mapped_grad = upsample_back_rows(
                upper, lower, upper_next, lower_prev, all_masks
            ).astype(BF16)
            mapped_grad = jnp.pad(mapped_grad, ((0, 0), (0, PITCH - ROWW), (0, 0)))
            mapped_grad = mapped_grad.reshape(SLOTS * PITCH, -1)
        mine = jnp.concatenate([ahead, behind], axis=0)
        sorted_norms.append(
            sort_step(
                step, tab, ids, mine, to_sibling(mine), dataset_table, gain_one, bias_one, unit_size
            )
        )
    sorted_norms[-1], mapped_grad = tied(sorted_norms[-1], mapped_grad)
    group_grad = lax.all_gather(mapped_grad, "blk", tiled=True)
    attended, outputs, lse, sorted_norm, bias, ks, vs = attend(
        tab, query, key_weight, value_weight, sorted_norms, sorted_keys, units, kinds, heads
    )
    attended, group_grad = tied(attended, group_grad)

    def as_cells(flattened):
        return flattened.reshape(SLOTS, ROWW, flattened.shape[-1])

    after_attn = stream_start + dot32(attended, out_weight)
    normed_two = layer_norm(after_attn, norm2_gain, norm2_bias).astype(BF16)
    pre_act = dot32(normed_two, fc1_weight)
    hidden = gelu_tanh(pre_act).astype(BF16)
    block_out = (after_attn + dot32(hidden, fc2_weight)).astype(BF16)
    channels = project_weight.shape[1]

    def exchanged(values):
        values = values.reshape(cycle_size, -1, channels)
        return lax.all_to_all(values, "blk", 0, 0).reshape(-1, channels)

    grad_rows, mapped_rows, conv_shares = merge(
        tab,
        exchanged(pack(tab, block_out, project_weight)),
        group_grad,
        (unit1_first, unit1_second, unit2_first, unit2_second),
        output_weight,
        cycle_size,
    )
    conv_shares = conv_shares.reshape(cycle_size, -1, channels)
    group_mapped = lax.all_gather(mapped_rows, "blk", tiled=True)
    reassembled_grad = unpack(tab.came, exchanged(grad_rows))

    def shared_out(*gradients):
        parts = []
        for gradient in gradients:
            parts.append(gradient.astype(BF16).reshape(cycle_size, -1, gradient.shape[-1]))
        return jnp.concatenate(parts, axis=1) if len(parts) > 1 else parts[0]

    dp_pos = lax.axis_index("dp")
    groups = lax.axis_size("dp")
    bits = groups.bit_length() - 1
    one_way = list(range(bits))
    other_way = one_way[::-1]

    def wide(gradient):
        return gradient.reshape(cycle_size, -1, width_model)

    def scattering(shares):
        count, share_rows, share_width = shares.shape
        parts = shares.reshape(count, groups, share_rows // groups, share_width)
        return jnp.swapaxes(parts, 0, 1).reshape(-1, share_width)

    def scattered(parts):
        return lax.psum_scatter(parts, "dp", scatter_dimension=0, tiled=True)

    def dp_halving(values, order, index):
        return halving(values, dp_pos, order[index], 1, "dp")

    def dp_halved(values, order, index):
        return summed(*dp_halving(values, order, index))

    project_grad = t_dot(block_out, reassembled_grad)
    block_grad = block_cotangent.astype(F32) + dot_t(reassembled_grad, project_weight)
    mlp_grad = block_grad.astype(BF16)
    fc2_parts = scattering(shared_out(t_dot(hidden, mlp_grad)))
    mlp_grad, fc2_parts = tied(mlp_grad, fc2_parts)
    fc2_sums = scattered(fc2_parts)
    conv_sums = core_summed(conv_shares, core)
    pre_grad = gelu_back(pre_act, dot_t(mlp_grad, fc2_weight)).astype(BF16)
    fc1_grad = t_dot(normed_two, pre_grad)
    normed_two_grad = dot_t(pre_grad, fc1_weight)
    norm_two_pull = jax.vjp(layer_norm, after_attn, norm2_gain, norm2_bias)[1]
    attn_side, norm2_gain_grad, norm2_bias_grad = norm_two_pull(normed_two_grad)
    after_grad = block_grad + attn_side
    branch_grad = after_grad.astype(BF16)
    out_proj_grad = t_dot(attended, branch_grad)
    attended_grad = dot_t(branch_grad, out_weight).astype(BF16)

    rows = width_model // cycle_size
    rows = width_model // cycle_size
    fc1_sums = core_summed(shared_out(fc1_grad), core)
    out_sums = core_summed(shared_out(out_proj_grad, wide(project_grad)), core)
    attended_grad, conv_sums, fc1_sums, out_sums, fc2_sums = tied(
        attended_grad, conv_sums, fc1_sums, out_sums, fc2_sums
    )
    conv_sums, conv_got = dp_halving(conv_sums, one_way, 0)
    fc1_sums, fc1_got = dp_halving(fc1_sums, other_way, 0)
    out_sums, out_got = dp_halving(out_sums, one_way, 0)
    fc2_sums = lax.psum_scatter(fc2_sums, "blk", scatter_dimension=0, tiled=True)
    query_low, key_grad, value_grad, token_grad = attend_back(
        tab, cycle_pos, query, attended_grad, outputs, lse, ks, vs, key_weight, value_weight, sorted_norm,
        bias, unit_size, units, kinds, heads,
    )
    query_low, key_grad, value_grad, token_grad, conv_got, fc1_got, out_got, fc2_sums = tied(
        query_low, key_grad, value_grad, token_grad, conv_got, fc1_got, out_got, fc2_sums
    )
    normed_one_grad = lax.psum_scatter(token_grad, "blk", scatter_dimension=0, tiled=True)
    conv_sums = summed(conv_sums, conv_got)
    fc1_sums = summed(fc1_sums, fc1_got)
    out_sums = summed(out_sums, out_got)
    query_grad = t_dot(normed_one, query_low)
    key_sums = core_summed(shared_out(key_grad, value_grad), core)
    query_sums = core_summed(shared_out(query_grad), core)

    for index in range(bits):
        if index:
            conv_sums = dp_halved(conv_sums, one_way, index)
            fc1_sums = dp_halved(fc1_sums, other_way, index)
            out_sums = dp_halved(out_sums, one_way, index)
        key_sums = dp_halved(key_sums, one_way, index)
        query_sums = dp_halved(query_sums, other_way, index)
    late = [conv_sums, fc1_sums, out_sums, key_sums, query_sums]
    late_orders = [one_way, other_way, one_way, one_way, other_way]
    chip_sums = ChipSums(
        jnp.concatenate([part.reshape(chips, -1, 256) for part in late], axis=1), chip
    )
    for turn in range(1, chips):
        chip_sums.step(turn)
    around = unpack(tab.around, group_mapped).reshape(3, SLOTS, ROWW, channels)
    merged = upsample_forward(around[0], around[1], around[2], all_masks).astype(BF16)
    fc2_all = gathered_over_groups(fc2_sums, dp_pos)
    normed_one_grad, fc2_all, *chip_sums.moving = tied(
        normed_one_grad, fc2_all, *chip_sums.moving
    )
    gather = GroupGather(chip_sums.result(), dp_pos)
    normed_one_grad = normed_one_grad.astype(F32) + dot_t(query_low, query_weight)

    norm_one_pull = jax.vjp(layer_norm, stream_start, norm1_gain, norm1_bias)[1]
    start_side, norm1_gain_grad, norm1_bias_grad = norm_one_pull(normed_one_grad)
    tokens_grad = after_grad + start_side
    table_rows = dataset_table.shape[0]
    dataset = jnp.full_like(number, -1)
    for item in range(item_count):
        dataset = jnp.where(number == item, ids[item], dataset)
    dataset = jnp.where(is_real, dataset, -1).reshape(1, -1)
    onehot = (dataset == lax.broadcasted_iota(jnp.int32, (table_rows, 1), 0)).astype(F32)
    table_grad = jnp.dot(onehot, tokens_grad, precision=HIGH)
    table_split = jnp.swapaxes(table_grad.reshape(table_rows, cycle_size, rows), 0, 1)
    small = [table_split.reshape(cycle_size, -1)] + [
        gradient.reshape(cycle_size, -1)
        for gradient in (norm1_gain_grad, norm1_bias_grad, norm2_gain_grad, norm2_bias_grad)
    ]
    small = jnp.concatenate(small, axis=1).astype(BF16)
    small_rows = -(-small.shape[1] // 1024) * 8
    small = jnp.pad(small, ((0, 0), (0, small_rows * 128 - small.shape[1])))
    small = small.reshape(cycle_size, small_rows, 128)
    small = core_summed(small, core)
    for bit in range(bits):
        gather.step(bit)
        small = over_groups(small, bit)
    small = sum_over_chips(small, chip).reshape(-1)
    table_size = table_rows * rows
    norms = [small[table_size + index * rows :][:rows] for index in range(4)]

    unit_share = 9 * channels // cycle_size
    out_share = channels // cycle_size
    convs, fc1_share, outs, keys_values, query_share = whole_shares(
        gather.result(), late, late_orders
    )
    return (
        block_out,
        merged,
        tokens_grad,
        small[:table_size].reshape(table_rows, rows),
        norms[0],
        norms[1],
        query_share,
        keys_values[:rows],
        keys_values[rows:],
        outs[:rows],
        norms[2],
        norms[3],
        fc1_share,
        fc2_all.reshape(-1, width_model).astype(F32),
        outs[rows:].reshape(rows, channels),
        convs[:unit_share],
        convs[unit_share : 2 * unit_share],
        convs[2 * unit_share : 3 * unit_share],
        convs[3 * unit_share : 4 * unit_share],
        convs[4 * unit_share :],
    )


def solution(mesh):
    split = P(("dp", "blk"), None)
    placed = (split, P("dp", None), P("dp", None)) + (P(),) * 17 + (split, split)
    rows, line = P("blk", None), P("blk")
    return jax.shard_map(
        shards,
        mesh=mesh,
        in_specs=placed,
        out_specs=(
            split, split, split, P(None, "blk"), line, line, rows, rows, rows, rows, line, line,
            rows, rows, rows, rows, rows, rows, rows, rows,
        ),
        check_vma=False,
    )
```

```python
import functools
import math
import typing

import jax
import jax.numpy as jnp
from jax import lax
from jax.experimental import pallas as pl
from jax.experimental.pallas import tpu as pltpu
from jax.sharding import PartitionSpec as P
import numpy as np

HEADS = 12
HEAD = 64
ROWW = 40
SLOTS = 12
HALF = SLOTS // 2
REACH = 6
PITCH = 48
CH = 256

NEG = -1e30
EPS = 1e-06
HIGH = lax.Precision.HIGHEST
KEYS = 672
SPARE_KEYS = 768
QROWS = 64
TOGETHER = 5
TOGETHER_BACK = 2
ROWS = 1024
VMEM = 60 * 1024 * 1024
NT = (((1,), (1,)), ((), ()))
FLIP = (((0,), (0,)), ((), ()))
F32 = jnp.float32
BF16 = jnp.bfloat16


def cost(microseconds):
    return pl.CostEstimate(flops=microseconds * 10**9, bytes_accessed=10**6, transcendentals=0)


def own_blocks(heads, feats):
    row = lax.broadcasted_iota(jnp.int32, (heads * QROWS, feats), 0) // QROWS
    col = lax.broadcasted_iota(jnp.int32, (heads * QROWS, feats), 1) // HEAD
    return row == col


def spread(block, heads):
    wide = jnp.concatenate([block] * heads, axis=0)
    return jnp.where(own_blocks(heads, block.shape[1]), wide, jnp.zeros((), block.dtype))


def gathered(wide, heads):
    kept = jnp.where(own_blocks(heads, wide.shape[1]), wide, 0.0)
    total = kept[:QROWS]
    for head in range(1, heads):
        total = total + kept[head * QROWS : (head + 1) * QROWS]
    return total


def lanes(column, width):
    return jnp.concatenate([column] * (width // 128), axis=1)


class Tables(typing.NamedTuple):
    koff: jax.Array
    kcnt: jax.Array
    kdst: jax.Array
    kstart: jax.Array
    klen: jax.Array
    qfirst: jax.Array
    qcount: jax.Array
    ubase: jax.Array
    uspare: jax.Array
    uwidth: jax.Array
    uitem: jax.Array
    qbase: jax.Array
    qspare: jax.Array
    qwidth: jax.Array
    qitem: jax.Array
    wwidth: jax.Array
    wup: jax.Array
    wdown: jax.Array
    wgroup: jax.Array
    wcame: jax.Array
    sent: jax.Array
    back: jax.Array
    came: jax.Array
    around: jax.Array


TABLES = len(Tables._fields)


def pieces(cycle_size):
    return -(-(SLOTS + 2 * REACH) // cycle_size), -(-SLOTS // cycle_size)


def floor_div(value, by):
    return lax.div(value + 16 * by, by) - 16


def first_slot(begin, device, cycle_size):
    return -floor_div(device - begin, cycle_size)


def unit_source(unit, me, chips):
    chip, core = lax.div(me, 2), lax.rem(me, 2)
    turn, half = lax.div(unit, 4), lax.rem(unit, 2)
    other = lax.rem(lax.div(unit, 2), 2)
    turn = jnp.where(half == 0, -turn, turn)
    source = 2 * lax.rem(chip + turn + chips, chips) + jnp.where(other == 0, core, 1 - core)
    return source, half


def geometry_kernel(cycle_size, unit_size, lengths, place, *refs):
    tab = Tables(*refs)
    item_count = lengths.shape[0]
    items = item_count + 1
    chips = cycle_size // 2
    units = 4 * chips
    me = place[0]
    many, few = pieces(cycle_size)
    facts, start = [], 0
    for item in range(item_count):
        length = lengths[item]
        height = jnp.where(length == 1200, 30, jnp.where(length == 576, 24, 0))
        facts.append((start, start + height, jnp.where(length == 1200, 40, 24)))
        start = start + height

    def fact(row):
        number, width = item_count, 0
        for item, (begin, end, item_width) in enumerate(facts):
            inside = (row >= begin) & (row < end)
            number = jnp.where(inside, item, number)
            width = jnp.where(inside, item_width, width)
        return number, width

    def up(value, align):
        return lax.div(value + (align - 1), align) * align

    def sort(rows, align, base, spare_base, widths, numbers, first):
        known = [fact(row) for row in rows]
        counts = [
            sum(jnp.where(number == item, width, 0) for number, width in known)
            for item in range(item_count)
        ]
        counts.append(sum(ROWW - width for _, width in known))
        offsets, total = [], 0
        for count in counts:
            offsets.append(total)
            total = total + up(count, align)
        spare = offsets[-1]
        for slot, (number, width) in enumerate(known):
            begin = sum(jnp.where(number == item, offsets[item], 0) for item in range(item_count))
            for other, other_width in known[:slot]:
                begin = begin + jnp.where(other == number, other_width, 0)
            base[first + slot] = begin
            spare_base[first + slot] = spare - width
            widths[first + slot] = width
            numbers[first + slot] = number
            spare = spare + ROWW - width
        return counts, offsets

    def one_unit(unit, lens):
        source, half = unit_source(unit, me, chips)
        rows = [(half * HALF + slot) * cycle_size + source for slot in range(HALF)]
        counts, offsets = sort(
            rows, 16, tab.ubase, tab.uspare, tab.uwidth, tab.uitem, unit * HALF
        )
        for item in range(items):
            tab.koff[unit * items + item] = offsets[item] + unit * unit_size
            tab.kcnt[unit * items + item] = counts[item]
        return tuple(length + up(count, 16) for length, count in zip(lens, counts))

    lens = lax.fori_loop(0, units, one_unit, (jnp.int32(0),) * items)
    starts = [jnp.int32(0)]
    for item in range(items):
        size = SPARE_KEYS if item == items - 1 else KEYS
        tab.klen[item] = lens[item]
        tab.kstart[item] = starts[item]
        starts.append(starts[item] + up(lens[item], size))
    tab.kstart[items] = starts[items]

    def place_unit(unit, at):
        for item in range(items):
            tab.kdst[unit * items + item] = at[item]
        return tuple(
            spot + up(tab.kcnt[unit * items + item], 16) for item, spot in enumerate(at)
        )

    lax.fori_loop(0, units, place_unit, tuple(starts[:items]))
    for index in range(SLOTS + 2 * REACH):
        row = SLOTS * me - REACH + index
        width, above, below = 0, 0, 0
        for begin, end, item_width in facts:
            inside = (row >= begin) & (row < end)
            width = jnp.where(inside, item_width, width)
            above = jnp.where(inside & (row > begin), 1, above)
            below = jnp.where(inside & (row + 1 < end), 1, below)
        tab.wwidth[index] = width
        tab.wup[index] = above
        tab.wdown[index] = below
        inner = jnp.clip(row, 0, SLOTS * cycle_size - 1)
        slot = lax.div(inner, cycle_size)
        device = inner - slot * cycle_size
        tab.wgroup[index] = (device * SLOTS + slot) * PITCH
        slot = floor_div(row, cycle_size)
        device = row - slot * cycle_size
        turn = slot - first_slot(SLOTS * me - REACH, device, cycle_size)
        tab.wcame[index] = (device * many + turn) * PITCH
    for device in range(cycle_size):
        first = first_slot(SLOTS * device - REACH, me, cycle_size)
        for turn in range(many):
            tab.sent[device * many + turn] = first + turn
        first = first_slot(SLOTS * me, device, cycle_size)
        for turn in range(few):
            tab.back[device * few + turn] = (first + turn) * cycle_size + device - SLOTS * me
    for slot in range(SLOTS):
        row = slot * cycle_size + me
        source = lax.div(row, SLOTS)
        turn = slot - first_slot(source * SLOTS, me, cycle_size)
        tab.came[slot] = (source * few + turn) * PITCH
        for turn in range(3):
            near = jnp.clip(row + turn - 1, 0, SLOTS * cycle_size - 1)
            tab.around[turn * SLOTS + slot] = near * PITCH
    rows = [slot * cycle_size + me for slot in range(SLOTS)]
    counts, offsets = sort(rows, QROWS, tab.qbase, tab.qspare, tab.qwidth, tab.qitem, 0)
    for item in range(items):
        tab.qfirst[item] = lax.div(offsets[item], QROWS)
        tab.qcount[item] = lax.div(counts[item] + (QROWS - 1), QROWS)


def geometry(lengths, cycle_pos, cycle_size, unit_size):
    items = lengths.shape[0] + 1
    units = 2 * cycle_size
    sizes = [units * items] * 3 + [items + 1] + [items] * 3 + [units * HALF] * 4 + [SLOTS] * 4
    sizes += [SLOTS + 2 * REACH] * 5
    many, few = pieces(cycle_size)
    sizes += [cycle_size * many, cycle_size * few, SLOTS, 3 * SLOTS]
    smem = pl.BlockSpec(memory_space=pltpu.SMEM)
    return Tables(
        *pl.pallas_call(
            functools.partial(geometry_kernel, cycle_size, unit_size),
            in_specs=[smem, smem],
            out_specs=[smem] * TABLES,
            out_shape=[jax.ShapeDtypeStruct((size,), jnp.int32) for size in sizes],
            name="geometry",
        )(lengths, cycle_pos.reshape(1))
    )


def places(base, spare, width, first, slots):
    token = lax.broadcasted_iota(jnp.int32, (1, slots * ROWW), 1)
    place = jnp.zeros_like(token)
    for slot in range(slots):
        column = token - slot * ROWW
        here = jnp.where(column < width[first + slot], base[first + slot], spare[first + slot])
        place = jnp.where((column >= 0) & (column < ROWW), here + column, place)
    return place


def sorter(place, rows):
    spot = lax.broadcasted_iota(jnp.int32, (rows, place.shape[1]), 0)
    return jnp.where(spot == place, 1.0, 0.0).astype(BF16)


def query_sorter(tab, rows):
    return sorter(places(tab.qbase, tab.qspare, tab.qwidth, 0, SLOTS), rows)


def with_dataset(values, width, item, first, ids, table_ref):
    column = lax.broadcasted_iota(jnp.int32, (ROWW, 1), 0)
    parts = []
    for slot in range(values.shape[0] // ROWW):
        number = jnp.minimum(item[first + slot], ids.shape[0] - 1)
        added = table_ref[pl.ds(ids[number], 1), :]
        real = column < width[first + slot]
        parts.append(values[slot * ROWW : (slot + 1) * ROWW] + jnp.where(real, added, 0.0))
    return jnp.concatenate(parts, axis=0)


def layer_norm(hidden, norm_gain, norm_bias):
    centred = hidden - jnp.mean(hidden, axis=-1, keepdims=True)
    variance = jnp.mean(centred * centred, axis=-1, keepdims=True)
    return centred * lax.rsqrt(variance + EPS) * norm_gain + norm_bias


def sort_step_kernel(step, ubase, uspare, uwidth, uitem, ids, *refs):
    mine_ref, other_ref, table_ref, gain_ref, bias_ref, out_ref = refs
    unit_size = out_ref.shape[0] // 4
    count = HALF * ROWW
    for unit in range(4):
        source = (mine_ref, other_ref)[unit // 2]
        first = (4 * step + unit) * HALF
        values = source[unit % 2 * count : (unit % 2 + 1) * count, :].astype(F32)
        values = with_dataset(values, uwidth, uitem, first, ids, table_ref)
        normed = layer_norm(values, gain_ref[...], bias_ref[...]).astype(BF16)
        matrix = sorter(places(ubase, uspare, uwidth, first, HALF), unit_size)
        out_ref[unit * unit_size : (unit + 1) * unit_size, :] = jnp.dot(
            matrix, normed, preferred_element_type=F32
        ).astype(BF16)


def sort_step(step, tab, ids, mine, other, table, gain, bias, unit_size):
    return pl.pallas_call(
        functools.partial(sort_step_kernel, step),
        grid_spec=pltpu.PrefetchScalarGridSpec(
            num_scalar_prefetch=5,
            in_specs=[pl.BlockSpec(memory_space=pltpu.VMEM)] * 5,
            out_specs=pl.BlockSpec(memory_space=pltpu.VMEM),
        ),
        out_shape=jax.ShapeDtypeStruct((4 * unit_size, mine.shape[1]), BF16),
        cost_estimate=cost(3),
        compiler_params=pltpu.CompilerParams(vmem_limit_bytes=VMEM),
        name="sort_step",
    )(tab.ubase, tab.uspare, tab.uwidth, tab.uitem, ids, mine, other, table, gain, bias)


def own_start_kernel(qbase, qspare, qwidth, qitem, ids, *refs):
    tokens_ref, table_ref, gain_ref, bias_ref, weight_ref, start_ref, normed_ref, query_ref = refs
    values = tokens_ref[...].astype(F32)
    values = with_dataset(values, qwidth, qitem, 0, ids, table_ref)
    start_ref[...] = values
    normed = layer_norm(values, gain_ref[...], bias_ref[...]).astype(BF16)
    normed_ref[...] = normed
    matrix = sorter(places(qbase, qspare, qwidth, 0, SLOTS), query_ref.shape[0])
    sorted_norm = jnp.dot(matrix, normed, preferred_element_type=F32).astype(BF16)
    query = jnp.dot(sorted_norm, weight_ref[...], preferred_element_type=F32)
    query_ref[...] = (query * (1.0 / math.sqrt(HEAD))).astype(BF16)


def own_start(tab, ids, tokens, table, gain, bias, weight, query_rows):
    vmem = pl.BlockSpec(memory_space=pltpu.VMEM)
    return pl.pallas_call(
        own_start_kernel,
        grid_spec=pltpu.PrefetchScalarGridSpec(
            num_scalar_prefetch=5, in_specs=[vmem] * 5, out_specs=[vmem] * 3
        ),
        out_shape=[
            jax.ShapeDtypeStruct(tokens.shape, F32),
            jax.ShapeDtypeStruct(tokens.shape, BF16),
            jax.ShapeDtypeStruct((query_rows, tokens.shape[1]), BF16),
        ],
        cost_estimate=cost(5),
        compiler_params=pltpu.CompilerParams(vmem_limit_bytes=VMEM),
        name="own_start",
    )(tab.qbase, tab.qspare, tab.qwidth, tab.qitem, ids, tokens, table, gain, bias, weight)


def query_blocks(first, many, most, body):
    def run(number, none):
        body(first + most * number, most)
        return none

    runs = lax.div(many, most)
    lax.fori_loop(0, runs, run, 0)
    for count in range(1, most):

        @pl.when(many - most * runs == count)
        def _(count=count):
            body(first + most * runs, count)


def for_items(items, klen, body):
    def one(item, none):
        body(item, KEYS, (klen[item] + KEYS - 1) // KEYS)
        return none

    lax.fori_loop(0, items - 1, one, 0)
    last = items - 1
    body(last, SPARE_KEYS, (klen[last] + SPARE_KEYS - 1) // SPARE_KEYS)


def as_column(row):
    return row.T[:, :1]


def attend_kernel(heads, units, items, *refs):
    tab, refs = Tables(*refs[:TABLES]), refs[TABLES:]
    koff, kcnt, kdst, kstart, klen, qfirst, qcount = tab[:7]
    steps = units // 4
    q_ref, wk_ref, wv_ref = refs[:3]
    n_refs, refs = refs[3 : 3 + steps], refs[3 + steps :]
    att_ref, o_ref, lse_ref, ns_ref, bias_ref, ks_ref, vs_ref = refs[:7]
    acc_ref, top_ref, total_ref, matrix = refs[7:]
    stride = n_refs[0].shape[0]
    cols = heads * QROWS
    width = ns_ref.shape[1]
    o_ref[...] = jnp.zeros_like(o_ref)
    lse_ref[...] = jnp.zeros_like(lse_ref)
    used = kstart[items]

    @pl.when(pl.program_id(0) == 0)
    def _():
        matrix[...] = query_sorter(tab, o_ref.shape[0])

        def one_item(item, size, blocks):
            def one_unit(turn, unit, none):
                entry = (4 * turn + unit) * items + item
                count, source, target = kcnt[entry], koff[entry] - turn * stride, kdst[entry]

                def step(part, none):
                    src = pl.ds(pl.multiple_of(source + 64 * part, 16), 64)
                    dst = pl.ds(pl.multiple_of(target + 64 * part, 16), 64)
                    ns_ref[dst, :] = n_refs[turn][src, :]
                    row = lax.broadcasted_iota(jnp.int32, (64, 128), 0) + 64 * part
                    bias_ref[dst, :] = jnp.where(row < count, 0.0, NEG).astype(BF16)
                    return none

                return lax.fori_loop(0, (count + 63) // 64, step, none)

            for turn in range(steps):
                lax.fori_loop(0, 4, functools.partial(one_unit, turn), 0)
            end = kstart[item] + klen[item]

            def clear(part, none):
                tail = pl.ds(pl.multiple_of(end + 64 * part, 16), 64)
                ns_ref[tail, :] = jnp.zeros((64, width), BF16)
                bias_ref[tail, :] = jnp.full((64, 128), NEG, BF16)
                return none

            lax.fori_loop(0, (kstart[item + 1] - end + 63) // 64 + 1, clear, 0)

        for_items(items, klen, one_item)

        def clear(part, none):
            tail = pl.ds(pl.multiple_of(used + 64 * part, 16), 64)
            ns_ref[tail, :] = jnp.zeros((64, width), BF16)
            return none

        lax.fori_loop(0, (ns_ref.shape[0] - used) // 64, clear, 0)

    def project(block, none):
        here = pl.ds(pl.multiple_of(block * ROWS, ROWS), ROWS)
        rows = ns_ref[here, :]
        ks_ref[here, :] = jnp.dot(rows, wk_ref[...], preferred_element_type=F32).astype(BF16)
        vs_ref[here, :] = jnp.dot(rows, wv_ref[...], preferred_element_type=F32).astype(BF16)
        return none

    lax.fori_loop(0, (used + ROWS - 1) // ROWS, project, 0)

    def one_item(item, size, blocks):
        def some_queries(place, count):
            wide = count * cols
            rows = pl.ds(pl.multiple_of(place * QROWS, QROWS), count * QROWS)
            block = q_ref[rows, :]
            queries = jnp.concatenate(
                [spread(block[n * QROWS : (n + 1) * QROWS], heads) for n in range(count)], axis=0
            )
            top, total, acc = top_ref.at[:, :wide], total_ref.at[:, :wide], acc_ref.at[:wide]
            top[...] = jnp.full((8, wide), NEG, F32)
            total[...] = jnp.zeros((8, wide), F32)
            acc[...] = jnp.zeros((wide, heads * HEAD), F32)

            def step(number, none):
                here = pl.ds(pl.multiple_of(kstart[item] + number * size, 16), size)
                scores = lax.dot_general(
                    ks_ref[here, :], queries, NT, preferred_element_type=F32
                ) + lanes(bias_ref[here, :].astype(F32), wide)
                best = jnp.max(jnp.max(scores.reshape(size // 8, 8, wide), axis=0), axis=0)
                old = top[...]
                best = jnp.maximum(old, jnp.broadcast_to(best[None], (8, wide)))
                top[...] = best
                shrink = jnp.exp(old - best)
                weights = jnp.exp(scores - best[:1])
                total[...] = total[...] * shrink + jnp.sum(
                    weights.reshape(size // 8, 8, wide), axis=0
                )
                acc[...] = acc[...] * as_column(shrink) + lax.dot_general(
                    weights.astype(BF16),
                    vs_ref[here, :],
                    (((0,), (0,)), ((), ())),
                    preferred_element_type=F32,
                )
                return none

            lax.fori_loop(0, blocks, step, 0)
            summed = jnp.broadcast_to(jnp.sum(total[...], axis=0, keepdims=True), (8, wide))
            lse = top[...] + jnp.log(summed)
            out = acc[...] * as_column(1.0 / summed)
            for n in range(count):
                part = slice(n * cols, (n + 1) * cols)
                lse_ref[pl.ds(place + n, 1), :] = lse[:1, part]
                o_ref[pl.ds(pl.multiple_of((place + n) * QROWS, QROWS), QROWS), :] = gathered(
                    out[part], heads
                )

        query_blocks(qfirst[item], qcount[item], TOGETHER, some_queries)

    for_items(items, klen, one_item)
    att_ref[...] = lax.dot_general(
        matrix[...], o_ref[...].astype(BF16), FLIP, preferred_element_type=F32
    ).astype(BF16)


def attend_back_kernel(heads, units, items, unit_size, me, *refs):
    tab, refs = Tables(*refs[:TABLES]), refs[TABLES:]
    koff, kcnt, kdst, kstart, klen, qfirst, qcount = tab[:7]
    q_ref, grad_ref, o_ref, lse_ref, ks_ref, vs_ref, wk_ref, wv_ref, ns_ref, bias_ref = refs[:10]
    dq_ref, gk_ref, gv_ref, dn_ref = refs[10:14]
    (
        spread_q, spread_do, delta, dq_acc, dk_acc, dv_acc, gk_acc, gv_acc, dn_acc,
        matrix, do_ref, dqs, unit_rows,
    ) = refs[14:]
    feats = heads * HEAD
    cols = heads * QROWS
    flip = FLIP
    dqs[...] = jnp.zeros_like(dqs)
    gk_acc[...] = jnp.zeros_like(gk_acc)
    gv_acc[...] = jnp.zeros_like(gv_acc)
    used = qfirst[items - 1] + qcount[items - 1]

    @pl.when(pl.program_id(0) == 0)
    def _():
        dn_acc[...] = jnp.zeros_like(dn_acc)
        matrix[...] = query_sorter(tab, q_ref.shape[0])

    do_ref[...] = jnp.dot(matrix[...], grad_ref[...], preferred_element_type=F32).astype(BF16)

    def prepare(place, none):
        rows = pl.ds(pl.multiple_of(place * QROWS, QROWS), QROWS)
        grads = do_ref[rows, :]
        spread_q[place] = spread(q_ref[rows, :], heads)
        spread_do[place] = spread(grads, heads)
        product = spread(grads.astype(F32) * o_ref[rows, :], heads)
        delta[place] = lax.dot_general(
            jnp.ones((8, feats), F32), product, NT, precision=HIGH, preferred_element_type=F32
        )
        dq_acc[place] = jnp.zeros((cols, feats), F32)
        return none

    lax.fori_loop(0, used, prepare, 0)

    def one_item(item, size, blocks):
        def one_block(number, none):
            here = pl.ds(pl.multiple_of(kstart[item] + number * size, 16), size)
            dk_acc[:size] = jnp.zeros((size, feats), F32)
            dv_acc[:size] = jnp.zeros((size, feats), F32)

            def some_queries(place, count):
                wide = count * cols
                spot = pl.ds(place, count)
                queries = spread_q[spot].reshape(wide, feats)
                grads = spread_do[spot].reshape(wide, feats)
                row = [lse_ref[pl.ds(place + n, 1), :] for n in range(count)]
                log_total = jnp.concatenate(row, axis=1)
                shift = jnp.concatenate([delta[place + n, :1, :] for n in range(count)], axis=1)
                keys = ks_ref[here, :]
                scores = lax.dot_general(keys, queries, NT, preferred_element_type=F32)
                weights = jnp.exp(scores + lanes(bias_ref[here, :].astype(F32), wide) - log_total)
                slopes = lax.dot_general(vs_ref[here, :], grads, NT, preferred_element_type=F32)
                score_grads = (weights * (slopes - shift)).astype(BF16)
                dv_acc[:size] += jnp.dot(weights.astype(BF16), grads, preferred_element_type=F32)
                dk_acc[:size] += jnp.dot(score_grads, queries, preferred_element_type=F32)
                part = lax.dot_general(score_grads, keys, flip, preferred_element_type=F32)
                dq_acc[spot] += part.reshape(count, cols, feats)

            query_blocks(qfirst[item], qcount[item], TOGETHER_BACK, some_queries)
            dk = dk_acc[:size].astype(BF16)
            dv = dv_acc[:size].astype(BF16)
            dn_acc[here, :] += (
                lax.dot_general(dk, wk_ref[...], NT, preferred_element_type=F32)
                + lax.dot_general(dv, wv_ref[...], NT, preferred_element_type=F32)
            ).astype(dn_acc.dtype)
            rows = ns_ref[here, :]
            gk_acc[...] += lax.dot_general(rows, dk, flip, preferred_element_type=F32)
            gv_acc[...] += lax.dot_general(rows, dv, flip, preferred_element_type=F32)
            return none

        lax.fori_loop(0, jnp.where(qcount[item] > 0, blocks, 0), one_block, 0)

    for_items(items, klen, one_item)

    def finish(place, none):
        rows = pl.ds(pl.multiple_of(place * QROWS, QROWS), QROWS)
        scale = 1.0 / math.sqrt(HEAD)
        dqs[rows, :] = (gathered(dq_acc[place], heads) * scale).astype(BF16)
        return none

    lax.fori_loop(0, used, finish, 0)
    dq_ref[...] = lax.dot_general(
        matrix[...], dqs[...], flip, preferred_element_type=F32
    ).astype(BF16)
    gk_ref[...] = gk_acc[...].astype(BF16)
    gv_ref[...] = gv_acc[...].astype(BF16)

    @pl.when(pl.program_id(0) == pl.num_programs(0) - 1)
    def _():
        unit_rows[...] = jnp.zeros_like(unit_rows)
        count = HALF * ROWW

        def one_unit(unit, none):
            def one_item(item, none):
                entry = unit * items + item
                source, target = koff[entry] - unit * unit_size, kdst[entry]

                def step(part, none):
                    src = pl.ds(pl.multiple_of(source + 64 * part, 16), 64)
                    dst = pl.ds(pl.multiple_of(target + 64 * part, 16), 64)
                    unit_rows[src, :] = dn_acc[dst, :]
                    return none

                return lax.fori_loop(0, (kcnt[entry] + 63) // 64, step, none)

            lax.fori_loop(0, items, one_item, 0)
            place = places(tab.ubase, tab.uspare, tab.uwidth, unit * HALF, HALF)
            source, half = unit_source(unit, me[0], units // 4)
            spot = (2 * source + half) * count
            dn_ref[pl.ds(pl.multiple_of(spot, 16), count), :] = lax.dot_general(
                sorter(place, unit_size), unit_rows[...], flip, preferred_element_type=F32
            ).astype(BF16)
            return none

        lax.fori_loop(0, units, one_unit, 0)


def gelu_parts(values):
    slope = 0.7978845608028654
    bent = jnp.tanh(slope * (values + 0.044715 * values * values * values))
    return bent, slope * (1.0 + 3.0 * 0.044715 * values * values)


def gelu(values):
    return 0.5 * values * (1.0 + gelu_parts(values)[0])


def gelu_slope(values):
    bent, inner = gelu_parts(values)
    return 0.5 * (1.0 + bent) + 0.5 * values * (1.0 - bent * bent) * inner


def merge_kernel(
    cycle_size, wwidth, wup, wdown, wgroup, wcame, back,
    came_ref, group_ref, k11, k12, k21, k22, out_weight, grad_ref, mapped_ref, shares_ref,
    x1, x2, x3, x4, g3, real_ref, up_ref, down_ref, c1, m1, c3, m2g, m1g, win_ref, rows_ref,
):
    window = SLOTS + 2 * REACH
    column = lax.broadcasted_iota(jnp.int32, (PITCH, 128), 0)
    for row in range(window):
        spots = pl.ds(row * PITCH, PITCH)
        win_ref[spots, :CH] = came_ref[pl.ds(pl.multiple_of(wcame[row], 16), PITCH), :]
        win_ref[spots, CH:] = group_ref[pl.ds(pl.multiple_of(wgroup[row], 16), PITCH), :]
        real = jnp.where(column < wwidth[row], 1.0, 0.0)
        real_ref[spots, :] = real
        up_ref[spots, :] = real * wup[row].astype(F32)
        down_ref[spots, :] = real * wdown[row].astype(F32)

    def at(low, high):
        return slice(low * PITCH, high * PITCH)

    def masked(ref, values, low, high):
        return values * lanes(ref[at(low, high), :], CH)

    def fill(taps, values, low, high):
        spots = at(low + 1, high + 1)
        size = values.shape[0]
        taps[spots, :CH] = pltpu.roll(values, 1, 0).astype(BF16)
        taps[spots, CH : 2 * CH] = values.astype(BF16)
        taps[spots, 2 * CH :] = pltpu.roll(values, size - 1, 0).astype(BF16)

    def conv(taps, kernel, low, high):
        def part(row_step):
            rows = taps[at(low + 1 + row_step, high + 1 + row_step), :]
            first = (row_step + 1) * 3 * CH
            return jnp.dot(rows, kernel[first : first + 3 * CH, :], preferred_element_type=F32)

        total = masked(real_ref, part(0), low, high)
        total = total + masked(up_ref, part(-1), low, high)
        return total + masked(down_ref, part(1), low, high)

    def conv_back(kernel, low, high):
        def part(row_step):
            rows = at(low + 1 + row_step, high + 1 + row_step)
            total = None
            for col_step in (-1, 0, 1):
                first = (8 - (3 * (row_step + 1) + col_step + 1)) * CH
                side = (col_step + 1) * CH
                now = lax.dot_general(
                    g3[rows, side : side + CH],
                    kernel[first : first + CH, :],
                    NT,
                    preferred_element_type=F32,
                )
                total = now if total is None else total + now
            return total

        total = masked(real_ref, part(0), low, high)
        total = total + masked(up_ref, part(-1), low, high)
        return total + masked(down_ref, part(1), low, high)

    own, last = REACH, REACH + SLOTS
    unit_share = 9 * CH // cycle_size
    out_share = CH // cycle_size
    share_rows = 4 * unit_share + out_share

    def weight_grad(taps, gradient, tensor):
        piece = math.gcd(3 * CH, unit_share)
        for row_step, mask in ((-1, up_ref), (0, real_ref), (1, down_ref)):
            now = masked(mask, gradient, own, last).astype(BF16)
            rows = taps[at(own + 1 + row_step, last + 1 + row_step), :]
            block = lax.dot_general(rows, now, FLIP, preferred_element_type=F32).astype(BF16)
            for part in range(3 * CH // piece):
                spot = (row_step + 1) * 3 * CH + part * piece
                share, offset = divmod(spot, unit_share)
                first = share * share_rows + tensor * unit_share + offset
                shares_ref[first : first + piece, :] = block[part * piece : (part + 1) * piece]

    def start(low, high):
        return win_ref[at(low, high), :CH].astype(F32)

    fill(x1, masked(real_ref, gelu(start(0, 24)), 0, 24), 0, 24)
    c1[at(1, 23), :] = conv(x1, k11, 1, 23)
    fill(x2, masked(real_ref, gelu(c1[at(1, 23), :]), 1, 23), 1, 23)
    m1[at(2, 22), :] = start(2, 22) + conv(x2, k12, 2, 22)
    fill(x3, masked(real_ref, gelu(m1[at(2, 22), :]), 2, 22), 2, 22)
    c3[at(3, 21), :] = conv(x3, k21, 3, 21)
    fill(x4, masked(real_ref, gelu(c3[at(3, 21), :]), 3, 21), 3, 21)
    merged = (m1[at(own, last), :] + conv(x4, k22, own, last)).astype(BF16)

    def send(values, ref):
        rows_ref[...] = values
        for piece in range(back.shape[0]):
            row = jnp.minimum(back[piece], SLOTS - 1)
            block = rows_ref[pl.ds(pl.multiple_of(row * PITCH, PITCH), PITCH), :]
            ref[piece * PITCH : (piece + 1) * PITCH, :] = block.astype(BF16)

    mapped_ref[...] = jnp.dot(merged, out_weight[...], preferred_element_type=F32).astype(BF16)
    block = lax.dot_general(
        merged, win_ref[at(own, last), CH:], FLIP, preferred_element_type=F32
    ).astype(BF16)
    for share in range(cycle_size):
        first = share * share_rows + 4 * unit_share
        shares_ref[first : first + out_share, :] = block[share * out_share : (share + 1) * out_share]

    m2g[at(2, 22), :] = lax.dot_general(
        win_ref[at(2, 22), CH:], out_weight[...], NT, preferred_element_type=F32
    )
    fill(g3, masked(real_ref, m2g[at(2, 22), :], 2, 22), 2, 22)
    weight_grad(x4, m2g[at(own, last), :], 3)
    now = gelu_slope(c3[at(3, 21), :]) * conv_back(k22, 3, 21)
    fill(g3, now, 3, 21)
    weight_grad(x3, now[at(own - 3, last - 3)], 2)
    m1g[at(4, 20), :] = m2g[at(4, 20), :] + gelu_slope(m1[at(4, 20), :]) * conv_back(k21, 4, 20)
    fill(g3, masked(real_ref, m1g[at(4, 20), :], 4, 20), 4, 20)
    weight_grad(x2, m1g[at(own, last), :], 1)
    now = gelu_slope(c1[at(5, 19), :]) * conv_back(k12, 5, 19)
    fill(g3, now, 5, 19)
    weight_grad(x1, now[at(own - 5, last - 5)], 0)
    now = gelu_slope(start(own, last)) * conv_back(k11, own, last)
    send(m1g[at(own, last), :] + now, grad_ref)


def pack_kernel(sent, block_ref, weight_ref, out_ref, rows_ref):
    rows_ref[...] = jnp.dot(block_ref[...], weight_ref[...], preferred_element_type=F32)
    blank = jnp.zeros((PITCH - ROWW, CH), F32)
    for piece in range(sent.shape[0]):
        slot = jnp.clip(sent[piece], 0, SLOTS - 1)
        block = rows_ref[pl.ds(pl.multiple_of(slot * ROWW, 8), ROWW), :]
        out_ref[piece * PITCH : (piece + 1) * PITCH, :] = jnp.concatenate(
            [block, blank], axis=0
        ).astype(BF16)


def pack(tab, block_out, weight):
    vmem = pl.BlockSpec(memory_space=pltpu.VMEM)
    return pl.pallas_call(
        pack_kernel,
        grid_spec=pltpu.PrefetchScalarGridSpec(
            num_scalar_prefetch=1,
            in_specs=[vmem] * 2,
            out_specs=vmem,
            scratch_shapes=[pltpu.VMEM((block_out.shape[0], CH), F32)],
        ),
        out_shape=jax.ShapeDtypeStruct((tab.sent.shape[0] * PITCH, CH), BF16),
        cost_estimate=cost(2),
        compiler_params=pltpu.CompilerParams(vmem_limit_bytes=VMEM),
        name="pack",
    )(tab.sent, block_out, weight)


def unpack_kernel(came, rows_ref, out_ref):
    parts = []
    for slot in range(came.shape[0]):
        block = rows_ref[pl.ds(pl.multiple_of(came[slot], 16), PITCH), :].astype(F32)
        parts.append(block[:ROWW])
    out_ref[...] = jnp.concatenate(parts, axis=0).astype(BF16)


def unpack(came, rows):
    vmem = pl.BlockSpec(memory_space=pltpu.VMEM)
    return pl.pallas_call(
        unpack_kernel,
        grid_spec=pltpu.PrefetchScalarGridSpec(
            num_scalar_prefetch=1, in_specs=[vmem], out_specs=vmem
        ),
        out_shape=jax.ShapeDtypeStruct((came.shape[0] * ROWW, CH), BF16),
        cost_estimate=cost(1),
        compiler_params=pltpu.CompilerParams(vmem_limit_bytes=VMEM),
        name="unpack",
    )(came, rows)


def merge(tab, came, group, kernels, out_weight, cycle_size):
    window = SLOTS + 2 * REACH
    vmem = pl.BlockSpec(memory_space=pltpu.VMEM)
    padded = (window + 2) * PITCH
    share_rows = 4 * (9 * CH // cycle_size) + CH // cycle_size
    small = pltpu.VMEM((window * PITCH, 128), F32)
    large = pltpu.VMEM((window * PITCH, CH), F32)
    return pl.pallas_call(
        functools.partial(merge_kernel, cycle_size),
        grid_spec=pltpu.PrefetchScalarGridSpec(
            num_scalar_prefetch=6,
            in_specs=[vmem] * 7,
            out_specs=[vmem] * 3,
            scratch_shapes=[pltpu.VMEM((padded, 3 * CH), BF16)] * 5
            + [small] * 3
            + [large] * 5
            + [
                pltpu.VMEM((window * PITCH, 2 * CH), BF16),
                pltpu.VMEM((SLOTS * PITCH, CH), F32),
            ],
        ),
        out_shape=[
            jax.ShapeDtypeStruct((tab.back.shape[0] * PITCH, CH), BF16),
            jax.ShapeDtypeStruct((SLOTS * PITCH, CH), BF16),
            jax.ShapeDtypeStruct((cycle_size * share_rows, CH), BF16),
        ],
        cost_estimate=cost(25),
        compiler_params=pltpu.CompilerParams(vmem_limit_bytes=VMEM),
        name="merge",
    )(
        tab.wwidth, tab.wup, tab.wdown, tab.wgroup, tab.wcame, tab.back,
        came, group, *kernels, out_weight,
    )


def attend(tab, query, key_weight, value_weight, norms, sorted_keys, units, items, heads):
    feats = heads * HEAD
    cols = heads * QROWS
    width = query.shape[1]
    groups = width // feats
    blocks8 = (query.shape[0] // QROWS + 7) // 8 * 8
    once = pl.Buffered(1) if units > 16 else None

    def part(rows, columns=feats):
        return pl.BlockSpec((rows, columns), lambda group, *_: (0, group), pipeline_mode=once)

    def whole(rows, columns):
        return pl.BlockSpec(
            (rows, columns), lambda group, *_: (0, 0), pipeline_mode=pl.Buffered(1)
        )

    return pl.pallas_call(
        functools.partial(attend_kernel, heads, units, items),
        grid_spec=pltpu.PrefetchScalarGridSpec(
            num_scalar_prefetch=TABLES,
            grid=(groups,),
            in_specs=[part(query.shape[0]), part(width), part(width)]
            + [whole(*norm.shape) for norm in norms],
            out_specs=[
                part(SLOTS * ROWW),
                part(query.shape[0]),
                part(blocks8, cols),
                whole(sorted_keys, width),
                whole(sorted_keys, 128),
                part(sorted_keys),
                part(sorted_keys),
            ],
            scratch_shapes=[
                pltpu.VMEM((TOGETHER * cols, feats), F32),
                pltpu.VMEM((8, TOGETHER * cols), F32),
                pltpu.VMEM((8, TOGETHER * cols), F32),
                pltpu.VMEM((query.shape[0], SLOTS * ROWW), BF16),
            ],
        ),
        out_shape=[
            jax.ShapeDtypeStruct((SLOTS * ROWW, width), BF16),
            jax.ShapeDtypeStruct(query.shape, F32),
            jax.ShapeDtypeStruct((blocks8, groups * cols), F32),
            jax.ShapeDtypeStruct((sorted_keys, width), BF16),
            jax.ShapeDtypeStruct((sorted_keys, 128), BF16),
            jax.ShapeDtypeStruct((sorted_keys, width), BF16),
            jax.ShapeDtypeStruct((sorted_keys, width), BF16),
        ],
        cost_estimate=cost(70),
        compiler_params=pltpu.CompilerParams(vmem_limit_bytes=VMEM),
        name="attend",
    )(*tab, query, key_weight, value_weight, *norms)


def attend_back(
    tab, cycle_pos, query, grads, outputs, lse, ks, vs, key_weight, value_weight, ns, bias,
    unit_size, units, items, heads,
):
    feats = heads * HEAD
    cols = heads * QROWS
    rows, width = query.shape
    groups = width // feats
    blocks = rows // QROWS
    once = pl.Buffered(1) if units > 16 else None

    def part(rows, columns=feats):
        return pl.BlockSpec((rows, columns), lambda group, *_: (0, group), pipeline_mode=once)

    def whole(rows, columns):
        return pl.BlockSpec(
            (rows, columns), lambda group, *_: (0, 0), pipeline_mode=pl.Buffered(1)
        )

    return pl.pallas_call(
        functools.partial(attend_back_kernel, heads, units, items, unit_size),
        grid_spec=pltpu.PrefetchScalarGridSpec(
            num_scalar_prefetch=TABLES + 1,
            grid=(groups,),
            in_specs=[
                part(rows),
                part(grads.shape[0]),
                part(rows),
                part(lse.shape[0], cols),
                part(ks.shape[0]),
                part(ks.shape[0]),
                part(width),
                part(width),
                whole(*ns.shape),
                whole(*bias.shape),
            ],
            out_specs=[
                part(grads.shape[0]),
                part(width),
                part(width),
                whole(units * HALF * ROWW, width),
            ],
            scratch_shapes=[
                pltpu.VMEM((blocks, cols, feats), BF16),
                pltpu.VMEM((blocks, cols, feats), BF16),
                pltpu.VMEM((blocks, 8, cols), F32),
                pltpu.VMEM((blocks, cols, feats), F32),
                pltpu.VMEM((SPARE_KEYS, feats), F32),
                pltpu.VMEM((SPARE_KEYS, feats), F32),
                pltpu.VMEM((width, feats), F32),
                pltpu.VMEM((width, feats), F32),
                pltpu.VMEM(ns.shape, BF16),
                pltpu.VMEM((rows, grads.shape[0]), BF16),
                pltpu.VMEM((rows, feats), BF16),
                pltpu.VMEM((rows, feats), BF16),
                pltpu.VMEM((unit_size, width), BF16),
            ],
        ),
        out_shape=[
            jax.ShapeDtypeStruct(grads.shape, BF16),
            jax.ShapeDtypeStruct((width, width), BF16),
            jax.ShapeDtypeStruct((width, width), BF16),
            jax.ShapeDtypeStruct((units * HALF * ROWW, width), BF16),
        ],
        cost_estimate=cost(90),
        compiler_params=pltpu.CompilerParams(vmem_limit_bytes=VMEM),
        name="attend_back",
    )(cycle_pos.reshape(1), *tab, query, grads, outputs, lse, ks, vs, key_weight, value_weight, ns, bias)


@functools.cache
def most_rows(cycle_size, item_count):
    rows = np.arange(SLOTS)[:, None] * cycle_size + np.arange(cycle_size)
    most_keys = most_unit = most_queries = 0
    lists = [()]
    while lists:
        heights = lists.pop()
        if len(heights) < item_count:
            for height in (24, 30):
                if sum(heights) + height <= SLOTS * cycle_size:
                    lists.append(heights + (height,))
        if not heights:
            continue
        ends = np.cumsum(heights)
        number = np.searchsorted(ends, rows, side="right")
        wide = np.array([24 if height == 24 else ROWW for height in heights] + [0])[number]
        kinds = np.arange(len(heights))
        counts = [((number == kind) * wide) for kind in kinds] + [ROWW - wide]
        counts = np.stack(counts)

        def rounded(values, align):
            return -(-values // align) * align

        units = rounded(counts.reshape(len(counts), 2, HALF, cycle_size).sum(2), 16)
        most_unit = max(most_unit, units.sum(0).max())
        keys = units.sum((1, 2))
        keys = rounded(keys[:-1], KEYS).sum() + rounded(keys[-1], SPARE_KEYS)
        most_keys = max(most_keys, keys)
        most_queries = max(most_queries, rounded(counts.sum(1), QROWS).sum(0).max())
    return int(most_keys), int(most_unit), int(most_queries)


def passed(value, axis, target):
    pairs = [(source, target(source)) for source in range(lax.axis_size(axis))]
    return lax.ppermute(value, axis, pairs)


def passed_along(value, axis, steps):
    count = lax.axis_size(axis)
    return passed(value, axis, lambda source: (source + steps) % count)


def tied(*values):
    return lax.optimization_barrier(values)


def to_sibling(value):
    return passed(value, "blk", lambda source: source ^ 1)


def gelu_tanh(values):
    return (
        0.5
        * values
        * (1.0 + jnp.tanh(0.7978845608028654 * (values + 0.044715 * values * values * values)))
    )


def gelu_back(values, gradient):
    return jax.vjp(gelu_tanh, values)[1](gradient)[0]


def item_facts(lengths):
    facts, start = [], 0
    for item in range(lengths.shape[0]):
        length = lengths[item]
        height = jnp.where(length == 1200, 30, jnp.where(length == 576, 24, 0))
        width = jnp.where(length == 1200, 40, 24)
        facts.append((start, start + height, height, width))
        start = start + height
    return facts


def row_facts(facts, rows):
    number = jnp.full_like(rows, len(facts))
    local, height, width = rows, jnp.zeros_like(rows), jnp.zeros_like(rows)
    for item, (start, end, item_height, item_width) in enumerate(facts):
        inside = (rows >= start) & (rows < end)
        number = jnp.where(inside, item, number)
        local = jnp.where(inside, rows - start, local)
        height = jnp.where(inside, item_height, height)
        width = jnp.where(inside, item_width, width)
    return number, local, height, width


def tap_masks(local_row, height, width):
    column = lax.broadcasted_iota(jnp.int32, (1, ROWW), 1)
    is_real = column < width
    all_masks = []
    for row_step in (-1, 0, 1):
        rows_fine = (local_row + row_step >= 0) & (local_row + row_step < height)
        for col_step in (-1, 0, 1):
            cols_fine = (column + col_step >= 0) & (column + col_step < width)
            all_masks.append(is_real & rows_fine & cols_fine)
    return is_real, all_masks


def side_shift(values, col_step):
    if col_step == 0:
        return values
    empty_col = jnp.zeros_like(values[:, :1])
    if col_step < 0:
        return jnp.concatenate([empty_col, values[:, :-1]], axis=1)
    return jnp.concatenate([values[:, 1:], empty_col], axis=1)


def from_above(values, cycle_pos):
    got = passed_along(values, "blk", 1)
    empty_row = jnp.zeros_like(values[:1])
    return jnp.where(cycle_pos == 0, jnp.concatenate([empty_row, got[:-1]], axis=0), got)


def from_below(values, cycle_pos, cycle_size):
    got = passed_along(values, "blk", -1)
    empty_row = jnp.zeros_like(values[:1])
    return jnp.where(
        cycle_pos == cycle_size - 1, jnp.concatenate([got[1:], empty_row], axis=0), got
    )


def upsample_forward(row_above, values, row_below, all_masks):
    center = values.astype(F32)
    upper_value = jnp.where(all_masks[1][:, :, None], row_above, values).astype(F32)
    lower_value = jnp.where(all_masks[7][:, :, None], row_below, values).astype(F32)
    pieces = []
    for half_rows in (0.75 * center + 0.25 * upper_value, 0.75 * center + 0.25 * lower_value):
        left_value = jnp.where(all_masks[3][:, :, None], side_shift(half_rows, -1), half_rows)
        right_value = jnp.where(all_masks[5][:, :, None], side_shift(half_rows, 1), half_rows)
        pieces.append(0.75 * half_rows + 0.25 * left_value)
        pieces.append(0.75 * half_rows + 0.25 * right_value)
    joined = jnp.concatenate(pieces, axis=2)
    return joined.reshape(-1, joined.shape[2])


def upsample_back_columns(gradient, all_masks):
    channels = gradient.shape[2] // 4
    left_fine = all_masks[3][:, :, None]
    right_fine = all_masks[5][:, :, None]
    halves = []
    for half in (0, 1):
        left_part = gradient[:, :, 2 * half * channels : (2 * half + 1) * channels].astype(F32)
        right_part = gradient[:, :, (2 * half + 1) * channels : (2 * half + 2) * channels].astype(
            F32
        )
        side = jnp.where(right_fine, side_shift(left_part, 1), 0.0)
        side = side + jnp.where(left_fine, 0.0, left_part)
        side = side + jnp.where(left_fine, side_shift(right_part, -1), 0.0)
        side = side + jnp.where(right_fine, 0.0, right_part)
        halves.append(0.75 * (left_part + right_part) + 0.25 * side)
    return [half.astype(BF16) for half in halves]


def upsample_back_rows(upper, lower, upper_next, lower_prev, all_masks):
    up_fine = all_masks[1][:, :, None]
    down_fine = all_masks[7][:, :, None]
    rows = jnp.where(down_fine, upper_next, lower).astype(F32)
    rows = rows + jnp.where(up_fine, lower_prev, upper).astype(F32)
    return 0.75 * (upper.astype(F32) + lower.astype(F32)) + 0.25 * rows


def dot32(left, right, **more):
    return jnp.dot(left, right, preferred_element_type=F32, **more)


def dot_t(left, right):
    return lax.dot_general(left, right, NT, preferred_element_type=F32)


def t_dot(left, right):
    return lax.dot_general(left, right, (((0,), (0,)), ((), ())), preferred_element_type=F32)


def halving(values, device, bit, axis, pairs_axis):
    half = values.shape[axis] // 2
    mine = (device >> bit) & 1
    keep = lax.dynamic_slice_in_dim(values, mine * half, half, axis=axis)
    send = lax.dynamic_slice_in_dim(values, (1 - mine) * half, half, axis=axis)
    return keep, passed(send, pairs_axis, lambda source: source ^ (1 << bit))


def summed(keep, got):
    return (keep.astype(F32) + got.astype(F32)).astype(BF16)


def core_summed(shares, core):
    cycle_size, rows, width = shares.shape
    paired = shares.reshape(cycle_size // 2, 2, rows, width)
    keep = lax.dynamic_index_in_dim(paired, core, 1, keepdims=False)
    send = lax.dynamic_index_in_dim(paired, 1 - core, 1, keepdims=False)
    return (keep.astype(F32) + to_sibling(send).astype(F32)).astype(BF16)


class ChipSums:
    def __init__(self, values, chip):
        half = values.shape[1] // 2
        self.chip, self.chips = chip, values.shape[0]
        self.parts = [(values[:, :half], 1), (values[:, half:], -1)]
        self.moving = [self.block(part, way, 1).astype(BF16) for part, way in self.parts]

    def block(self, part, way, offset):
        spot = (self.chip - way * offset) % self.chips
        return lax.dynamic_index_in_dim(part, spot, 0, keepdims=False).astype(F32)

    def step(self, number):
        moved = []
        for value, (part, way) in zip(self.moving, self.parts):
            got = passed_along(value, "blk", 2 * way).astype(F32)
            moved.append((got + self.block(part, way, number + 1)).astype(BF16))
        self.moving = moved

    def result(self):
        return jnp.concatenate(self.moving, axis=0)


class GroupGather:
    def __init__(self, values, dp_pos):
        self.dp_pos, self.bits = dp_pos, lax.axis_size("dp").bit_length() - 1
        half = values.shape[0] // 2
        self.held = [part[(None,) * self.bits] for part in (values[:half], values[half:])]

    def step(self, number):
        held = []
        for value, bit in zip(self.held, (number, self.bits - 1 - number)):
            axis = self.bits - 1 - bit
            got = passed(value, "dp", lambda source, bit=bit: source ^ (1 << bit))
            mine = (self.dp_pos >> bit) & 1
            held.append(
                jnp.where(
                    mine == 0,
                    jnp.concatenate([value, got], axis=axis),
                    jnp.concatenate([got, value], axis=axis),
                )
            )
        self.held = held

    def result(self):
        shape = (1 << self.bits,)
        return jnp.concatenate(
            [value.reshape(shape + value.shape[self.bits :]) for value in self.held], axis=1
        )


def gathered_over_groups(values, dp_pos):
    gather = GroupGather(values, dp_pos)
    for number in range(gather.bits):
        gather.step(number)
    return gather.result()


def over_groups(values, bit):
    got = passed(values, "dp", lambda source: source ^ (1 << bit))
    return (values.astype(F32) + got.astype(F32)).astype(BF16)


def sum_over_chips(values, chip):
    chips = values.shape[0]
    total = lax.dynamic_index_in_dim(values, chip, 0, keepdims=False).astype(F32)
    for step in range(1, chips):
        send = lax.dynamic_index_in_dim(values, (chip + step) % chips, 0, keepdims=False)
        total = total + passed_along(send, "blk", 2 * step).astype(F32)
    return total


def whole_shares(whole, parts, orders):
    groups = whole.shape[0]
    bits = groups.bit_length() - 1
    out, place = [], 0
    for part, order in zip(parts, orders):
        rows, width = part.shape[1:]
        size = rows * width // 256
        pieces = []
        for turn in range(groups):
            device = sum(((turn >> (bits - 1 - index)) & 1) << bit for index, bit in enumerate(order))
            pieces.append(whole[device, place : place + size].reshape(rows, width))
        out.append(jnp.concatenate(pieces, axis=0).astype(F32))
        place += size
    return out


def shards(
    tokens,
    item_lengths,
    dataset_ids,
    dataset_table,
    norm1_gain,
    norm1_bias,
    query_weight,
    key_weight,
    value_weight,
    out_weight,
    norm2_gain,
    norm2_bias,
    fc1_weight,
    fc2_weight,
    project_weight,
    unit1_first,
    unit1_second,
    unit2_first,
    unit2_second,
    output_weight,
    block_cotangent,
    merged_cotangent,
):
    cycle_size = lax.axis_size("blk")
    cycle_pos = lax.axis_index("blk")
    chips = cycle_size // 2
    chip, core = cycle_pos // 2, cycle_pos % 2
    lengths = item_lengths[0]
    item_count = lengths.shape[0]
    kinds = item_count + 1
    width_model = tokens.shape[1]
    heads = 4 if cycle_size <= 8 else 2
    half_tokens = HALF * ROWW
    token_count = tokens.shape[0]

    facts = item_facts(lengths)
    own_rows = lax.broadcasted_iota(jnp.int32, (SLOTS, 1), 0) * cycle_size + cycle_pos
    number, local_row, height, width = row_facts(facts, own_rows)
    is_real, all_masks = tap_masks(local_row, height, width)
    units = 4 * chips
    most_keys, most_unit, query_rows = most_rows(cycle_size, item_count)
    unit_size = most_unit + 48
    sorted_keys = (most_keys + 128 + ROWS - 1) // ROWS * ROWS
    tab = geometry(lengths, cycle_pos, cycle_size, unit_size)
    ids = dataset_ids[0]
    gain_one, bias_one = norm1_gain.reshape(1, -1), norm1_bias.reshape(1, -1)

    stream_start, normed_one, query = own_start(
        tab, ids, tokens, dataset_table, gain_one, bias_one, query_weight, query_rows
    )
    ahead, behind = tokens[:half_tokens], tokens[half_tokens:]
    sorted_norms = []
    for step in range(chips):
        if step:
            ahead = passed_along(ahead, "blk", 2)
            behind = passed_along(behind, "blk", -2)
            ahead, behind, sorted_norms[-1] = tied(ahead, behind, sorted_norms[-1])
        if step == 1:
            ahead, behind, stream_start, normed_one, query = tied(
                ahead, behind, stream_start, normed_one, query
            )
            ahead, behind, merged_cotangent = tied(ahead, behind, merged_cotangent)
            upper, lower = upsample_back_columns(
                merged_cotangent.reshape(SLOTS, ROWW, -1), all_masks
            )
        if step == 2:
            ahead, behind, upper, lower = tied(ahead, behind, upper, lower)
            upper_next = from_below(upper, cycle_pos, cycle_size)
            lower_prev = from_above(lower, cycle_pos)
        if step == chips - 1:
            ahead, behind, upper_next, lower_prev = tied(ahead, behind, upper_next, lower_prev)
            mapped_grad = upsample_back_rows(
                upper, lower, upper_next, lower_prev, all_masks
            ).astype(BF16)
            mapped_grad = jnp.pad(mapped_grad, ((0, 0), (0, PITCH - ROWW), (0, 0)))
            mapped_grad = mapped_grad.reshape(SLOTS * PITCH, -1)
        mine = jnp.concatenate([ahead, behind], axis=0)
        sorted_norms.append(
            sort_step(
                step, tab, ids, mine, to_sibling(mine), dataset_table, gain_one, bias_one, unit_size
            )
        )
    sorted_norms[-1], mapped_grad = tied(sorted_norms[-1], mapped_grad)
    group_grad = lax.all_gather(mapped_grad, "blk", tiled=True)
    attended, outputs, lse, sorted_norm, bias, ks, vs = attend(
        tab, query, key_weight, value_weight, sorted_norms, sorted_keys, units, kinds, heads
    )
    attended, group_grad = tied(attended, group_grad)

    def as_cells(flattened):
        return flattened.reshape(SLOTS, ROWW, flattened.shape[-1])

    after_attn = stream_start + dot32(attended, out_weight)
    normed_two = layer_norm(after_attn, norm2_gain, norm2_bias).astype(BF16)
    pre_act = dot32(normed_two, fc1_weight)
    hidden = gelu_tanh(pre_act).astype(BF16)
    block_out = (after_attn + dot32(hidden, fc2_weight)).astype(BF16)
    channels = project_weight.shape[1]

    def exchanged(values):
        values = values.reshape(cycle_size, -1, channels)
        return lax.all_to_all(values, "blk", 0, 0).reshape(-1, channels)

    grad_rows, mapped_rows, conv_shares = merge(
        tab,
        exchanged(pack(tab, block_out, project_weight)),
        group_grad,
        (unit1_first, unit1_second, unit2_first, unit2_second),
        output_weight,
        cycle_size,
    )
    conv_shares = conv_shares.reshape(cycle_size, -1, channels)
    group_mapped = lax.all_gather(mapped_rows, "blk", tiled=True)
    reassembled_grad = unpack(tab.came, exchanged(grad_rows))

    def shared_out(*gradients):
        parts = []
        for gradient in gradients:
            parts.append(gradient.astype(BF16).reshape(cycle_size, -1, gradient.shape[-1]))
        return jnp.concatenate(parts, axis=1) if len(parts) > 1 else parts[0]

    dp_pos = lax.axis_index("dp")
    groups = lax.axis_size("dp")
    bits = groups.bit_length() - 1
    one_way = list(range(bits))
    other_way = one_way[::-1]

    def wide(gradient):
        return gradient.reshape(cycle_size, -1, width_model)

    def scattering(shares):
        count, share_rows, share_width = shares.shape
        parts = shares.reshape(count, groups, share_rows // groups, share_width)
        return jnp.swapaxes(parts, 0, 1).reshape(-1, share_width)

    def scattered(parts):
        return lax.psum_scatter(parts, "dp", scatter_dimension=0, tiled=True)

    def dp_halving(values, order, index):
        return halving(values, dp_pos, order[index], 1, "dp")

    def dp_halved(values, order, index):
        return summed(*dp_halving(values, order, index))

    project_grad = t_dot(block_out, reassembled_grad)
    block_grad = block_cotangent.astype(F32) + dot_t(reassembled_grad, project_weight)
    mlp_grad = block_grad.astype(BF16)
    fc2_parts = scattering(shared_out(t_dot(hidden, mlp_grad)))
    mlp_grad, fc2_parts = tied(mlp_grad, fc2_parts)
    fc2_sums = scattered(fc2_parts)
    conv_sums = core_summed(conv_shares, core)
    pre_grad = gelu_back(pre_act, dot_t(mlp_grad, fc2_weight)).astype(BF16)
    fc1_grad = t_dot(normed_two, pre_grad)
    normed_two_grad = dot_t(pre_grad, fc1_weight)
    norm_two_pull = jax.vjp(layer_norm, after_attn, norm2_gain, norm2_bias)[1]
    attn_side, norm2_gain_grad, norm2_bias_grad = norm_two_pull(normed_two_grad)
    after_grad = block_grad + attn_side
    branch_grad = after_grad.astype(BF16)
    out_proj_grad = t_dot(attended, branch_grad)
    attended_grad = dot_t(branch_grad, out_weight).astype(BF16)

    rows = width_model // cycle_size
    rows = width_model // cycle_size
    fc1_sums = core_summed(shared_out(fc1_grad), core)
    out_sums = core_summed(shared_out(out_proj_grad, wide(project_grad)), core)
    attended_grad, conv_sums, fc1_sums, out_sums, fc2_sums = tied(
        attended_grad, conv_sums, fc1_sums, out_sums, fc2_sums
    )
    conv_sums, conv_got = dp_halving(conv_sums, one_way, 0)
    fc1_sums, fc1_got = dp_halving(fc1_sums, other_way, 0)
    out_sums, out_got = dp_halving(out_sums, one_way, 0)
    fc2_sums = lax.psum_scatter(fc2_sums, "blk", scatter_dimension=0, tiled=True)
    query_low, key_grad, value_grad, token_grad = attend_back(
        tab, cycle_pos, query, attended_grad, outputs, lse, ks, vs, key_weight, value_weight, sorted_norm,
        bias, unit_size, units, kinds, heads,
    )
    query_low, key_grad, value_grad, token_grad, conv_got, fc1_got, out_got, fc2_sums = tied(
        query_low, key_grad, value_grad, token_grad, conv_got, fc1_got, out_got, fc2_sums
    )
    normed_one_grad = lax.psum_scatter(token_grad, "blk", scatter_dimension=0, tiled=True)
    conv_sums = summed(conv_sums, conv_got)
    fc1_sums = summed(fc1_sums, fc1_got)
    out_sums = summed(out_sums, out_got)
    query_grad = t_dot(normed_one, query_low)
    key_sums = core_summed(shared_out(key_grad, value_grad), core)
    query_sums = core_summed(shared_out(query_grad), core)

    for index in range(bits):
        if index:
            conv_sums = dp_halved(conv_sums, one_way, index)
            fc1_sums = dp_halved(fc1_sums, other_way, index)
            out_sums = dp_halved(out_sums, one_way, index)
        key_sums = dp_halved(key_sums, one_way, index)
        query_sums = dp_halved(query_sums, other_way, index)
    late = [conv_sums, fc1_sums, out_sums, key_sums, query_sums]
    late_orders = [one_way, other_way, one_way, one_way, other_way]
    chip_sums = ChipSums(
        jnp.concatenate([part.reshape(chips, -1, 256) for part in late], axis=1), chip
    )
    for turn in range(1, chips):
        chip_sums.step(turn)
    around = unpack(tab.around, group_mapped).reshape(3, SLOTS, ROWW, channels)
    merged = upsample_forward(around[0], around[1], around[2], all_masks).astype(BF16)
    fc2_all = gathered_over_groups(fc2_sums, dp_pos)
    normed_one_grad, fc2_all, *chip_sums.moving = tied(
        normed_one_grad, fc2_all, *chip_sums.moving
    )
    gather = GroupGather(chip_sums.result(), dp_pos)
    normed_one_grad = normed_one_grad.astype(F32) + dot_t(query_low, query_weight)

    norm_one_pull = jax.vjp(layer_norm, stream_start, norm1_gain, norm1_bias)[1]
    start_side, norm1_gain_grad, norm1_bias_grad = norm_one_pull(normed_one_grad)
    tokens_grad = after_grad + start_side
    table_rows = dataset_table.shape[0]
    dataset = jnp.full_like(number, -1)
    for item in range(item_count):
        dataset = jnp.where(number == item, ids[item], dataset)
    dataset = jnp.where(is_real, dataset, -1).reshape(1, -1)
    onehot = (dataset == lax.broadcasted_iota(jnp.int32, (table_rows, 1), 0)).astype(F32)
    table_grad = jnp.dot(onehot, tokens_grad, precision=HIGH)
    table_split = jnp.swapaxes(table_grad.reshape(table_rows, cycle_size, rows), 0, 1)
    small = [table_split.reshape(cycle_size, -1)] + [
        gradient.reshape(cycle_size, -1)
        for gradient in (norm1_gain_grad, norm1_bias_grad, norm2_gain_grad, norm2_bias_grad)
    ]
    small = jnp.concatenate(small, axis=1).astype(BF16)
    small_rows = -(-small.shape[1] // 1024) * 8
    small = jnp.pad(small, ((0, 0), (0, small_rows * 128 - small.shape[1])))
    small = small.reshape(cycle_size, small_rows, 128)
    small = core_summed(small, core)
    for bit in range(bits):
        gather.step(bit)
        small = over_groups(small, bit)
    small = sum_over_chips(small, chip).reshape(-1)
    table_size = table_rows * rows
    norms = [small[table_size + index * rows :][:rows] for index in range(4)]

    unit_share = 9 * channels // cycle_size
    out_share = channels // cycle_size
    convs, fc1_share, outs, keys_values, query_share = whole_shares(
        gather.result(), late, late_orders
    )
    return (
        block_out,
        merged,
        tokens_grad,
        small[:table_size].reshape(table_rows, rows),
        norms[0],
        norms[1],
        query_share,
        keys_values[:rows],
        keys_values[rows:],
        outs[:rows],
        norms[2],
        norms[3],
        fc1_share,
        fc2_all.reshape(-1, width_model).astype(F32),
        outs[rows:].reshape(rows, channels),
        convs[:unit_share],
        convs[unit_share : 2 * unit_share],
        convs[2 * unit_share : 3 * unit_share],
        convs[3 * unit_share : 4 * unit_share],
        convs[4 * unit_share :],
    )


def solution(mesh):
    split = P(("dp", "blk"), None)
    placed = (split, P("dp", None), P("dp", None)) + (P(),) * 17 + (split, split)
    rows, line = P("blk", None), P("blk")
    return jax.shard_map(
        shards,
        mesh=mesh,
        in_specs=placed,
        out_specs=(
            split, split, split, P(None, "blk"), line, line, rows, rows, rows, rows, line, line,
            rows, rows, rows, rows, rows, rows, rows, rows,
        ),
        check_vma=False,
    )
```

```python
import functools
import math
import typing

import jax
import jax.numpy as jnp
from jax import lax
from jax.experimental import pallas as pl
from jax.experimental.pallas import tpu as pltpu
from jax.sharding import PartitionSpec as P
import numpy as np

HEADS = 12
HEAD = 64
ROWW = 40
SLOTS = 12
HALF = SLOTS // 2
REACH = 6
PITCH = 48
CH = 256

NEG = -1e30
EPS = 1e-06
HIGH = lax.Precision.HIGHEST
KEYS = 672
SPARE_KEYS = 768
QROWS = 64
TOGETHER = 5
TOGETHER_BACK = 2
ROWS = 1024
VMEM = 60 * 1024 * 1024
NT = (((1,), (1,)), ((), ()))
FLIP = (((0,), (0,)), ((), ()))
F32 = jnp.float32
BF16 = jnp.bfloat16


def cost(microseconds):
    return pl.CostEstimate(flops=microseconds * 10**9, bytes_accessed=10**6, transcendentals=0)


def own_blocks(heads, feats):
    row = lax.broadcasted_iota(jnp.int32, (heads * QROWS, feats), 0) // QROWS
    col = lax.broadcasted_iota(jnp.int32, (heads * QROWS, feats), 1) // HEAD
    return row == col


def spread(block, heads):
    wide = jnp.concatenate([block] * heads, axis=0)
    return jnp.where(own_blocks(heads, block.shape[1]), wide, jnp.zeros((), block.dtype))


def gathered(wide, heads):
    kept = jnp.where(own_blocks(heads, wide.shape[1]), wide, 0.0)
    total = kept[:QROWS]
    for head in range(1, heads):
        total = total + kept[head * QROWS : (head + 1) * QROWS]
    return total


def lanes(column, width):
    return jnp.concatenate([column] * (width // 128), axis=1)


class Tables(typing.NamedTuple):
    koff: jax.Array
    kcnt: jax.Array
    kdst: jax.Array
    kstart: jax.Array
    klen: jax.Array
    qfirst: jax.Array
    qcount: jax.Array
    ubase: jax.Array
    uspare: jax.Array
    uwidth: jax.Array
    uitem: jax.Array
    qbase: jax.Array
    qspare: jax.Array
    qwidth: jax.Array
    qitem: jax.Array
    wwidth: jax.Array
    wup: jax.Array
    wdown: jax.Array
    wgroup: jax.Array
    wcame: jax.Array
    sent: jax.Array
    back: jax.Array
    came: jax.Array
    around: jax.Array


TABLES = len(Tables._fields)


def pieces(cycle_size):
    return -(-(SLOTS + 2 * REACH) // cycle_size), -(-SLOTS // cycle_size)


def floor_div(value, by):
    return lax.div(value + 16 * by, by) - 16


def first_slot(begin, device, cycle_size):
    return -floor_div(device - begin, cycle_size)


def unit_source(unit, me, chips):
    chip, core = lax.div(me, 2), lax.rem(me, 2)
    turn, half = lax.div(unit, 4), lax.rem(unit, 2)
    other = lax.rem(lax.div(unit, 2), 2)
    turn = jnp.where(half == 0, -turn, turn)
    source = 2 * lax.rem(chip + turn + chips, chips) + jnp.where(other == 0, core, 1 - core)
    return source, half


def geometry_kernel(cycle_size, unit_size, lengths, place, *refs):
    tab = Tables(*refs)
    item_count = lengths.shape[0]
    items = item_count + 1
    chips = cycle_size // 2
    units = 4 * chips
    me = place[0]
    many, few = pieces(cycle_size)
    facts, start = [], 0
    for item in range(item_count):
        length = lengths[item]
        height = jnp.where(length == 1200, 30, jnp.where(length == 576, 24, 0))
        facts.append((start, start + height, jnp.where(length == 1200, 40, 24)))
        start = start + height

    def fact(row):
        number, width = item_count, 0
        for item, (begin, end, item_width) in enumerate(facts):
            inside = (row >= begin) & (row < end)
            number = jnp.where(inside, item, number)
            width = jnp.where(inside, item_width, width)
        return number, width

    def up(value, align):
        return lax.div(value + (align - 1), align) * align

    def sort(rows, align, base, spare_base, widths, numbers, first):
        known = [fact(row) for row in rows]
        counts = [
            sum(jnp.where(number == item, width, 0) for number, width in known)
            for item in range(item_count)
        ]
        counts.append(sum(ROWW - width for _, width in known))
        offsets, total = [], 0
        for count in counts:
            offsets.append(total)
            total = total + up(count, align)
        spare = offsets[-1]
        for slot, (number, width) in enumerate(known):
            begin = sum(jnp.where(number == item, offsets[item], 0) for item in range(item_count))
            for other, other_width in known[:slot]:
                begin = begin + jnp.where(other == number, other_width, 0)
            base[first + slot] = begin
            spare_base[first + slot] = spare - width
            widths[first + slot] = width
            numbers[first + slot] = number
            spare = spare + ROWW - width
        return counts, offsets

    def one_unit(unit, lens):
        source, half = unit_source(unit, me, chips)
        rows = [(half * HALF + slot) * cycle_size + source for slot in range(HALF)]
        counts, offsets = sort(
            rows, 16, tab.ubase, tab.uspare, tab.uwidth, tab.uitem, unit * HALF
        )
        for item in range(items):
            tab.koff[unit * items + item] = offsets[item] + unit * unit_size
            tab.kcnt[unit * items + item] = counts[item]
        return tuple(length + up(count, 16) for length, count in zip(lens, counts))

    lens = lax.fori_loop(0, units, one_unit, (jnp.int32(0),) * items)
    starts = [jnp.int32(0)]
    for item in range(items):
        size = SPARE_KEYS if item == items - 1 else KEYS
        tab.klen[item] = lens[item]
        tab.kstart[item] = starts[item]
        starts.append(starts[item] + up(lens[item], size))
    tab.kstart[items] = starts[items]

    def place_unit(unit, at):
        for item in range(items):
            tab.kdst[unit * items + item] = at[item]
        return tuple(
            spot + up(tab.kcnt[unit * items + item], 16) for item, spot in enumerate(at)
        )

    lax.fori_loop(0, units, place_unit, tuple(starts[:items]))
    for index in range(SLOTS + 2 * REACH):
        row = SLOTS * me - REACH + index
        width, above, below = 0, 0, 0
        for begin, end, item_width in facts:
            inside = (row >= begin) & (row < end)
            width = jnp.where(inside, item_width, width)
            above = jnp.where(inside & (row > begin), 1, above)
            below = jnp.where(inside & (row + 1 < end), 1, below)
        tab.wwidth[index] = width
        tab.wup[index] = above
        tab.wdown[index] = below
        inner = jnp.clip(row, 0, SLOTS * cycle_size - 1)
        slot = lax.div(inner, cycle_size)
        device = inner - slot * cycle_size
        tab.wgroup[index] = (device * SLOTS + slot) * PITCH
        slot = floor_div(row, cycle_size)
        device = row - slot * cycle_size
        turn = slot - first_slot(SLOTS * me - REACH, device, cycle_size)
        tab.wcame[index] = (device * many + turn) * PITCH
    for device in range(cycle_size):
        first = first_slot(SLOTS * device - REACH, me, cycle_size)
        for turn in range(many):
            tab.sent[device * many + turn] = first + turn
        first = first_slot(SLOTS * me, device, cycle_size)
        for turn in range(few):
            tab.back[device * few + turn] = (first + turn) * cycle_size + device - SLOTS * me
    for slot in range(SLOTS):
        row = slot * cycle_size + me
        source = lax.div(row, SLOTS)
        turn = slot - first_slot(source * SLOTS, me, cycle_size)
        tab.came[slot] = (source * few + turn) * PITCH
        for turn in range(3):
            near = jnp.clip(row + turn - 1, 0, SLOTS * cycle_size - 1)
            tab.around[turn * SLOTS + slot] = near * PITCH
    rows = [slot * cycle_size + me for slot in range(SLOTS)]
    counts, offsets = sort(rows, QROWS, tab.qbase, tab.qspare, tab.qwidth, tab.qitem, 0)
    for item in range(items):
        tab.qfirst[item] = lax.div(offsets[item], QROWS)
        tab.qcount[item] = lax.div(counts[item] + (QROWS - 1), QROWS)


def geometry(lengths, cycle_pos, cycle_size, unit_size):
    items = lengths.shape[0] + 1
    units = 2 * cycle_size
    sizes = [units * items] * 3 + [items + 1] + [items] * 3 + [units * HALF] * 4 + [SLOTS] * 4
    sizes += [SLOTS + 2 * REACH] * 5
    many, few = pieces(cycle_size)
    sizes += [cycle_size * many, cycle_size * few, SLOTS, 3 * SLOTS]
    smem = pl.BlockSpec(memory_space=pltpu.SMEM)
    return Tables(
        *pl.pallas_call(
            functools.partial(geometry_kernel, cycle_size, unit_size),
            in_specs=[smem, smem],
            out_specs=[smem] * TABLES,
            out_shape=[jax.ShapeDtypeStruct((size,), jnp.int32) for size in sizes],
            name="geometry",
        )(lengths, cycle_pos.reshape(1))
    )


def places(base, spare, width, first, slots):
    token = lax.broadcasted_iota(jnp.int32, (1, slots * ROWW), 1)
    place = jnp.zeros_like(token)
    for slot in range(slots):
        column = token - slot * ROWW
        here = jnp.where(column < width[first + slot], base[first + slot], spare[first + slot])
        place = jnp.where((column >= 0) & (column < ROWW), here + column, place)
    return place


def unsorter(base, spare, width, first, slots, rows):
    token = lax.broadcasted_iota(jnp.int32, (slots * ROWW, 1), 0)
    place = jnp.zeros_like(token)
    for slot in range(slots):
        column = token - slot * ROWW
        here = jnp.where(column < width[first + slot], base[first + slot], spare[first + slot])
        place = jnp.where((column >= 0) & (column < ROWW), here + column, place)
    spot = lax.broadcasted_iota(jnp.int32, (slots * ROWW, rows), 1)
    return jnp.where(spot == place, 1.0, 0.0).astype(BF16)


def query_unsorter(tab, rows):
    return unsorter(tab.qbase, tab.qspare, tab.qwidth, 0, SLOTS, rows)


def sorter(place, rows):
    spot = lax.broadcasted_iota(jnp.int32, (rows, place.shape[1]), 0)
    return jnp.where(spot == place, 1.0, 0.0).astype(BF16)


def query_sorter(tab, rows):
    return sorter(places(tab.qbase, tab.qspare, tab.qwidth, 0, SLOTS), rows)


def with_dataset(values, width, item, first, ids, table_ref):
    column = lax.broadcasted_iota(jnp.int32, (ROWW, 1), 0)
    parts = []
    for slot in range(values.shape[0] // ROWW):
        number = jnp.minimum(item[first + slot], ids.shape[0] - 1)
        added = table_ref[pl.ds(ids[number], 1), :]
        real = column < width[first + slot]
        parts.append(values[slot * ROWW : (slot + 1) * ROWW] + jnp.where(real, added, 0.0))
    return jnp.concatenate(parts, axis=0)


def layer_norm(hidden, norm_gain, norm_bias):
    centred = hidden - jnp.mean(hidden, axis=-1, keepdims=True)
    variance = jnp.mean(centred * centred, axis=-1, keepdims=True)
    return centred * lax.rsqrt(variance + EPS) * norm_gain + norm_bias


def sort_step_kernel(step, ubase, uspare, uwidth, uitem, ids, *refs):
    mine_ref, other_ref, table_ref, gain_ref, bias_ref, out_ref = refs
    unit_size = out_ref.shape[0] // 4
    count = HALF * ROWW
    for unit in range(4):
        source = (mine_ref, other_ref)[unit // 2]
        first = (4 * step + unit) * HALF
        values = source[unit % 2 * count : (unit % 2 + 1) * count, :].astype(F32)
        values = with_dataset(values, uwidth, uitem, first, ids, table_ref)
        normed = layer_norm(values, gain_ref[...], bias_ref[...]).astype(BF16)
        matrix = sorter(places(ubase, uspare, uwidth, first, HALF), unit_size)
        out_ref[unit * unit_size : (unit + 1) * unit_size, :] = jnp.dot(
            matrix, normed, preferred_element_type=F32
        ).astype(BF16)


def sort_step(step, tab, ids, mine, other, table, gain, bias, unit_size):
    return pl.pallas_call(
        functools.partial(sort_step_kernel, step),
        grid_spec=pltpu.PrefetchScalarGridSpec(
            num_scalar_prefetch=5,
            in_specs=[pl.BlockSpec(memory_space=pltpu.VMEM)] * 5,
            out_specs=pl.BlockSpec(memory_space=pltpu.VMEM),
        ),
        out_shape=jax.ShapeDtypeStruct((4 * unit_size, mine.shape[1]), BF16),
        cost_estimate=cost(3),
        compiler_params=pltpu.CompilerParams(vmem_limit_bytes=VMEM),
        name="sort_step",
    )(tab.ubase, tab.uspare, tab.uwidth, tab.uitem, ids, mine, other, table, gain, bias)


def own_start_kernel(qbase, qspare, qwidth, qitem, ids, *refs):
    tokens_ref, table_ref, gain_ref, bias_ref, weight_ref, start_ref, normed_ref, query_ref = refs
    values = tokens_ref[...].astype(F32)
    values = with_dataset(values, qwidth, qitem, 0, ids, table_ref)
    start_ref[...] = values
    normed = layer_norm(values, gain_ref[...], bias_ref[...]).astype(BF16)
    normed_ref[...] = normed
    matrix = sorter(places(qbase, qspare, qwidth, 0, SLOTS), query_ref.shape[0])
    sorted_norm = jnp.dot(matrix, normed, preferred_element_type=F32).astype(BF16)
    query = jnp.dot(sorted_norm, weight_ref[...], preferred_element_type=F32)
    query_ref[...] = (query * (1.0 / math.sqrt(HEAD))).astype(BF16)


def own_start(tab, ids, tokens, table, gain, bias, weight, query_rows):
    vmem = pl.BlockSpec(memory_space=pltpu.VMEM)
    return pl.pallas_call(
        own_start_kernel,
        grid_spec=pltpu.PrefetchScalarGridSpec(
            num_scalar_prefetch=5, in_specs=[vmem] * 5, out_specs=[vmem] * 3
        ),
        out_shape=[
            jax.ShapeDtypeStruct(tokens.shape, F32),
            jax.ShapeDtypeStruct(tokens.shape, BF16),
            jax.ShapeDtypeStruct((query_rows, tokens.shape[1]), BF16),
        ],
        cost_estimate=cost(5),
        compiler_params=pltpu.CompilerParams(vmem_limit_bytes=VMEM),
        name="own_start",
    )(tab.qbase, tab.qspare, tab.qwidth, tab.qitem, ids, tokens, table, gain, bias, weight)


def query_blocks(first, many, most, body):
    def run(number, none):
        body(first + most * number, most)
        return none

    runs = lax.div(many, most)
    lax.fori_loop(0, runs, run, 0)
    for count in range(1, most):

        @pl.when(many - most * runs == count)
        def _(count=count):
            body(first + most * runs, count)


def for_items(items, klen, body):
    def one(item, none):
        body(item, KEYS, (klen[item] + KEYS - 1) // KEYS)
        return none

    lax.fori_loop(0, items - 1, one, 0)
    last = items - 1
    body(last, SPARE_KEYS, (klen[last] + SPARE_KEYS - 1) // SPARE_KEYS)


def as_column(row):
    return row.T[:, :1]


def attend_kernel(heads, units, items, *refs):
    tab, refs = Tables(*refs[:TABLES]), refs[TABLES:]
    koff, kcnt, kdst, kstart, klen, qfirst, qcount = tab[:7]
    steps = units // 4
    q_ref, wk_ref, wv_ref = refs[:3]
    n_refs, refs = refs[3 : 3 + steps], refs[3 + steps :]
    att_ref, o_ref, lse_ref, ns_ref, bias_ref, ks_ref, vs_ref = refs[:7]
    acc_ref, top_ref, total_ref, matrix = refs[7:]
    stride = n_refs[0].shape[0]
    cols = heads * QROWS
    width = ns_ref.shape[1]
    o_ref[...] = jnp.zeros_like(o_ref)
    lse_ref[...] = jnp.zeros_like(lse_ref)
    used = kstart[items]

    @pl.when(pl.program_id(0) == 0)
    def _():
        matrix[...] = query_unsorter(tab, o_ref.shape[0])

        def one_item(item, size, blocks):
            def one_unit(turn, unit, none):
                entry = (4 * turn + unit) * items + item
                count, source, target = kcnt[entry], koff[entry] - turn * stride, kdst[entry]

                def step(part, none):
                    src = pl.ds(pl.multiple_of(source + 64 * part, 16), 64)
                    dst = pl.ds(pl.multiple_of(target + 64 * part, 16), 64)
                    ns_ref[dst, :] = n_refs[turn][src, :]
                    row = lax.broadcasted_iota(jnp.int32, (64, 128), 0) + 64 * part
                    bias_ref[dst, :] = jnp.where(row < count, 0.0, NEG).astype(BF16)
                    return none

                return lax.fori_loop(0, (count + 63) // 64, step, none)

            for turn in range(steps):
                lax.fori_loop(0, 4, functools.partial(one_unit, turn), 0)
            end = kstart[item] + klen[item]

            def clear(part, none):
                tail = pl.ds(pl.multiple_of(end + 64 * part, 16), 64)
                ns_ref[tail, :] = jnp.zeros((64, width), BF16)
                bias_ref[tail, :] = jnp.full((64, 128), NEG, BF16)
                return none

            lax.fori_loop(0, (kstart[item + 1] - end + 63) // 64 + 1, clear, 0)

        for_items(items, klen, one_item)

        def clear(part, none):
            tail = pl.ds(pl.multiple_of(used + 64 * part, 16), 64)
            ns_ref[tail, :] = jnp.zeros((64, width), BF16)
            return none

        lax.fori_loop(0, (ns_ref.shape[0] - used) // 64, clear, 0)

    def project(block, none):
        here = pl.ds(pl.multiple_of(block * ROWS, ROWS), ROWS)
        rows = ns_ref[here, :]
        ks_ref[here, :] = jnp.dot(rows, wk_ref[...], preferred_element_type=F32).astype(BF16)
        vs_ref[here, :] = jnp.dot(rows, wv_ref[...], preferred_element_type=F32).astype(BF16)
        return none

    lax.fori_loop(0, (used + ROWS - 1) // ROWS, project, 0)

    def one_item(item, size, blocks):
        def some_queries(place, count):
            wide = count * cols
            rows = pl.ds(pl.multiple_of(place * QROWS, QROWS), count * QROWS)
            block = q_ref[rows, :]
            queries = jnp.concatenate(
                [spread(block[n * QROWS : (n + 1) * QROWS], heads) for n in range(count)], axis=0
            )
            top, total, acc = top_ref.at[:, :wide], total_ref.at[:, :wide], acc_ref.at[:wide]
            top[...] = jnp.full((8, wide), NEG, F32)
            total[...] = jnp.zeros((8, wide), F32)
            acc[...] = jnp.zeros((wide, heads * HEAD), F32)

            def step(number, none):
                here = pl.ds(pl.multiple_of(kstart[item] + number * size, 16), size)
                scores = lax.dot_general(
                    ks_ref[here, :], queries, NT, preferred_element_type=F32
                ) + lanes(bias_ref[here, :].astype(F32), wide)
                best = jnp.max(jnp.max(scores.reshape(size // 8, 8, wide), axis=0), axis=0)
                old = top[...]
                best = jnp.maximum(old, jnp.broadcast_to(best[None], (8, wide)))
                top[...] = best
                shrink = jnp.exp(old - best)
                weights = jnp.exp(scores - best[:1])
                total[...] = total[...] * shrink + jnp.sum(
                    weights.reshape(size // 8, 8, wide), axis=0
                )
                acc[...] = acc[...] * as_column(shrink) + lax.dot_general(
                    weights.astype(BF16),
                    vs_ref[here, :],
                    (((0,), (0,)), ((), ())),
                    preferred_element_type=F32,
                )
                return none

            lax.fori_loop(0, blocks, step, 0)
            summed = jnp.broadcast_to(jnp.sum(total[...], axis=0, keepdims=True), (8, wide))
            lse = top[...] + jnp.log(summed)
            out = acc[...] * as_column(1.0 / summed)
            for n in range(count):
                part = slice(n * cols, (n + 1) * cols)
                lse_ref[pl.ds(place + n, 1), :] = lse[:1, part]
                o_ref[pl.ds(pl.multiple_of((place + n) * QROWS, QROWS), QROWS), :] = gathered(
                    out[part], heads
                )

        query_blocks(qfirst[item], qcount[item], TOGETHER, some_queries)

    for_items(items, klen, one_item)
    att_ref[...] = jnp.dot(
        matrix[...], o_ref[...].astype(BF16), preferred_element_type=F32
    ).astype(BF16)


def attend_back_kernel(heads, units, items, unit_size, me, *refs):
    tab, refs = Tables(*refs[:TABLES]), refs[TABLES:]
    koff, kcnt, kdst, kstart, klen, qfirst, qcount = tab[:7]
    q_ref, grad_ref, o_ref, lse_ref, ks_ref, vs_ref, wk_ref, wv_ref, ns_ref, bias_ref = refs[:10]
    dq_ref, gk_ref, gv_ref, dn_ref = refs[10:14]
    (
        spread_q, spread_do, delta, dq_acc, dk_acc, dv_acc, gk_acc, gv_acc, dn_acc,
        matrix, back_matrix, do_ref, dqs, unit_rows,
    ) = refs[14:]
    feats = heads * HEAD
    cols = heads * QROWS
    flip = FLIP
    dqs[...] = jnp.zeros_like(dqs)
    gk_acc[...] = jnp.zeros_like(gk_acc)
    gv_acc[...] = jnp.zeros_like(gv_acc)
    used = qfirst[items - 1] + qcount[items - 1]

    @pl.when(pl.program_id(0) == 0)
    def _():
        dn_acc[...] = jnp.zeros_like(dn_acc)
        matrix[...] = query_sorter(tab, q_ref.shape[0])
        back_matrix[...] = query_unsorter(tab, q_ref.shape[0])

    do_ref[...] = jnp.dot(matrix[...], grad_ref[...], preferred_element_type=F32).astype(BF16)

    def prepare(place, none):
        rows = pl.ds(pl.multiple_of(place * QROWS, QROWS), QROWS)
        grads = do_ref[rows, :]
        spread_q[place] = spread(q_ref[rows, :], heads)
        spread_do[place] = spread(grads, heads)
        product = spread(grads.astype(F32) * o_ref[rows, :], heads)
        delta[place] = lax.dot_general(
            jnp.ones((8, feats), F32), product, NT, precision=HIGH, preferred_element_type=F32
        )
        dq_acc[place] = jnp.zeros((cols, feats), F32)
        return none

    lax.fori_loop(0, used, prepare, 0)

    def one_item(item, size, blocks):
        def one_block(number, none):
            here = pl.ds(pl.multiple_of(kstart[item] + number * size, 16), size)
            dk_acc[:size] = jnp.zeros((size, feats), F32)
            dv_acc[:size] = jnp.zeros((size, feats), F32)

            def some_queries(place, count):
                wide = count * cols
                spot = pl.ds(place, count)
                queries = spread_q[spot].reshape(wide, feats)
                grads = spread_do[spot].reshape(wide, feats)
                row = [lse_ref[pl.ds(place + n, 1), :] for n in range(count)]
                log_total = jnp.concatenate(row, axis=1)
                shift = jnp.concatenate([delta[place + n, :1, :] for n in range(count)], axis=1)
                keys = ks_ref[here, :]
                scores = lax.dot_general(keys, queries, NT, preferred_element_type=F32)
                weights = jnp.exp(scores + lanes(bias_ref[here, :].astype(F32), wide) - log_total)
                slopes = lax.dot_general(vs_ref[here, :], grads, NT, preferred_element_type=F32)
                score_grads = (weights * (slopes - shift)).astype(BF16)
                dv_acc[:size] += jnp.dot(weights.astype(BF16), grads, preferred_element_type=F32)
                dk_acc[:size] += jnp.dot(score_grads, queries, preferred_element_type=F32)
                part = lax.dot_general(score_grads, keys, flip, preferred_element_type=F32)
                dq_acc[spot] += part.reshape(count, cols, feats)

            query_blocks(qfirst[item], qcount[item], TOGETHER_BACK, some_queries)
            dk = dk_acc[:size].astype(BF16)
            dv = dv_acc[:size].astype(BF16)
            dn_acc[here, :] += (
                lax.dot_general(dk, wk_ref[...], NT, preferred_element_type=F32)
                + lax.dot_general(dv, wv_ref[...], NT, preferred_element_type=F32)
            ).astype(dn_acc.dtype)
            rows = ns_ref[here, :]
            gk_acc[...] += lax.dot_general(rows, dk, flip, preferred_element_type=F32)
            gv_acc[...] += lax.dot_general(rows, dv, flip, preferred_element_type=F32)
            return none

        lax.fori_loop(0, jnp.where(qcount[item] > 0, blocks, 0), one_block, 0)

    for_items(items, klen, one_item)

    def finish(place, none):
        rows = pl.ds(pl.multiple_of(place * QROWS, QROWS), QROWS)
        scale = 1.0 / math.sqrt(HEAD)
        dqs[rows, :] = (gathered(dq_acc[place], heads) * scale).astype(BF16)
        return none

    lax.fori_loop(0, used, finish, 0)
    dq_ref[...] = jnp.dot(back_matrix[...], dqs[...], preferred_element_type=F32).astype(BF16)
    gk_ref[...] = gk_acc[...].astype(BF16)
    gv_ref[...] = gv_acc[...].astype(BF16)

    @pl.when(pl.program_id(0) == pl.num_programs(0) - 1)
    def _():
        unit_rows[...] = jnp.zeros_like(unit_rows)
        count = HALF * ROWW

        def one_unit(unit, none):
            def one_item(item, none):
                entry = unit * items + item
                source, target = koff[entry] - unit * unit_size, kdst[entry]

                def step(part, none):
                    src = pl.ds(pl.multiple_of(source + 64 * part, 16), 64)
                    dst = pl.ds(pl.multiple_of(target + 64 * part, 16), 64)
                    unit_rows[src, :] = dn_acc[dst, :]
                    return none

                return lax.fori_loop(0, (kcnt[entry] + 63) // 64, step, none)

            lax.fori_loop(0, items, one_item, 0)
            back = unsorter(tab.ubase, tab.uspare, tab.uwidth, unit * HALF, HALF, unit_size)
            source, half = unit_source(unit, me[0], units // 4)
            spot = (2 * source + half) * count
            dn_ref[pl.ds(pl.multiple_of(spot, 16), count), :] = jnp.dot(
                back, unit_rows[...], preferred_element_type=F32
            ).astype(BF16)
            return none

        lax.fori_loop(0, units, one_unit, 0)


def gelu_parts(values):
    slope = 0.7978845608028654
    bent = jnp.tanh(slope * (values + 0.044715 * values * values * values))
    return bent, slope * (1.0 + 3.0 * 0.044715 * values * values)


def gelu(values):
    return 0.5 * values * (1.0 + gelu_parts(values)[0])


def gelu_slope(values):
    bent, inner = gelu_parts(values)
    return 0.5 * (1.0 + bent) + 0.5 * values * (1.0 - bent * bent) * inner


def merge_kernel(
    cycle_size, wwidth, wup, wdown, wgroup, wcame, back,
    came_ref, group_ref, k11, k12, k21, k22, out_weight, grad_ref, mapped_ref, shares_ref,
    x1, x2, x3, x4, g3, real_ref, up_ref, down_ref, c1, m1, c3, m2g, m1g, win_ref, rows_ref,
):
    window = SLOTS + 2 * REACH
    column = lax.broadcasted_iota(jnp.int32, (PITCH, 128), 0)
    for row in range(window):
        spots = pl.ds(row * PITCH, PITCH)
        win_ref[spots, :CH] = came_ref[pl.ds(pl.multiple_of(wcame[row], 16), PITCH), :]
        win_ref[spots, CH:] = group_ref[pl.ds(pl.multiple_of(wgroup[row], 16), PITCH), :]
        real = jnp.where(column < wwidth[row], 1.0, 0.0)
        real_ref[spots, :] = real
        up_ref[spots, :] = real * wup[row].astype(F32)
        down_ref[spots, :] = real * wdown[row].astype(F32)

    def at(low, high):
        return slice(low * PITCH, high * PITCH)

    def masked(ref, values, low, high):
        return values * lanes(ref[at(low, high), :], CH)

    def fill(taps, values, low, high):
        spots = at(low + 1, high + 1)
        size = values.shape[0]
        taps[spots, :CH] = pltpu.roll(values, 1, 0).astype(BF16)
        taps[spots, CH : 2 * CH] = values.astype(BF16)
        taps[spots, 2 * CH :] = pltpu.roll(values, size - 1, 0).astype(BF16)

    def conv(taps, kernel, low, high):
        def part(row_step):
            rows = taps[at(low + 1 + row_step, high + 1 + row_step), :]
            first = (row_step + 1) * 3 * CH
            return jnp.dot(rows, kernel[first : first + 3 * CH, :], preferred_element_type=F32)

        total = masked(real_ref, part(0), low, high)
        total = total + masked(up_ref, part(-1), low, high)
        return total + masked(down_ref, part(1), low, high)

    def conv_back(kernel, low, high):
        def part(row_step):
            rows = at(low + 1 + row_step, high + 1 + row_step)
            total = None
            for col_step in (-1, 0, 1):
                first = (8 - (3 * (row_step + 1) + col_step + 1)) * CH
                side = (col_step + 1) * CH
                now = lax.dot_general(
                    g3[rows, side : side + CH],
                    kernel[first : first + CH, :],
                    NT,
                    preferred_element_type=F32,
                )
                total = now if total is None else total + now
            return total

        total = masked(real_ref, part(0), low, high)
        total = total + masked(up_ref, part(-1), low, high)
        return total + masked(down_ref, part(1), low, high)

    own, last = REACH, REACH + SLOTS
    unit_share = 9 * CH // cycle_size
    out_share = CH // cycle_size
    share_rows = 4 * unit_share + out_share

    def weight_grad(taps, gradient, tensor):
        piece = math.gcd(3 * CH, unit_share)
        for row_step, mask in ((-1, up_ref), (0, real_ref), (1, down_ref)):
            now = masked(mask, gradient, own, last).astype(BF16)
            rows = taps[at(own + 1 + row_step, last + 1 + row_step), :]
            block = lax.dot_general(rows, now, FLIP, preferred_element_type=F32).astype(BF16)
            for part in range(3 * CH // piece):
                spot = (row_step + 1) * 3 * CH + part * piece
                share, offset = divmod(spot, unit_share)
                first = share * share_rows + tensor * unit_share + offset
                shares_ref[first : first + piece, :] = block[part * piece : (part + 1) * piece]

    def start(low, high):
        return win_ref[at(low, high), :CH].astype(F32)

    fill(x1, masked(real_ref, gelu(start(0, 24)), 0, 24), 0, 24)
    c1[at(1, 23), :] = conv(x1, k11, 1, 23)
    fill(x2, masked(real_ref, gelu(c1[at(1, 23), :]), 1, 23), 1, 23)
    m1[at(2, 22), :] = start(2, 22) + conv(x2, k12, 2, 22)
    fill(x3, masked(real_ref, gelu(m1[at(2, 22), :]), 2, 22), 2, 22)
    c3[at(3, 21), :] = conv(x3, k21, 3, 21)
    fill(x4, masked(real_ref, gelu(c3[at(3, 21), :]), 3, 21), 3, 21)
    merged = (m1[at(own, last), :] + conv(x4, k22, own, last)).astype(BF16)

    def send(values, ref):
        rows_ref[...] = values
        for piece in range(back.shape[0]):
            row = jnp.minimum(back[piece], SLOTS - 1)
            block = rows_ref[pl.ds(pl.multiple_of(row * PITCH, PITCH), PITCH), :]
            ref[piece * PITCH : (piece + 1) * PITCH, :] = block.astype(BF16)

    mapped_ref[...] = jnp.dot(merged, out_weight[...], preferred_element_type=F32).astype(BF16)
    block = lax.dot_general(
        merged, win_ref[at(own, last), CH:], FLIP, preferred_element_type=F32
    ).astype(BF16)
    for share in range(cycle_size):
        first = share * share_rows + 4 * unit_share
        shares_ref[first : first + out_share, :] = block[share * out_share : (share + 1) * out_share]

    m2g[at(2, 22), :] = lax.dot_general(
        win_ref[at(2, 22), CH:], out_weight[...], NT, preferred_element_type=F32
    )
    fill(g3, masked(real_ref, m2g[at(2, 22), :], 2, 22), 2, 22)
    weight_grad(x4, m2g[at(own, last), :], 3)
    now = gelu_slope(c3[at(3, 21), :]) * conv_back(k22, 3, 21)
    fill(g3, now, 3, 21)
    weight_grad(x3, now[at(own - 3, last - 3)], 2)
    m1g[at(4, 20), :] = m2g[at(4, 20), :] + gelu_slope(m1[at(4, 20), :]) * conv_back(k21, 4, 20)
    fill(g3, masked(real_ref, m1g[at(4, 20), :], 4, 20), 4, 20)
    weight_grad(x2, m1g[at(own, last), :], 1)
    now = gelu_slope(c1[at(5, 19), :]) * conv_back(k12, 5, 19)
    fill(g3, now, 5, 19)
    weight_grad(x1, now[at(own - 5, last - 5)], 0)
    now = gelu_slope(start(own, last)) * conv_back(k11, own, last)
    send(m1g[at(own, last), :] + now, grad_ref)


def pack_kernel(sent, block_ref, weight_ref, out_ref, rows_ref):
    rows_ref[...] = jnp.dot(block_ref[...], weight_ref[...], preferred_element_type=F32)
    blank = jnp.zeros((PITCH - ROWW, CH), F32)
    for piece in range(sent.shape[0]):
        slot = jnp.clip(sent[piece], 0, SLOTS - 1)
        block = rows_ref[pl.ds(pl.multiple_of(slot * ROWW, 8), ROWW), :]
        out_ref[piece * PITCH : (piece + 1) * PITCH, :] = jnp.concatenate(
            [block, blank], axis=0
        ).astype(BF16)


def pack(tab, block_out, weight):
    vmem = pl.BlockSpec(memory_space=pltpu.VMEM)
    return pl.pallas_call(
        pack_kernel,
        grid_spec=pltpu.PrefetchScalarGridSpec(
            num_scalar_prefetch=1,
            in_specs=[vmem] * 2,
            out_specs=vmem,
            scratch_shapes=[pltpu.VMEM((block_out.shape[0], CH), F32)],
        ),
        out_shape=jax.ShapeDtypeStruct((tab.sent.shape[0] * PITCH, CH), BF16),
        cost_estimate=cost(2),
        compiler_params=pltpu.CompilerParams(vmem_limit_bytes=VMEM),
        name="pack",
    )(tab.sent, block_out, weight)


def unpack_kernel(came, rows_ref, out_ref):
    parts = []
    for slot in range(came.shape[0]):
        block = rows_ref[pl.ds(pl.multiple_of(came[slot], 16), PITCH), :].astype(F32)
        parts.append(block[:ROWW])
    out_ref[...] = jnp.concatenate(parts, axis=0).astype(BF16)


def unpack(came, rows):
    vmem = pl.BlockSpec(memory_space=pltpu.VMEM)
    return pl.pallas_call(
        unpack_kernel,
        grid_spec=pltpu.PrefetchScalarGridSpec(
            num_scalar_prefetch=1, in_specs=[vmem], out_specs=vmem
        ),
        out_shape=jax.ShapeDtypeStruct((came.shape[0] * ROWW, CH), BF16),
        cost_estimate=cost(1),
        compiler_params=pltpu.CompilerParams(vmem_limit_bytes=VMEM),
        name="unpack",
    )(came, rows)


def merge(tab, came, group, kernels, out_weight, cycle_size):
    window = SLOTS + 2 * REACH
    vmem = pl.BlockSpec(memory_space=pltpu.VMEM)
    padded = (window + 2) * PITCH
    share_rows = 4 * (9 * CH // cycle_size) + CH // cycle_size
    small = pltpu.VMEM((window * PITCH, 128), F32)
    large = pltpu.VMEM((window * PITCH, CH), F32)
    return pl.pallas_call(
        functools.partial(merge_kernel, cycle_size),
        grid_spec=pltpu.PrefetchScalarGridSpec(
            num_scalar_prefetch=6,
            in_specs=[vmem] * 7,
            out_specs=[vmem] * 3,
            scratch_shapes=[pltpu.VMEM((padded, 3 * CH), BF16)] * 5
            + [small] * 3
            + [large] * 5
            + [
                pltpu.VMEM((window * PITCH, 2 * CH), BF16),
                pltpu.VMEM((SLOTS * PITCH, CH), F32),
            ],
        ),
        out_shape=[
            jax.ShapeDtypeStruct((tab.back.shape[0] * PITCH, CH), BF16),
            jax.ShapeDtypeStruct((SLOTS * PITCH, CH), BF16),
            jax.ShapeDtypeStruct((cycle_size * share_rows, CH), BF16),
        ],
        cost_estimate=cost(25),
        compiler_params=pltpu.CompilerParams(vmem_limit_bytes=VMEM),
        name="merge",
    )(
        tab.wwidth, tab.wup, tab.wdown, tab.wgroup, tab.wcame, tab.back,
        came, group, *kernels, out_weight,
    )


def attend(tab, query, key_weight, value_weight, norms, sorted_keys, units, items, heads):
    feats = heads * HEAD
    cols = heads * QROWS
    width = query.shape[1]
    groups = width // feats
    blocks8 = (query.shape[0] // QROWS + 7) // 8 * 8
    once = pl.Buffered(1) if units > 16 else None

    def part(rows, columns=feats):
        return pl.BlockSpec((rows, columns), lambda group, *_: (0, group), pipeline_mode=once)

    def whole(rows, columns):
        return pl.BlockSpec(
            (rows, columns), lambda group, *_: (0, 0), pipeline_mode=pl.Buffered(1)
        )

    return pl.pallas_call(
        functools.partial(attend_kernel, heads, units, items),
        grid_spec=pltpu.PrefetchScalarGridSpec(
            num_scalar_prefetch=TABLES,
            grid=(groups,),
            in_specs=[part(query.shape[0]), part(width), part(width)]
            + [whole(*norm.shape) for norm in norms],
            out_specs=[
                part(SLOTS * ROWW),
                part(query.shape[0]),
                part(blocks8, cols),
                whole(sorted_keys, width),
                whole(sorted_keys, 128),
                part(sorted_keys),
                part(sorted_keys),
            ],
            scratch_shapes=[
                pltpu.VMEM((TOGETHER * cols, feats), F32),
                pltpu.VMEM((8, TOGETHER * cols), F32),
                pltpu.VMEM((8, TOGETHER * cols), F32),
                pltpu.VMEM((SLOTS * ROWW, query.shape[0]), BF16),
            ],
        ),
        out_shape=[
            jax.ShapeDtypeStruct((SLOTS * ROWW, width), BF16),
            jax.ShapeDtypeStruct(query.shape, F32),
            jax.ShapeDtypeStruct((blocks8, groups * cols), F32),
            jax.ShapeDtypeStruct((sorted_keys, width), BF16),
            jax.ShapeDtypeStruct((sorted_keys, 128), BF16),
            jax.ShapeDtypeStruct((sorted_keys, width), BF16),
            jax.ShapeDtypeStruct((sorted_keys, width), BF16),
        ],
        cost_estimate=cost(70),
        compiler_params=pltpu.CompilerParams(vmem_limit_bytes=VMEM),
        name="attend",
    )(*tab, query, key_weight, value_weight, *norms)


def attend_back(
    tab, cycle_pos, query, grads, outputs, lse, ks, vs, key_weight, value_weight, ns, bias,
    unit_size, units, items, heads,
):
    feats = heads * HEAD
    cols = heads * QROWS
    rows, width = query.shape
    groups = width // feats
    blocks = rows // QROWS
    once = pl.Buffered(1) if units > 16 else None

    def part(rows, columns=feats):
        return pl.BlockSpec((rows, columns), lambda group, *_: (0, group), pipeline_mode=once)

    def whole(rows, columns):
        return pl.BlockSpec(
            (rows, columns), lambda group, *_: (0, 0), pipeline_mode=pl.Buffered(1)
        )

    return pl.pallas_call(
        functools.partial(attend_back_kernel, heads, units, items, unit_size),
        grid_spec=pltpu.PrefetchScalarGridSpec(
            num_scalar_prefetch=TABLES + 1,
            grid=(groups,),
            in_specs=[
                part(rows),
                part(grads.shape[0]),
                part(rows),
                part(lse.shape[0], cols),
                part(ks.shape[0]),
                part(ks.shape[0]),
                part(width),
                part(width),
                whole(*ns.shape),
                whole(*bias.shape),
            ],
            out_specs=[
                part(grads.shape[0]),
                part(width),
                part(width),
                whole(units * HALF * ROWW, width),
            ],
            scratch_shapes=[
                pltpu.VMEM((blocks, cols, feats), BF16),
                pltpu.VMEM((blocks, cols, feats), BF16),
                pltpu.VMEM((blocks, 8, cols), F32),
                pltpu.VMEM((blocks, cols, feats), F32),
                pltpu.VMEM((SPARE_KEYS, feats), F32),
                pltpu.VMEM((SPARE_KEYS, feats), F32),
                pltpu.VMEM((width, feats), F32),
                pltpu.VMEM((width, feats), F32),
                pltpu.VMEM(ns.shape, BF16),
                pltpu.VMEM((rows, grads.shape[0]), BF16),
                pltpu.VMEM((grads.shape[0], rows), BF16),
                pltpu.VMEM((rows, feats), BF16),
                pltpu.VMEM((rows, feats), BF16),
                pltpu.VMEM((unit_size, width), BF16),
            ],
        ),
        out_shape=[
            jax.ShapeDtypeStruct(grads.shape, BF16),
            jax.ShapeDtypeStruct((width, width), BF16),
            jax.ShapeDtypeStruct((width, width), BF16),
            jax.ShapeDtypeStruct((units * HALF * ROWW, width), BF16),
        ],
        cost_estimate=cost(90),
        compiler_params=pltpu.CompilerParams(vmem_limit_bytes=VMEM),
        name="attend_back",
    )(cycle_pos.reshape(1), *tab, query, grads, outputs, lse, ks, vs, key_weight, value_weight, ns, bias)


@functools.cache
def most_rows(cycle_size, item_count):
    rows = np.arange(SLOTS)[:, None] * cycle_size + np.arange(cycle_size)
    most_keys = most_unit = most_queries = 0
    lists = [()]
    while lists:
        heights = lists.pop()
        if len(heights) < item_count:
            for height in (24, 30):
                if sum(heights) + height <= SLOTS * cycle_size:
                    lists.append(heights + (height,))
        if not heights:
            continue
        ends = np.cumsum(heights)
        number = np.searchsorted(ends, rows, side="right")
        wide = np.array([24 if height == 24 else ROWW for height in heights] + [0])[number]
        kinds = np.arange(len(heights))
        counts = [((number == kind) * wide) for kind in kinds] + [ROWW - wide]
        counts = np.stack(counts)

        def rounded(values, align):
            return -(-values // align) * align

        units = rounded(counts.reshape(len(counts), 2, HALF, cycle_size).sum(2), 16)
        most_unit = max(most_unit, units.sum(0).max())
        keys = units.sum((1, 2))
        keys = rounded(keys[:-1], KEYS).sum() + rounded(keys[-1], SPARE_KEYS)
        most_keys = max(most_keys, keys)
        most_queries = max(most_queries, rounded(counts.sum(1), QROWS).sum(0).max())
    return int(most_keys), int(most_unit), int(most_queries)


def passed(value, axis, target):
    pairs = [(source, target(source)) for source in range(lax.axis_size(axis))]
    return lax.ppermute(value, axis, pairs)


def passed_along(value, axis, steps):
    count = lax.axis_size(axis)
    return passed(value, axis, lambda source: (source + steps) % count)


def tied(*values):
    return lax.optimization_barrier(values)


def to_sibling(value):
    return passed(value, "blk", lambda source: source ^ 1)


def gelu_tanh(values):
    return (
        0.5
        * values
        * (1.0 + jnp.tanh(0.7978845608028654 * (values + 0.044715 * values * values * values)))
    )


def gelu_back(values, gradient):
    return jax.vjp(gelu_tanh, values)[1](gradient)[0]


def item_facts(lengths):
    facts, start = [], 0
    for item in range(lengths.shape[0]):
        length = lengths[item]
        height = jnp.where(length == 1200, 30, jnp.where(length == 576, 24, 0))
        width = jnp.where(length == 1200, 40, 24)
        facts.append((start, start + height, height, width))
        start = start + height
    return facts


def row_facts(facts, rows):
    number = jnp.full_like(rows, len(facts))
    local, height, width = rows, jnp.zeros_like(rows), jnp.zeros_like(rows)
    for item, (start, end, item_height, item_width) in enumerate(facts):
        inside = (rows >= start) & (rows < end)
        number = jnp.where(inside, item, number)
        local = jnp.where(inside, rows - start, local)
        height = jnp.where(inside, item_height, height)
        width = jnp.where(inside, item_width, width)
    return number, local, height, width


def tap_masks(local_row, height, width):
    column = lax.broadcasted_iota(jnp.int32, (1, ROWW), 1)
    is_real = column < width
    all_masks = []
    for row_step in (-1, 0, 1):
        rows_fine = (local_row + row_step >= 0) & (local_row + row_step < height)
        for col_step in (-1, 0, 1):
            cols_fine = (column + col_step >= 0) & (column + col_step < width)
            all_masks.append(is_real & rows_fine & cols_fine)
    return is_real, all_masks


def side_shift(values, col_step):
    if col_step == 0:
        return values
    empty_col = jnp.zeros_like(values[:, :1])
    if col_step < 0:
        return jnp.concatenate([empty_col, values[:, :-1]], axis=1)
    return jnp.concatenate([values[:, 1:], empty_col], axis=1)


def from_above(values, cycle_pos):
    got = passed_along(values, "blk", 1)
    empty_row = jnp.zeros_like(values[:1])
    return jnp.where(cycle_pos == 0, jnp.concatenate([empty_row, got[:-1]], axis=0), got)


def from_below(values, cycle_pos, cycle_size):
    got = passed_along(values, "blk", -1)
    empty_row = jnp.zeros_like(values[:1])
    return jnp.where(
        cycle_pos == cycle_size - 1, jnp.concatenate([got[1:], empty_row], axis=0), got
    )


def upsample_forward(row_above, values, row_below, all_masks):
    center = values.astype(F32)
    upper_value = jnp.where(all_masks[1][:, :, None], row_above, values).astype(F32)
    lower_value = jnp.where(all_masks[7][:, :, None], row_below, values).astype(F32)
    pieces = []
    for half_rows in (0.75 * center + 0.25 * upper_value, 0.75 * center + 0.25 * lower_value):
        left_value = jnp.where(all_masks[3][:, :, None], side_shift(half_rows, -1), half_rows)
        right_value = jnp.where(all_masks[5][:, :, None], side_shift(half_rows, 1), half_rows)
        pieces.append(0.75 * half_rows + 0.25 * left_value)
        pieces.append(0.75 * half_rows + 0.25 * right_value)
    joined = jnp.concatenate(pieces, axis=2)
    return joined.reshape(-1, joined.shape[2])


def upsample_back_columns(gradient, all_masks):
    channels = gradient.shape[2] // 4
    left_fine = all_masks[3][:, :, None]
    right_fine = all_masks[5][:, :, None]
    halves = []
    for half in (0, 1):
        left_part = gradient[:, :, 2 * half * channels : (2 * half + 1) * channels].astype(F32)
        right_part = gradient[:, :, (2 * half + 1) * channels : (2 * half + 2) * channels].astype(
            F32
        )
        side = jnp.where(right_fine, side_shift(left_part, 1), 0.0)
        side = side + jnp.where(left_fine, 0.0, left_part)
        side = side + jnp.where(left_fine, side_shift(right_part, -1), 0.0)
        side = side + jnp.where(right_fine, 0.0, right_part)
        halves.append(0.75 * (left_part + right_part) + 0.25 * side)
    return [half.astype(BF16) for half in halves]


def upsample_back_rows(upper, lower, upper_next, lower_prev, all_masks):
    up_fine = all_masks[1][:, :, None]
    down_fine = all_masks[7][:, :, None]
    rows = jnp.where(down_fine, upper_next, lower).astype(F32)
    rows = rows + jnp.where(up_fine, lower_prev, upper).astype(F32)
    return 0.75 * (upper.astype(F32) + lower.astype(F32)) + 0.25 * rows


def dot32(left, right, **more):
    return jnp.dot(left, right, preferred_element_type=F32, **more)


def dot_t(left, right):
    return lax.dot_general(left, right, NT, preferred_element_type=F32)


def t_dot(left, right):
    return lax.dot_general(left, right, (((0,), (0,)), ((), ())), preferred_element_type=F32)


def halving(values, device, bit, axis, pairs_axis):
    half = values.shape[axis] // 2
    mine = (device >> bit) & 1
    keep = lax.dynamic_slice_in_dim(values, mine * half, half, axis=axis)
    send = lax.dynamic_slice_in_dim(values, (1 - mine) * half, half, axis=axis)
    return keep, passed(send, pairs_axis, lambda source: source ^ (1 << bit))


def summed(keep, got):
    return (keep.astype(F32) + got.astype(F32)).astype(BF16)


def core_summed(shares, core):
    cycle_size, rows, width = shares.shape
    paired = shares.reshape(cycle_size // 2, 2, rows, width)
    keep = lax.dynamic_index_in_dim(paired, core, 1, keepdims=False)
    send = lax.dynamic_index_in_dim(paired, 1 - core, 1, keepdims=False)
    return (keep.astype(F32) + to_sibling(send).astype(F32)).astype(BF16)


class ChipSums:
    def __init__(self, values, chip):
        half = values.shape[1] // 2
        self.chip, self.chips = chip, values.shape[0]
        self.parts = [(values[:, :half], 1), (values[:, half:], -1)]
        self.moving = [self.block(part, way, 1).astype(BF16) for part, way in self.parts]

    def block(self, part, way, offset):
        spot = (self.chip - way * offset) % self.chips
        return lax.dynamic_index_in_dim(part, spot, 0, keepdims=False).astype(F32)

    def step(self, number):
        moved = []
        for value, (part, way) in zip(self.moving, self.parts):
            got = passed_along(value, "blk", 2 * way).astype(F32)
            moved.append((got + self.block(part, way, number + 1)).astype(BF16))
        self.moving = moved

    def result(self):
        return jnp.concatenate(self.moving, axis=0)


class GroupGather:
    def __init__(self, values, dp_pos):
        self.dp_pos, self.bits = dp_pos, lax.axis_size("dp").bit_length() - 1
        half = values.shape[0] // 2
        self.held = [part[(None,) * self.bits] for part in (values[:half], values[half:])]

    def step(self, number):
        held = []
        for value, bit in zip(self.held, (number, self.bits - 1 - number)):
            axis = self.bits - 1 - bit
            got = passed(value, "dp", lambda source, bit=bit: source ^ (1 << bit))
            mine = (self.dp_pos >> bit) & 1
            held.append(
                jnp.where(
                    mine == 0,
                    jnp.concatenate([value, got], axis=axis),
                    jnp.concatenate([got, value], axis=axis),
                )
            )
        self.held = held

    def result(self):
        shape = (1 << self.bits,)
        return jnp.concatenate(
            [value.reshape(shape + value.shape[self.bits :]) for value in self.held], axis=1
        )


def gathered_over_groups(values, dp_pos):
    gather = GroupGather(values, dp_pos)
    for number in range(gather.bits):
        gather.step(number)
    return gather.result()


def over_groups(values):
    total = values.astype(F32)
    for partner in range(1, lax.axis_size("dp")):
        got = passed(values, "dp", lambda source, partner=partner: source ^ partner)
        total = total + got.astype(F32)
    return total.astype(BF16)


def sum_over_chips(values, chip):
    chips = values.shape[0]
    total = lax.dynamic_index_in_dim(values, chip, 0, keepdims=False).astype(F32)
    for step in range(1, chips):
        send = lax.dynamic_index_in_dim(values, (chip + step) % chips, 0, keepdims=False)
        total = total + passed_along(send, "blk", 2 * step).astype(F32)
    return total


def whole_shares(whole, parts, orders):
    groups = whole.shape[0]
    bits = groups.bit_length() - 1
    out, place = [], 0
    for part, order in zip(parts, orders):
        rows, width = part.shape[1:]
        size = rows * width // 256
        pieces = []
        for turn in range(groups):
            device = sum(((turn >> (bits - 1 - index)) & 1) << bit for index, bit in enumerate(order))
            pieces.append(whole[device, place : place + size].reshape(rows, width))
        out.append(jnp.concatenate(pieces, axis=0).astype(F32))
        place += size
    return out


def shards(
    tokens,
    item_lengths,
    dataset_ids,
    dataset_table,
    norm1_gain,
    norm1_bias,
    query_weight,
    key_weight,
    value_weight,
    out_weight,
    norm2_gain,
    norm2_bias,
    fc1_weight,
    fc2_weight,
    project_weight,
    unit1_first,
    unit1_second,
    unit2_first,
    unit2_second,
    output_weight,
    block_cotangent,
    merged_cotangent,
):
    cycle_size = lax.axis_size("blk")
    cycle_pos = lax.axis_index("blk")
    chips = cycle_size // 2
    chip, core = cycle_pos // 2, cycle_pos % 2
    lengths = item_lengths[0]
    item_count = lengths.shape[0]
    kinds = item_count + 1
    width_model = tokens.shape[1]
    heads = 4 if cycle_size <= 8 else 2
    half_tokens = HALF * ROWW
    token_count = tokens.shape[0]

    facts = item_facts(lengths)
    own_rows = lax.broadcasted_iota(jnp.int32, (SLOTS, 1), 0) * cycle_size + cycle_pos
    number, local_row, height, width = row_facts(facts, own_rows)
    is_real, all_masks = tap_masks(local_row, height, width)
    units = 4 * chips
    most_keys, most_unit, query_rows = most_rows(cycle_size, item_count)
    unit_size = most_unit + 48
    sorted_keys = (most_keys + 128 + ROWS - 1) // ROWS * ROWS
    tab = geometry(lengths, cycle_pos, cycle_size, unit_size)
    ids = dataset_ids[0]
    gain_one, bias_one = norm1_gain.reshape(1, -1), norm1_bias.reshape(1, -1)

    stream_start, normed_one, query = own_start(
        tab, ids, tokens, dataset_table, gain_one, bias_one, query_weight, query_rows
    )
    ahead, behind = tokens[:half_tokens], tokens[half_tokens:]
    sorted_norms = []
    for step in range(chips):
        if step:
            ahead = passed_along(ahead, "blk", 2)
            behind = passed_along(behind, "blk", -2)
            ahead, behind, sorted_norms[-1] = tied(ahead, behind, sorted_norms[-1])
        if step == 1:
            ahead, behind, stream_start, normed_one, query = tied(
                ahead, behind, stream_start, normed_one, query
            )
            ahead, behind, merged_cotangent = tied(ahead, behind, merged_cotangent)
            upper, lower = upsample_back_columns(
                merged_cotangent.reshape(SLOTS, ROWW, -1), all_masks
            )
        if step == 2:
            ahead, behind, upper, lower = tied(ahead, behind, upper, lower)
            upper_next = from_below(upper, cycle_pos, cycle_size)
            lower_prev = from_above(lower, cycle_pos)
        if step == chips - 1:
            ahead, behind, upper_next, lower_prev = tied(ahead, behind, upper_next, lower_prev)
            mapped_grad = upsample_back_rows(
                upper, lower, upper_next, lower_prev, all_masks
            ).astype(BF16)
            mapped_grad = jnp.pad(mapped_grad, ((0, 0), (0, PITCH - ROWW), (0, 0)))
            mapped_grad = mapped_grad.reshape(SLOTS * PITCH, -1)
        mine = jnp.concatenate([ahead, behind], axis=0)
        sorted_norms.append(
            sort_step(
                step, tab, ids, mine, to_sibling(mine), dataset_table, gain_one, bias_one, unit_size
            )
        )
    sorted_norms[-1], mapped_grad = tied(sorted_norms[-1], mapped_grad)
    group_grad = lax.all_gather(mapped_grad, "blk", tiled=True)
    attended, outputs, lse, sorted_norm, bias, ks, vs = attend(
        tab, query, key_weight, value_weight, sorted_norms, sorted_keys, units, kinds, heads
    )
    attended, group_grad = tied(attended, group_grad)

    def as_cells(flattened):
        return flattened.reshape(SLOTS, ROWW, flattened.shape[-1])

    after_attn = stream_start + dot32(attended, out_weight)
    normed_two = layer_norm(after_attn, norm2_gain, norm2_bias).astype(BF16)
    pre_act = dot32(normed_two, fc1_weight)
    hidden = gelu_tanh(pre_act).astype(BF16)
    block_out = (after_attn + dot32(hidden, fc2_weight)).astype(BF16)
    channels = project_weight.shape[1]

    def exchanged(values):
        values = values.reshape(cycle_size, -1, channels)
        return lax.all_to_all(values, "blk", 0, 0).reshape(-1, channels)

    grad_rows, mapped_rows, conv_shares = merge(
        tab,
        exchanged(pack(tab, block_out, project_weight)),
        group_grad,
        (unit1_first, unit1_second, unit2_first, unit2_second),
        output_weight,
        cycle_size,
    )
    conv_shares = conv_shares.reshape(cycle_size, -1, channels)
    group_mapped = lax.all_gather(mapped_rows, "blk", tiled=True)
    reassembled_grad = unpack(tab.came, exchanged(grad_rows))

    def shared_out(*gradients):
        parts = []
        for gradient in gradients:
            parts.append(gradient.astype(BF16).reshape(cycle_size, -1, gradient.shape[-1]))
        return jnp.concatenate(parts, axis=1) if len(parts) > 1 else parts[0]

    dp_pos = lax.axis_index("dp")
    groups = lax.axis_size("dp")
    bits = groups.bit_length() - 1
    one_way = list(range(bits))
    other_way = one_way[::-1]

    def wide(gradient):
        return gradient.reshape(cycle_size, -1, width_model)

    def scattering(shares):
        count, share_rows, share_width = shares.shape
        parts = shares.reshape(count, groups, share_rows // groups, share_width)
        return jnp.swapaxes(parts, 0, 1).reshape(-1, share_width)

    def scattered(parts):
        return lax.psum_scatter(parts, "dp", scatter_dimension=0, tiled=True)

    def dp_halving(values, order, index):
        return halving(values, dp_pos, order[index], 1, "dp")

    def dp_halved(values, order, index):
        return summed(*dp_halving(values, order, index))

    project_grad = t_dot(block_out, reassembled_grad)
    block_grad = block_cotangent.astype(F32) + dot_t(reassembled_grad, project_weight)
    mlp_grad = block_grad.astype(BF16)
    fc2_parts = scattering(shared_out(t_dot(hidden, mlp_grad)))
    mlp_grad, fc2_parts = tied(mlp_grad, fc2_parts)
    fc2_sums = scattered(fc2_parts)
    conv_sums = core_summed(conv_shares, core)
    pre_grad = gelu_back(pre_act, dot_t(mlp_grad, fc2_weight)).astype(BF16)
    fc1_grad = t_dot(normed_two, pre_grad)
    normed_two_grad = dot_t(pre_grad, fc1_weight)
    norm_two_pull = jax.vjp(layer_norm, after_attn, norm2_gain, norm2_bias)[1]
    attn_side, norm2_gain_grad, norm2_bias_grad = norm_two_pull(normed_two_grad)
    after_grad = block_grad + attn_side
    branch_grad = after_grad.astype(BF16)
    out_proj_grad = t_dot(attended, branch_grad)
    attended_grad = dot_t(branch_grad, out_weight).astype(BF16)

    rows = width_model // cycle_size
    rows = width_model // cycle_size
    fc1_sums = core_summed(shared_out(fc1_grad), core)
    out_sums = core_summed(shared_out(out_proj_grad, wide(project_grad)), core)
    attended_grad, conv_sums, fc1_sums, out_sums, fc2_sums = tied(
        attended_grad, conv_sums, fc1_sums, out_sums, fc2_sums
    )
    conv_sums, conv_got = dp_halving(conv_sums, one_way, 0)
    fc1_sums, fc1_got = dp_halving(fc1_sums, other_way, 0)
    out_sums, out_got = dp_halving(out_sums, one_way, 0)
    fc2_sums = lax.psum_scatter(fc2_sums, "blk", scatter_dimension=0, tiled=True)
    query_low, key_grad, value_grad, token_grad = attend_back(
        tab, cycle_pos, query, attended_grad, outputs, lse, ks, vs, key_weight, value_weight, sorted_norm,
        bias, unit_size, units, kinds, heads,
    )
    query_low, key_grad, value_grad, token_grad, conv_got, fc1_got, out_got, fc2_sums = tied(
        query_low, key_grad, value_grad, token_grad, conv_got, fc1_got, out_got, fc2_sums
    )
    normed_one_grad = lax.psum_scatter(token_grad, "blk", scatter_dimension=0, tiled=True)
    conv_sums = summed(conv_sums, conv_got)
    fc1_sums = summed(fc1_sums, fc1_got)
    out_sums = summed(out_sums, out_got)
    query_grad = t_dot(normed_one, query_low)
    key_sums = core_summed(shared_out(key_grad, value_grad), core)
    query_sums = core_summed(shared_out(query_grad), core)

    for index in range(bits):
        if index:
            conv_sums = dp_halved(conv_sums, one_way, index)
            fc1_sums = dp_halved(fc1_sums, other_way, index)
            out_sums = dp_halved(out_sums, one_way, index)
        key_sums = dp_halved(key_sums, one_way, index)
        query_sums = dp_halved(query_sums, other_way, index)
    late = [conv_sums, fc1_sums, out_sums, key_sums, query_sums]
    late_orders = [one_way, other_way, one_way, one_way, other_way]
    chip_sums = ChipSums(
        jnp.concatenate([part.reshape(chips, -1, 256) for part in late], axis=1), chip
    )
    for turn in range(1, chips - 1):
        chip_sums.step(turn)
    around = unpack(tab.around, group_mapped).reshape(3, SLOTS, ROWW, channels)
    merged = upsample_forward(around[0], around[1], around[2], all_masks).astype(BF16)
    fc2_all = gathered_over_groups(fc2_sums, dp_pos)
    normed_one_grad, fc2_all, *chip_sums.moving = tied(
        normed_one_grad, fc2_all, *chip_sums.moving
    )
    chip_sums.step(chips - 1)
    gather = GroupGather(chip_sums.result(), dp_pos)
    normed_one_grad = normed_one_grad.astype(F32) + dot_t(query_low, query_weight)

    norm_one_pull = jax.vjp(layer_norm, stream_start, norm1_gain, norm1_bias)[1]
    start_side, norm1_gain_grad, norm1_bias_grad = norm_one_pull(normed_one_grad)
    tokens_grad = after_grad + start_side
    table_rows = dataset_table.shape[0]
    dataset = jnp.full_like(number, -1)
    for item in range(item_count):
        dataset = jnp.where(number == item, ids[item], dataset)
    dataset = jnp.where(is_real, dataset, -1).reshape(1, -1)
    onehot = (dataset == lax.broadcasted_iota(jnp.int32, (table_rows, 1), 0)).astype(F32)
    table_grad = jnp.dot(onehot, tokens_grad, precision=HIGH)
    table_split = jnp.swapaxes(table_grad.reshape(table_rows, cycle_size, rows), 0, 1)
    small = [table_split.reshape(cycle_size, -1)] + [
        gradient.reshape(cycle_size, -1)
        for gradient in (norm1_gain_grad, norm1_bias_grad, norm2_gain_grad, norm2_bias_grad)
    ]
    small = jnp.concatenate(small, axis=1).astype(BF16)
    small_rows = -(-small.shape[1] // 1024) * 8
    small = jnp.pad(small, ((0, 0), (0, small_rows * 128 - small.shape[1])))
    small = small.reshape(cycle_size, small_rows, 128)
    small = over_groups(core_summed(small, core))
    for bit in range(bits):
        gather.step(bit)
    small = sum_over_chips(small, chip).reshape(-1)
    table_size = table_rows * rows
    norms = [small[table_size + index * rows :][:rows] for index in range(4)]

    unit_share = 9 * channels // cycle_size
    out_share = channels // cycle_size
    convs, fc1_share, outs, keys_values, query_share = whole_shares(
        gather.result(), late, late_orders
    )
    return (
        block_out,
        merged,
        tokens_grad,
        small[:table_size].reshape(table_rows, rows),
        norms[0],
        norms[1],
        query_share,
        keys_values[:rows],
        keys_values[rows:],
        outs[:rows],
        norms[2],
        norms[3],
        fc1_share,
        fc2_all.reshape(-1, width_model).astype(F32),
        outs[rows:].reshape(rows, channels),
        convs[:unit_share],
        convs[unit_share : 2 * unit_share],
        convs[2 * unit_share : 3 * unit_share],
        convs[3 * unit_share : 4 * unit_share],
        convs[4 * unit_share :],
    )


def solution(mesh):
    split = P(("dp", "blk"), None)
    placed = (split, P("dp", None), P("dp", None)) + (P(),) * 17 + (split, split)
    rows, line = P("blk", None), P("blk")
    return jax.shard_map(
        shards,
        mesh=mesh,
        in_specs=placed,
        out_specs=(
            split, split, split, P(None, "blk"), line, line, rows, rows, rows, rows, line, line,
            rows, rows, rows, rows, rows, rows, rows, rows,
        ),
        check_vma=False,
    )
```
